32 devices in a mesh: ctx: 2 (over x), fsdp: 16 (over z, y, core).
Axes of the slice: x: 2, y: 2, z: 4, core: 2. Of those that a mesh axis runs over, the one named last changes fastest.
Arguments:
- tokens_in: bfloat16 [2, 16, 512, 768], P(None, None, ('ctx', 'fsdp')), may hold values from -6 to 6
- out_grad: bfloat16 [2, 16, 512, 768], P(None, None, ('ctx', 'fsdp')), may hold values from -6 to 6
- seq_lengths: int32 [2, 16], replicated, may hold values from 257 to 512, as said below
- order: int32 [2, 16], replicated, may hold values from 0 to 15, as said below
- w_qkv: bfloat16 [768, 2304], P('fsdp'), may hold values from -0.21875 to 0.21875
- bias_q: bfloat16 [768], P('fsdp'), may hold values from -3 to 3
- bias_v: bfloat16 [768], P('fsdp'), may hold values from -3 to 3
- w_out: bfloat16 [768, 768], P('fsdp'), may hold values from -0.875 to 0.875
- bias_out: bfloat16 [768], P('fsdp'), may hold values from -3 to 3
- ln1_gain: bfloat16 [768], P('fsdp'), may hold values from 0.5 to 1.5
- ln1_bias: bfloat16 [768], P('fsdp'), may hold values from -2 to 2
- w_gate_up: bfloat16 [768, 6144], P('fsdp'), may hold values from -0.21875 to 0.21875
- w_down: bfloat16 [3072, 768], P('fsdp'), may hold values from -0.21875 to 0.21875
- bias_down: bfloat16 [768], P('fsdp'), may hold values from -3 to 3
- ln2_gain: bfloat16 [768], P('fsdp'), may hold values from 0.5 to 1.5
- ln2_bias: bfloat16 [768], P('fsdp'), may hold values from -2 to 2
Outputs:
- output: bfloat16 [2, 16, 512, 768], P(None, None, ('ctx', 'fsdp'))
- input_grad: bfloat16 [2, 16, 512, 768], P(None, None, ('ctx', 'fsdp'))
- grad_w_qkv: float32 [768, 2304], P('fsdp')
- grad_bias_q: float32 [768], P('fsdp')
- grad_bias_v: float32 [768], P('fsdp')
- grad_w_out: float32 [768, 768], P('fsdp')
- grad_bias_out: float32 [768], P('fsdp')
- grad_ln1_gain: float32 [768], P('fsdp')
- grad_ln1_bias: float32 [768], P('fsdp')
- grad_w_gate_up: float32 [768, 6144], P('fsdp')
- grad_w_down: float32 [3072, 768], P('fsdp')
- grad_bias_down: float32 [768], P('fsdp')
- grad_ln2_gain: float32 [768], P('fsdp')
- grad_ln2_bias: float32 [768], P('fsdp')
The draws below stay inside these ranges and needn't reach their ends.
Inputs may be any that keep to these rules, and one draw needn't show every extreme that they name: `seq_lengths`: a sequence's real tokens fill its slots 0 to length - 1; in each micro-batch some sequence fills all 512 slots. `order`: each row is a permutation of the micro-batch's sequences.
All inputs are finite; a program needn't handle non-finite values.
Results may differ from the reference program's by a relative error of at most 0.015.
Values may be sent and summed in bfloat16 or wider, within the bound.
A program may use at most 120 MiB of HBM per device.

```python
import math
import jax
import jax.numpy as jnp
from jax import lax

D = 768
HEADS = 12
HEAD_DIM = 64
FF = 3072
LMAX = 512
M = 2
NSEQ = 16


def shared_lengths(key):
    first_key, second_key = jax.random.split(key)
    lengths_drawn = jax.random.randint(first_key, (M, NSEQ), LMAX // 2 + 1, LMAX + 1)
    chosen = jax.random.randint(second_key, (M, 1), 0, NSEQ)
    column = jnp.arange(NSEQ)[None, :]
    return jnp.where(column == chosen, LMAX, lengths_drawn).astype(jnp.int32)


def draw_seq_lengths(key, part):
    lengths = shared_lengths(key)
    return lengths


def draw_order(key, part):
    lengths = shared_lengths(key)
    key = jax.random.fold_in(key, 11)
    shuffle = jax.random.permutation(key, NSEQ)
    column = jnp.arange(NSEQ, dtype=jnp.int32)[None, :]
    distinct = lengths * NSEQ + column
    rising = jnp.argsort(distinct, axis=1, stable=True).astype(jnp.int32)
    falling = rising[:, ::-1]
    parity = (jnp.arange(M) % 2)[:, None]
    sorted_rows = jnp.where(parity == 1, falling, rising)
    return sorted_rows[:, shuffle].astype(jnp.int32)


def steps_of(stream_key, extent, pieces, low, largest):
    def one(axis_at, blocks):
        steps = jax.random.uniform(jax.random.fold_in(jax.random.fold_in(stream_key, 6), axis_at), (blocks,), jnp.float32, low / len(pieces), largest / len(pieces))
        return jnp.repeat(jnp.exp(steps), extent[axis_at] // blocks).reshape((-1,) + (1,) * (len(extent) - axis_at - 1))

    factor_of = one(*pieces[0])
    for cut in pieces[1:]:
        factor_of = factor_of * one(*cut)
    return factor_of


def normal_values(key, extent, width, limit, cuts=(), held_as=jnp.bfloat16):
    drawn = width * jax.random.normal(key, extent, jnp.float32)
    if cuts:
        drawn = drawn * steps_of(key, extent, cuts, -0.22, 0.18)
    return jnp.clip(drawn, -limit, limit).astype(held_as)


def setup_inputs(seed: int = 0) -> dict:
    key_list = jax.random.split(jax.random.key(seed), 17)
    tokens_in = normal_values(key_list[0], (M, NSEQ, LMAX, D), 1.0, 6.0, ((2, 32),))
    out_grad = normal_values(key_list[1], (M, NSEQ, LMAX, D), 1.0, 6.0, ((2, 32),))
    seq_lengths = draw_seq_lengths(jax.random.fold_in(key_list[16], 71), 0)
    order = draw_order(jax.random.fold_in(key_list[16], 71), 0)
    w_qkv = normal_values(key_list[4], (D, 3 * D), D ** -0.5, 0.21875, ((0, 16),))
    bias_q = normal_values(key_list[5], (D,), 0.5, 3.0, ((0, 16),))
    bias_v = normal_values(key_list[6], (D,), 0.5, 3.0, ((0, 16),))
    w_out = normal_values(key_list[7], (D, D), (D // 16) ** -0.5, 0.875, ((0, 16),))
    bias_out = normal_values(key_list[8], (D,), 0.5, 3.0, ((0, 16),))
    ln1_gain = jnp.clip(1.0 + 0.1 * jax.random.normal(key_list[9], (D,), jnp.float32), 0.5, 1.5).astype(jnp.bfloat16)
    ln1_bias = normal_values(key_list[10], (D,), 0.3, 2.0, ((0, 16),))
    w_gate_up = normal_values(key_list[11], (D, 2 * FF), D ** -0.5, 0.21875, ((0, 16),))
    w_down = normal_values(key_list[12], (FF, D), (FF // 4) ** -0.5, 0.21875, ((0, 16),))
    bias_down = normal_values(key_list[13], (D,), 0.5, 3.0, ((0, 16),))
    ln2_gain = jnp.clip(1.0 + 0.1 * jax.random.normal(key_list[14], (D,), jnp.float32), 0.5, 1.5).astype(jnp.bfloat16)
    ln2_bias = normal_values(key_list[15], (D,), 0.3, 2.0, ((0, 16),))
    return {"tokens_in": tokens_in, "out_grad": out_grad, "seq_lengths": seq_lengths, "order": order, "w_qkv": w_qkv, "bias_q": bias_q, "bias_v": bias_v, "w_out": w_out, "bias_out": bias_out, "ln1_gain": ln1_gain, "ln1_bias": ln1_bias, "w_gate_up": w_gate_up, "w_down": w_down, "bias_down": bias_down, "ln2_gain": ln2_gain, "ln2_bias": ln2_bias}


@jax.custom_vjp
def low(v):
    return lax.optimization_barrier(v.astype(jnp.bfloat16)).astype(jnp.float32)

@jax.custom_vjp
def low_back(v):
    return v

def low_keep(v):
    return (low(v), None)

def low_pass(kept, grad):
    return (grad,)

def back_keep(v):
    return (v, None)

def back_low(kept, grad):
    return (low(grad),)
low.defvjp(low_keep, low_pass)
low_back.defvjp(back_keep, back_low)
EPSILON = 1e-12
NEGATIVE = -1e+30
HIGHEST_PRECISION = lax.Precision.HIGHEST

def slope_list(head_count):

    def powers(number):
        anchor = 2.0 ** (-2.0 ** (-(math.log2(number) - 3)))
        return [anchor ** (power_index + 1) for power_index in range(number)]
    closest = 2 ** int(math.floor(math.log2(head_count)))
    if closest == head_count:
        return powers(head_count)
    return powers(closest) + powers(2 * closest)[0::2][:head_count - closest]

def layer_norm(inputs, gain_row, offset_row):
    centre = inputs - lax.optimization_barrier(jnp.mean(inputs, axis=-1, keepdims=True))
    spread = lax.optimization_barrier(jnp.mean(centre * centre, axis=-1, keepdims=True))
    return centre * lax.rsqrt(spread + EPSILON) * gain_row + offset_row

def sequence_layer(tokens, length, params):
    w_qkv, bias_q, bias_v, w_out, bias_out, ln1_gain, ln1_bias, w_gate_up, w_down, bias_down, ln2_gain, ln2_bias = params
    projected = jnp.dot(tokens, w_qkv, precision=HIGHEST_PRECISION)
    queries = low(low_back(projected[:, :D] + bias_q))
    key_rows = low(low_back(projected[:, D:2 * D]))
    values = low(low_back(projected[:, 2 * D:] + bias_v))
    place = jnp.arange(LMAX)
    valid = place < length
    heads_q = queries.reshape(LMAX, HEADS, HEAD_DIM)
    heads_k = key_rows.reshape(LMAX, HEADS, HEAD_DIM)
    heads_v = values.reshape(LMAX, HEADS, HEAD_DIM)
    scores = jnp.einsum('qhd,khd->hqk', heads_q, heads_k, precision=HIGHEST_PRECISION) * 0.125
    slopes = jnp.array(slope_list(HEADS), jnp.float32)
    distance = jnp.abs(place[:, None] - place[None, :]).astype(jnp.float32)
    scores = scores - slopes[:, None, None] * distance[None]
    scores = jnp.where(valid[None, None, :], scores, NEGATIVE)
    scores = low_back(scores)
    attn_probs = low(jax.nn.softmax(scores, axis=-1))
    context = jnp.einsum('hqk,khd->qhd', attn_probs, heads_v, precision=HIGHEST_PRECISION).reshape(LMAX, D)
    context = low(low_back(context))
    attn_out = low_back(jnp.dot(context, w_out, precision=HIGHEST_PRECISION) + bias_out)
    normed_one = layer_norm(tokens + attn_out, ln1_gain, ln1_bias)
    gate_up = low_back(jnp.dot(low(normed_one), w_gate_up, precision=HIGHEST_PRECISION))
    hidden = low(jax.nn.gelu(gate_up[:, :FF], approximate=False) * gate_up[:, FF:])
    branch = low_back(jnp.dot(hidden, w_down, precision=HIGHEST_PRECISION) + bias_down)
    result = layer_norm(normed_one + branch, ln2_gain, ln2_bias)
    return jnp.where(valid[:, None], result, 0.0)

def reference(tokens_in, out_grad, seq_lengths, order, w_qkv, bias_q, bias_v, w_out, bias_out, ln1_gain, ln1_bias, w_gate_up, w_down, bias_down, ln2_gain, ln2_bias):
    params = tuple((element.astype(jnp.float32) for element in (w_qkv, bias_q, bias_v, w_out, bias_out, ln1_gain, ln1_bias, w_gate_up, w_down, bias_down, ln2_gain, ln2_bias)))
    dealt_tokens = jnp.take_along_axis(tokens_in, order[:, :, None, None], axis=1)
    dealt_lengths = jnp.take_along_axis(seq_lengths, order, axis=1)
    sequence_count = tokens_in.shape[0] * tokens_in.shape[1]
    flat_tokens = dealt_tokens.reshape(sequence_count, LMAX, D)
    flat_grads = out_grad.reshape(sequence_count, LMAX, D)
    flat_lengths = dealt_lengths.reshape(sequence_count)
    zero_sums = tuple((jnp.zeros_like(element) for element in params))

    def one_step(running, element):
        tokens, cotangent, length = element

        def forward(inputs, weights):
            return sequence_layer(inputs, length, weights)
        result, pull_back = jax.vjp(forward, tokens.astype(jnp.float32), params)
        grad_in, grad_params = pull_back(cotangent.astype(jnp.float32))
        running = tuple((left_sum + right_sum for left_sum, right_sum in zip(running, grad_params)))
        return (running, (result.astype(jnp.bfloat16), grad_in.astype(jnp.bfloat16)))
    sums, (results, grads_in) = lax.scan(one_step, zero_sums, (flat_tokens, flat_grads, flat_lengths))
    output = results.reshape(tokens_in.shape)
    dealt_grads = grads_in.reshape(tokens_in.shape)
    inverse = jnp.argsort(order, axis=1).astype(jnp.int32)
    input_grad = jnp.take_along_axis(dealt_grads, inverse[:, :, None, None], axis=1)
    return (output, input_grad, sums[0], sums[1], sums[2], sums[3], sums[4], sums[5], sums[6], sums[7], sums[8], sums[9], sums[10], sums[11])
```

```python
import functools
import math

import jax
import jax.numpy as jnp
from jax import lax
from jax.experimental import pallas as pl
from jax.experimental.pallas import tpu as pltpu
from jax.sharding import PartitionSpec as P

D = 768
HEADS = 12
HEAD_DIM = 64
FF = 3072
M = 2
EPSILON = 1e-12
NEGATIVE = -1e30
MESH = pl.DeviceIdType.MESH
BF = jnp.bfloat16
F32 = jnp.float32
LOG2E = math.log2(math.e)
VMEM_LIMIT = 62 << 20


def slope_list(head_count):

    def powers(number):
        anchor = 2.0 ** (-(2.0 ** (-(math.log2(number) - 3))))
        return [anchor ** (power_index + 1) for power_index in range(number)]

    closest = 2 ** int(math.floor(math.log2(head_count)))
    return powers(closest) + powers(2 * closest)[0::2][: head_count - closest]


def layer_norm(inputs, gain_row, offset_row):
    centre = inputs - jnp.mean(inputs, axis=-1, keepdims=True)
    spread = jnp.mean(centre * centre, axis=-1, keepdims=True)
    return centre * lax.rsqrt(spread + EPSILON) * gain_row + offset_row


def gated_unit(gate_up):
    return jax.nn.gelu(gate_up[:, :FF], approximate=False) * gate_up[:, FF:]


def rows_product(former, latter):
    return lax.dot_general(
        former, latter, (((0,), (0,)), ((), ())), preferred_element_type=jnp.float32
    )


def by_transpose(former, latter):
    return lax.dot_general(
        former, latter, (((1,), (1,)), ((), ())), preferred_element_type=jnp.float32
    )


def plain_product(former, latter):
    return jnp.dot(former, latter, preferred_element_type=jnp.float32)


def masked_scores(heads_q, heads_k, position, key_place, length, slopes):
    raw_scores = (
        jnp.einsum("qhd,khd->hqk", heads_q, heads_k, preferred_element_type=jnp.float32) * 0.125
    )
    distance = jnp.abs(position[:, None] - key_place[None, :]).astype(jnp.float32)
    raw_scores = raw_scores - slopes[:, None, None] * distance[None]
    return jnp.where((key_place < length)[None, None, :], raw_scores, NEGATIVE)


def fetch_weights(shards):
    return (
        lax.all_gather(shards[0], "fsdp", axis=0, tiled=True),
        lax.all_gather(shards[1], "fsdp", axis=0, tiled=True),
        lax.all_gather(shards[2], "fsdp", axis=0, tiled=True),
        lax.all_gather(shards[3], "fsdp", axis=0, tiled=True),
        lax.all_gather(shards[4], "fsdp", axis=0, tiled=True),
        lax.all_gather(shards[5], "fsdp", axis=0, tiled=True),
        lax.all_gather(shards[6], "fsdp", axis=0, tiled=True),
        lax.all_gather(shards[7], "fsdp", axis=0, tiled=True),
        lax.all_gather(shards[8], "fsdp", axis=0, tiled=True),
        lax.all_gather(shards[9], "fsdp", axis=0, tiled=True),
        lax.all_gather(shards[10], "fsdp", axis=0, tiled=True),
        lax.all_gather(shards[11], "fsdp", axis=0, tiled=True),
    )


def reduce_grads(grad_terms):
    shard_sums = (
        lax.psum_scatter(grad_terms[0], "fsdp", scatter_dimension=0, tiled=True),
        lax.psum_scatter(grad_terms[1], "fsdp", scatter_dimension=0, tiled=True),
        lax.psum_scatter(grad_terms[2], "fsdp", scatter_dimension=0, tiled=True),
        lax.psum_scatter(grad_terms[3], "fsdp", scatter_dimension=0, tiled=True),
        lax.psum_scatter(grad_terms[4], "fsdp", scatter_dimension=0, tiled=True),
        lax.psum_scatter(grad_terms[5], "fsdp", scatter_dimension=0, tiled=True),
        lax.psum_scatter(grad_terms[6], "fsdp", scatter_dimension=0, tiled=True),
        lax.psum_scatter(grad_terms[7], "fsdp", scatter_dimension=0, tiled=True),
        lax.psum_scatter(grad_terms[8], "fsdp", scatter_dimension=0, tiled=True),
        lax.psum_scatter(grad_terms[9], "fsdp", scatter_dimension=0, tiled=True),
        lax.psum_scatter(grad_terms[10], "fsdp", scatter_dimension=0, tiled=True),
        lax.psum_scatter(grad_terms[11], "fsdp", scatter_dimension=0, tiled=True),
    )
    return (
        lax.psum(shard_sums[0].astype(jnp.bfloat16), "ctx").astype(jnp.float32),
        lax.psum(shard_sums[1].astype(jnp.bfloat16), "ctx").astype(jnp.float32),
        lax.psum(shard_sums[2].astype(jnp.bfloat16), "ctx").astype(jnp.float32),
        lax.psum(shard_sums[3].astype(jnp.bfloat16), "ctx").astype(jnp.float32),
        lax.psum(shard_sums[4].astype(jnp.bfloat16), "ctx").astype(jnp.float32),
        lax.psum(shard_sums[5].astype(jnp.bfloat16), "ctx").astype(jnp.float32),
        lax.psum(shard_sums[6].astype(jnp.bfloat16), "ctx").astype(jnp.float32),
        lax.psum(shard_sums[7].astype(jnp.bfloat16), "ctx").astype(jnp.float32),
        lax.psum(shard_sums[8].astype(jnp.bfloat16), "ctx").astype(jnp.float32),
        lax.psum(shard_sums[9].astype(jnp.bfloat16), "ctx").astype(jnp.float32),
        lax.psum(shard_sums[10].astype(jnp.bfloat16), "ctx").astype(jnp.float32),
        lax.psum(shard_sums[11].astype(jnp.bfloat16), "ctx").astype(jnp.float32),
    )


def per_device_plain(
    tokens_in,
    out_grad,
    seq_lengths,
    order,
    w_qkv,
    bias_q,
    bias_v,
    w_out,
    bias_out,
    ln1_gain,
    ln1_bias,
    w_gate_up,
    w_down,
    bias_down,
    ln2_gain,
    ln2_bias,
):
    shards = (
        w_qkv,
        bias_q,
        bias_v,
        w_out,
        bias_out,
        ln1_gain,
        ln1_bias,
        w_gate_up,
        w_down,
        bias_down,
        ln2_gain,
        ln2_bias,
    )
    group_index = lax.axis_index("fsdp")
    ctx_index = lax.axis_index("ctx")
    dealt_tokens = jnp.take_along_axis(tokens_in, order[:, :, None, None], axis=1)
    tokens_grp, grads_grp = (
        lax.all_to_all(dealt_tokens, "fsdp", split_axis=1, concat_axis=2, tiled=True),
        lax.all_to_all(out_grad, "fsdp", split_axis=1, concat_axis=2, tiled=True),
    )
    dealt_lengths = jnp.take_along_axis(seq_lengths, order, axis=1)
    local_rows = tokens_grp.shape[2]
    key_place = jnp.arange(local_rows * lax.axis_size("ctx"))
    position = ctx_index * local_rows + jnp.arange(local_rows)
    slopes = jnp.array(slope_list(HEADS), jnp.float32)
    output_list = []
    input_list = []
    running = None
    for micro_batch in range(M):
        weights = fetch_weights(shards)
        (
            full_qkv,
            full_bias_q,
            full_bias_v,
            full_out,
            full_bias_out,
            full_ln1_gain,
            full_ln1_bias,
            full_gate_up,
            full_down,
            full_bias_down,
            full_ln2_gain,
            full_ln2_bias,
        ) = weights
        tokens = tokens_grp[micro_batch, 0]
        cotangent = grads_grp[micro_batch, 0]
        length = lax.dynamic_index_in_dim(
            dealt_lengths[micro_batch], group_index, 0, keepdims=False
        )
        valid_rows = position < length
        projected = plain_product(tokens, full_qkv)
        queries = (projected[:, :D] + full_bias_q.astype(jnp.float32)).astype(jnp.bfloat16)
        key_rows = projected[:, D : 2 * D].astype(jnp.bfloat16)
        values = (projected[:, 2 * D :] + full_bias_v.astype(jnp.float32)).astype(jnp.bfloat16)
        keys_all, values_all = (
            lax.all_gather(key_rows, "ctx", axis=0, tiled=True),
            lax.all_gather(values, "ctx", axis=0, tiled=True),
        )
        heads_q = queries.reshape(local_rows, HEADS, HEAD_DIM)
        heads_k = keys_all.reshape(-1, HEADS, HEAD_DIM)
        heads_v = values_all.reshape(-1, HEADS, HEAD_DIM)
        scores = masked_scores(heads_q, heads_k, position, key_place, length, slopes)
        row_max = jnp.max(scores, axis=-1, keepdims=True)
        exp_terms = jnp.exp(scores - row_max)
        row_total = jnp.sum(exp_terms, axis=-1, keepdims=True)
        log_total = row_max + jnp.log(row_total)
        attn_probs = (exp_terms / row_total).astype(jnp.bfloat16)
        context = (
            jnp.einsum("hqk,khd->qhd", attn_probs, heads_v, preferred_element_type=jnp.float32)
            .reshape(local_rows, D)
            .astype(jnp.bfloat16)
        )
        attn_out = plain_product(context, full_out) + full_bias_out.astype(jnp.float32)
        first_sum = tokens.astype(jnp.float32) + attn_out
        normed_one, norm_one_pull = jax.vjp(
            layer_norm,
            first_sum,
            full_ln1_gain.astype(jnp.float32),
            full_ln1_bias.astype(jnp.float32),
        )
        normed_low = normed_one.astype(jnp.bfloat16)
        gate_up = plain_product(normed_low, full_gate_up)
        hidden, gated_pull = jax.vjp(gated_unit, gate_up)
        hidden_low = hidden.astype(jnp.bfloat16)
        branch = plain_product(hidden_low, full_down) + full_bias_down.astype(jnp.float32)
        result, norm_two_pull = jax.vjp(
            layer_norm,
            normed_one + branch,
            full_ln2_gain.astype(jnp.float32),
            full_ln2_bias.astype(jnp.float32),
        )
        output_list.append(jnp.where(valid_rows[:, None], result, 0.0).astype(jnp.bfloat16))
        grad_result = jnp.where(valid_rows[:, None], cotangent.astype(jnp.float32), 0.0)
        grad_second, grad_ln2_gain, grad_ln2_bias = norm_two_pull(grad_result)
        grad_branch = grad_second.astype(jnp.bfloat16)
        grad_bias_down = jnp.sum(grad_branch.astype(jnp.float32), axis=0)
        grad_w_down = rows_product(hidden_low, grad_branch)
        grad_hidden = by_transpose(grad_branch, full_down)
        (grad_gate_up,) = gated_pull(grad_hidden)
        grad_gate_low = grad_gate_up.astype(jnp.bfloat16)
        grad_w_gate_up = rows_product(normed_low, grad_gate_low)
        grad_normed = grad_second + by_transpose(grad_gate_low, full_gate_up)
        grad_first, grad_ln1_gain, grad_ln1_bias = norm_one_pull(grad_normed)
        grad_attn = grad_first.astype(jnp.bfloat16)
        grad_bias_out = jnp.sum(grad_attn.astype(jnp.float32), axis=0)
        grad_w_out = rows_product(context, grad_attn)
        grad_context = (
            by_transpose(grad_attn, full_out)
            .astype(jnp.bfloat16)
            .reshape(local_rows, HEADS, HEAD_DIM)
        )
        scores = masked_scores(heads_q, heads_k, position, key_place, length, slopes)
        attn_exact = jnp.exp(scores - log_total)
        grad_values_term = jnp.einsum(
            "hqk,qhd->khd",
            attn_exact.astype(jnp.bfloat16),
            grad_context,
            preferred_element_type=jnp.float32,
        )
        grad_probs = jnp.einsum(
            "qhd,khd->hqk", grad_context, heads_v, preferred_element_type=jnp.float32
        )
        grad_scores = (
            attn_exact * (grad_probs - jnp.sum(attn_exact * grad_probs, axis=-1, keepdims=True))
        ).astype(jnp.bfloat16)
        grad_queries = (
            jnp.einsum("hqk,khd->qhd", grad_scores, heads_k, preferred_element_type=jnp.float32)
            * 0.125
        ).reshape(local_rows, D)
        grad_keys_term = (
            jnp.einsum("hqk,qhd->khd", grad_scores, heads_q, preferred_element_type=jnp.float32)
            * 0.125
        )
        grad_keys, grad_values = (
            lax.psum_scatter(
                grad_keys_term.reshape(-1, D).astype(jnp.bfloat16),
                "ctx",
                scatter_dimension=0,
                tiled=True,
            ).astype(jnp.float32),
            lax.psum_scatter(
                grad_values_term.reshape(-1, D).astype(jnp.bfloat16),
                "ctx",
                scatter_dimension=0,
                tiled=True,
            ).astype(jnp.float32),
        )
        grad_qkv = jnp.concatenate(
            [
                grad_queries.astype(jnp.bfloat16),
                grad_keys.astype(jnp.bfloat16),
                grad_values.astype(jnp.bfloat16),
            ],
            axis=1,
        )
        grad_w_qkv = rows_product(tokens, grad_qkv)
        grad_bias_q = jnp.sum(grad_qkv[:, :D].astype(jnp.float32), axis=0)
        grad_bias_v = jnp.sum(grad_qkv[:, 2 * D :].astype(jnp.float32), axis=0)
        grad_tokens = grad_first + by_transpose(grad_qkv, full_qkv)
        input_list.append(grad_tokens.astype(jnp.bfloat16))
        grad_terms = (
            grad_w_qkv,
            grad_bias_q,
            grad_bias_v,
            grad_w_out,
            grad_bias_out,
            grad_ln1_gain,
            grad_ln1_bias,
            grad_w_gate_up,
            grad_w_down,
            grad_bias_down,
            grad_ln2_gain,
            grad_ln2_bias,
        )
        reduced = reduce_grads(grad_terms)
        if micro_batch == 0:
            running = reduced
        else:
            running = tuple((left_sum + right_sum for left_sum, right_sum in zip(running, reduced)))
    output_stack = jnp.stack(output_list, axis=0)[:, None]
    input_stack = jnp.stack(input_list, axis=0)[:, None]
    output, dealt_grads = (
        lax.all_to_all(output_stack, "fsdp", split_axis=2, concat_axis=1, tiled=True),
        lax.all_to_all(input_stack, "fsdp", split_axis=2, concat_axis=1, tiled=True),
    )
    inverse = jnp.argsort(order, axis=1)
    input_grad = jnp.take_along_axis(dealt_grads, inverse[:, :, None, None], axis=1)
    return (
        output,
        input_grad,
        running[0],
        running[1],
        running[2],
        running[3],
        running[4],
        running[5],
        running[6],
        running[7],
        running[8],
        running[9],
        running[10],
        running[11],
    )


W0 = 256
W1 = 256
WIN = W0 + W1
PIECES = 16


def mm(a, b):
    return jnp.dot(a, b, preferred_element_type=F32)


def mm_nt(a, b):
    return lax.dot_general(a, b, (((1,), (1,)), ((), ())), preferred_element_type=F32)


def mm_tn(a, b):
    return lax.dot_general(a, b, (((0,), (0,)), ((), ())), preferred_element_type=F32)


def block(i, size):
    if isinstance(i, int):
        return pl.ds(i * size, size)
    return pl.ds(pl.multiple_of(i * size, size), size)


class Place:
    def __init__(self, fsdp):
        self.fsdp = fsdp
        self.total = 2 * fsdp
        self.Z = fsdp // 4
        self.x = lax.axis_index("ctx")
        self.f = lax.axis_index("fsdp")
        self.z = self.f // 4
        self.y = lax.rem(self.f // 2, 2)
        self.c = lax.rem(self.f, 2)
        self.me = self.x * fsdp + self.f
        self.cols = pl.ds(pl.multiple_of(self.x * W1, 128), WIN)
        self.give = pl.ds(pl.multiple_of(self.x * WIN, 128), W1)
        self.take = pl.ds(pl.multiple_of((1 - self.x) * WIN, 128), W1)
        self.pending = []

    def dev(self, x=None, z=None, y=None, c=None):
        x = self.x if x is None else x
        z = self.z if z is None else z
        y = self.y if y is None else y
        c = self.c if c is None else c
        return (x, z * 4 + y * 2 + c)

    def at(self, d):
        return (d // self.fsdp, lax.rem(d, self.fsdp))

    def barrier(self):
        sem = pltpu.get_barrier_semaphore()

        @pl.loop(1, self.total)
        def _(k):
            d = lax.rem(self.me + k, self.total)
            pl.semaphore_signal(sem, inc=1, device_id=self.at(d), device_id_type=MESH)

        pl.semaphore_wait(sem, self.total - 1)

    def go(self, copy, cond=None):
        if cond is None:
            copy.start()
        else:
            pl.when(cond)(copy.start)
        self.pending.append((cond, copy))

    def finish(self):
        for cond, copy in self.pending:
            if cond is None:
                copy.wait_send()
            else:
                pl.when(cond)(copy.wait_send)
        self.pending = []


def remote(src, dst, send, recv, device):
    return pltpu.make_async_remote_copy(
        src_ref=src, dst_ref=dst, send_sem=send, recv_sem=recv, device_id=device, device_id_type=MESH
    )


class Exchange:
    def __init__(self, pc, src, dst, sems, k, one=False):
        self.pc, self.src, self.dst, self.one = pc, src, dst, one
        self.send, self.recv, self.local = sems[0].at[k], sems[1].at[k], sems[2].at[k]

    def part(self, d):
        return self.src if self.one else self.src.at[d]

    def own(self):
        return pltpu.make_async_copy(self.part(self.pc.me), self.dst.at[self.pc.me], self.local)

    def start(self):
        pc = self.pc
        self.own().start()

        @pl.loop(1, pc.total)
        def _(k):
            d = lax.rem(pc.me + k, pc.total)
            remote(self.part(d), self.dst.at[pc.me], self.send, self.recv, pc.at(d)).start()

    def whole(self):
        r = self.dst.at[pl.ds(0, self.pc.total - 1)]
        return remote(r, r, self.send, self.recv, self.pc.dev(c=1 - self.pc.c))

    def wait(self):
        self.own().wait()
        self.whole().wait_recv()

    def done(self):
        self.whole().wait_send()


class Gather:
    def __init__(self, pc, own, slots, sems):
        self.pc, self.own, self.slots = pc, own, slots
        self.zs, self.zr, self.ys, self.yr, self.xs, self.xr, self.cs, self.cr, self.ls = sems

    @staticmethod
    def sems(Z):
        T = pltpu.SemaphoreType.DMA
        n = PIECES
        return [
            T((n, 2 * Z - 2)), T((n, 2 * Z - 2)), T((n, 2 * Z - 1)), T((n,)),
            T((n,)), T((n,)), T((n, 2)), T((n, 2)), T((n,)),
        ]

    def up(self):
        return jnp.minimum(self.pc.z + 1, self.pc.Z - 1)

    def down(self):
        return jnp.maximum(self.pc.z - 1, 0)

    def mine(self, p):
        pc = self.pc
        src = self.own(p, pc.cols)
        dst = self.slots(p, pc.z, pc.y, pc.c, pc.cols)
        return pltpu.make_async_copy(src, dst, self.ls.at[p])

    def start(self, p):
        pc = self.pc
        Z = pc.Z
        src = self.own(p, pc.cols)
        dst = self.slots(p, pc.z, pc.y, pc.c, pc.cols)
        self.mine(p).start()
        pc.go(remote(src, dst, self.zs.at[p, 0], self.zr.at[p, 0], pc.dev(z=self.up())), pc.z < Z - 1)
        k = Z - 1
        pc.go(remote(src, dst, self.zs.at[p, k], self.zr.at[p, k], pc.dev(z=self.down())), pc.z > 0)
        pc.go(remote(src, dst, self.ys.at[p, 0], self.yr.at[p], pc.dev(y=1 - pc.y)))

    def hop(self, p, h):
        pc = self.pc
        Z = pc.Z
        for upward in (True, False):
            k = (0 if upward else Z - 1) + h - 1
            if upward:
                z, here, onward, to = jnp.maximum(pc.z - h, 0), pc.z >= h, pc.z < Z - 1, self.up()
            else:
                z, here, onward, to = jnp.minimum(pc.z + h, Z - 1), pc.z + h < Z, pc.z > 0, self.down()
            ref = self.slots(p, z, pc.y, pc.c, pc.cols)
            pl.when(here)(remote(ref, ref, self.zs.at[p, k], self.zr.at[p, k], pc.dev(z=to)).wait_recv)
            if h < Z - 1:
                pc.go(
                    remote(ref, ref, self.zs.at[p, k + 1], self.zr.at[p, k + 1], pc.dev(z=to)),
                    jnp.logical_and(here, onward),
                )
            pc.go(remote(ref, ref, self.ys.at[p, 1 + k], self.yr.at[p], pc.dev(y=1 - pc.y)), here)

    def row(self, p):
        pc = self.pc
        ref = self.slots(p, slice(None), 1 - pc.y, pc.c, pc.cols)
        remote(ref, ref, self.ys.at[p, 0], self.yr.at[p], pc.dev(y=1 - pc.y)).wait_recv()
        self.mine(p).wait()
        ref = self.slots(p, slice(None), slice(None), pc.c, pc.give)
        pc.go(remote(ref, ref, self.xs.at[p], self.xr.at[p], pc.dev(x=1 - pc.x)))
        ref = self.slots(p, slice(None), slice(None), pc.c, pc.cols)
        pc.go(remote(ref, ref, self.cs.at[p, 0], self.cr.at[p, 0], pc.dev(c=1 - pc.c)))

    def plane(self, p):
        pc = self.pc
        ref = self.slots(p, slice(None), slice(None), pc.c, pc.take)
        remote(ref, ref, self.xs.at[p], self.xr.at[p], pc.dev(x=1 - pc.x)).wait_recv()
        pc.go(remote(ref, ref, self.cs.at[p, 1], self.cr.at[p, 1], pc.dev(c=1 - pc.c)))

    def core(self, p):
        pc = self.pc
        for k, cols in ((0, pc.cols), (1, pc.take)):
            ref = self.slots(p, slice(None), slice(None), 1 - pc.c, cols)
            remote(ref, ref, self.cs.at[p, k], self.cr.at[p, k], pc.dev(c=1 - pc.c)).wait_recv()


class Scatter:
    def __init__(self, pc, acc, from_c, from_x, from_y, from_z, from_f, sems):
        self.pc, self.acc = pc, acc
        self.from_c, self.from_x, self.from_y, self.from_z, self.from_f = from_c, from_x, from_y, from_z, from_f
        self.cs, self.cr, self.xs, self.xr, self.ys, self.yr, self.zs, self.zr, self.fs, self.fr, self.ls = sems
        z = pc.z
        self.inner = jnp.logical_or(z == 1, z == 2)
        self.outer = jnp.logical_not(self.inner)
        self.mate = z + 1 - 2 * lax.rem(z, 2)
        self.far_in = jnp.where(z < 2, 2, 1)
        self.far_out = jnp.where(z < 2, 3, 0)

    @staticmethod
    def sems():
        T = pltpu.SemaphoreType.DMA
        n = PIECES
        return [
            T((n,)), T((n,)), T((n,)), T((n,)), T((n,)), T((n,)), T((n, 5)), T((n, 4)), T((n,)), T((n,)), T((n,)),
        ]

    @staticmethod
    def buffers(Z, rows):
        n = PIECES
        return [
            pltpu.VMEM((n, Z, 2, rows, D), BF),
            pltpu.VMEM((n, Z, 2, rows, D), BF),
            pltpu.VMEM((n, Z, 2, rows, W1), BF),
            pltpu.VMEM((n, Z, rows, WIN), BF),
            pltpu.VMEM((n, 4, rows, WIN), BF),
            pltpu.VMEM((n, rows, WIN), BF),
        ]

    def load(self, p, terms):
        return pltpu.make_async_copy(terms(self.pc.c), self.acc.at[p], self.ls.at[p])

    def start(self, p, terms):
        pc = self.pc
        pc.go(remote(terms(1 - pc.c), self.from_c.at[p], self.cs.at[p], self.cr.at[p], pc.dev(c=1 - pc.c)))

    def core(self, p):
        pc = self.pc
        ref = self.from_c.at[p]
        remote(ref, ref, self.cs.at[p], self.cr.at[p], pc.dev(c=1 - pc.c)).wait_recv()

        @pl.loop(0, 2 * pc.Z)
        def _(k):
            z, y = k // 2, lax.rem(k, 2)
            self.acc[p, z, y] = self.acc[p, z, y] + self.from_c[p, z, y]

        src = self.acc.at[p, :, :, :, pc.take]
        pc.go(remote(src, self.from_x.at[p], self.xs.at[p], self.xr.at[p], pc.dev(x=1 - pc.x)))

    def plane(self, p):
        pc = self.pc
        ref = self.from_x.at[p]
        remote(ref, ref, self.xs.at[p], self.xr.at[p], pc.dev(x=1 - pc.x)).wait_recv()

        @pl.loop(0, 2 * pc.Z)
        def _(k):
            z, y = k // 2, lax.rem(k, 2)
            self.acc[p, z, y, :, pc.give] = self.acc[p, z, y, :, pc.give] + self.from_x[p, z, y]

        src = self.acc.at[p, :, 1 - pc.y, :, pc.cols]
        pc.go(remote(src, self.from_y.at[p], self.ys.at[p], self.yr.at[p], pc.dev(y=1 - pc.y)))

    def row(self, p):
        pc = self.pc
        ref = self.from_y.at[p]
        remote(ref, ref, self.ys.at[p], self.yr.at[p], pc.dev(y=1 - pc.y)).wait_recv()

        @pl.loop(0, pc.Z)
        def _(z):
            self.acc[p, z, pc.y, :, pc.cols] = self.acc[p, z, pc.y, :, pc.cols] + self.from_y[p, z]

        for k, z in enumerate((self.mate, self.far_in, self.far_out)):
            src = self.acc.at[p, z, pc.y, :, pc.cols]
            pc.go(
                remote(src, self.from_z.at[p, k], self.zs.at[p, k], self.zr.at[p, k], pc.dev(z=self.mate)),
                self.outer if k else None,
            )

    def middle(self, p):
        pc = self.pc
        far = ((1, self.far_in), (2, self.far_out))

        @pl.when(self.inner)
        def _():
            for k, z in far:
                ref = self.from_z.at[p, k]
                remote(ref, ref, self.zs.at[p, k], self.zr.at[p, k], pc.dev(z=self.mate)).wait_recv()
                self.acc[p, z, pc.y, :, pc.cols] = self.acc[p, z, pc.y, :, pc.cols] + self.from_z[p, k]

        for k, z in far:
            src = self.acc.at[p, z, pc.y, :, pc.cols]
            pc.go(
                remote(src, self.from_z.at[p, 3], self.zs.at[p, 2 + k], self.zr.at[p, 3], pc.dev(z=z)), self.inner
            )

    def line(self, p):
        pc = self.pc
        for k in (0, 3):
            ref = self.from_z.at[p, k]
            remote(ref, ref, self.zs.at[p, k], self.zr.at[p, k], pc.dev(z=self.mate)).wait_recv()
            self.acc[p, pc.z, pc.y, :, pc.cols] = self.acc[p, pc.z, pc.y, :, pc.cols] + self.from_z[p, k]
        src = self.acc.at[p, pc.z, pc.y, :, pc.cols]
        pc.go(remote(src, self.from_f.at[p], self.fs.at[p], self.fr.at[p], pc.dev(x=1 - pc.x)))

    def last(self, p, out):
        pc = self.pc
        ref = self.from_f.at[p]
        remote(ref, ref, self.fs.at[p], self.fr.at[p], pc.dev(x=1 - pc.x)).wait_recv()
        own = self.acc.at[p, pc.z, pc.y]
        out[:, pc.give] = own[:, pc.give].astype(F32)
        theirs = pl.ds(pl.multiple_of((1 - pc.x) * W0, 128), W1)
        out[:, pc.take] = self.from_f[p, :, theirs].astype(F32)
        both = pl.ds(pl.multiple_of(pc.x * W1, 128), W0)
        shared = pl.ds(W1, W0)
        out[:, shared] = own[:, shared].astype(F32) + self.from_f[p, :, both].astype(F32)


def row_mean(v):
    return jnp.sum(v, axis=-1, keepdims=True) * (1.0 / D)


BQ, BV, BO, G1, B1, BD, G2, B2 = range(8)


def forward_kernel(
    fsdp, rows,
    length, slopes, tokens_in, grads_in, small_in, wq_in, wo_in, wg_in, wd_in,
    X, QKV, DO, LSE, H1G, OUT, WQKV, DWA, DWD, SMALLG,
    wa, wd, xs, gs, small, smallf, qkv, dist, lse, ctxt, y1, y1b, xhat, rstd, act, slope_up, zed, acc,
    dfb, tr, *sems,
):
    pc = Place(fsdp)
    Z = pc.Z
    L = pc.total * tokens_in.shape[1]
    gsems, esems, osem = sems[:9], sems[9:12], sems[12]
    w_pc = wa.shape[1:]

    def own(p, cols):
        if p < 3:
            return wq_in.at[:, pl.ds(pl.multiple_of(D * p + cols.start, 128), cols.size)]
        if p == 3:
            return wo_in.at[:, cols]
        if p < 12:
            i, j = (p - 4) // 2, (p - 4) % 2
            return wg_in.at[:, pl.ds(pl.multiple_of(FF * j + D * i + cols.start, 128), cols.size)]
        return wd_in.at[pl.ds(rows * (p - 12), rows), cols]

    def slots(p, z, y, c, cols):
        if p < 12:
            return wa.at[p, z, y, c, :, cols]
        return wd.at[z, y, c, p - 12, :, cols]

    def w_cols(p, cols):
        return wa[p, :, :, :, :, cols].reshape(D, cols.size)

    def w_all(p):
        return wa[p].reshape(D, D)

    g = Gather(pc, own, slots, gsems)
    ex_x = Exchange(pc, tokens_in, xs, esems, 0)
    ex_g = Exchange(pc, grads_in, gs, esems, 1)
    len_s = length[0]

    def tokens(r):
        n = r.size // 16
        return xs[pl.ds(r.start // 16, n)].reshape(r.size, D)

    def prepare():
        k = lax.broadcasted_iota(jnp.int32, (L, L), 0)
        q = lax.broadcasted_iota(jnp.int32, (L, L), 1)
        dist[...] = jnp.where(k < len_s, jnp.abs(k - q).astype(F32), -NEGATIVE)

    def sum_small():
        def add(i, v):
            return v + small[i].astype(F32)

        smallf[...] = lax.fori_loop(1, fsdp, add, small[0].astype(F32))

    def project(p):
        @pl.loop(0, D // 256)
        def _(t):
            cols = block(t, 256)
            r = mm(xs[...].reshape(L, D), w_cols(p, cols))
            if p != 1:
                r = r + smallf[pl.ds(BQ if p == 0 else BV, 1), cols]
            qkv[p, :, cols] = r.astype(BF)

    def attend(j):
        cols = block(j, 128)
        lane = lax.broadcasted_iota(jnp.int32, (L, 128), 1)
        q2, k2 = qkv[0, :, cols], qkv[1, :, cols]
        vt = qkv[2, :, cols].T
        for q in range(L // 256):
            qr = pl.ds(256 * q, 256)
            parts = []
            for s in range(2):
                qm = jnp.where((lane < 64) if s == 0 else (lane >= 64), q2, jnp.zeros_like(q2))
                st = mm_nt(k2, qm[256 * q : 256 * q + 256])
                st = st * (0.125 * LOG2E) - dist[:, qr] * slopes[2 * j + s]
                top = jnp.max(st, axis=0, keepdims=True)
                e = jnp.exp2(st - top)
                total = jnp.sum(e, axis=0, keepdims=True)
                lse[2 * j + s, :, qr] = top + jnp.log2(total)
                pr = (e * (1.0 / total)).astype(BF)
                parts.append(mm(vt[64 * s : 64 * s + 64], pr))
            ctxt[qr, cols] = jnp.concatenate(parts, axis=0).T.astype(BF)

    def first_norm():
        @pl.loop(0, D // 256)
        def _(t):
            cols = block(t, 256)
            acc[:, cols] = mm(ctxt[...], w_cols(3, cols)) + smallf[pl.ds(BO, 1), cols]

        @pl.loop(0, L // 64)
        def _(i):
            r = block(i, 64)
            h = acc[r, :] + tokens(r).astype(F32)
            centre = h - row_mean(h)
            rs = lax.rsqrt(row_mean(centre * centre) + EPSILON)
            xh = centre * rs
            xhat[r, :] = xh
            rstd[r, :] = jnp.broadcast_to(rs, (64, 128))
            yy = xh * smallf[pl.ds(G1, 1), :] + smallf[pl.ds(B1, 1), :]
            y1[r, :] = yy
            y1b[r, :] = yy.astype(BF)

    def gated(i, s):
        wc = block(s, 256)
        cols = block(i * 3 + s, 256)
        a = mm(y1b[...], w_cols(4 + 2 * i, wc))
        u = mm(y1b[...], w_cols(5 + 2 * i, wc))
        cdf = 0.5 + 0.5 * lax.erf(a * math.sqrt(0.5))
        pdf = jnp.exp2(a * a * (-0.5 * LOG2E)) * (1.0 / math.sqrt(2.0 * math.pi))
        gelu = a * cdf
        zed[:, cols] = (gelu * u).astype(BF)
        act[:, cols] = gelu.astype(BF)
        slope_up[:, cols] = (u * (cdf + a * pdf)).astype(BF)

    def second_norm():
        @pl.loop(0, D // 256)
        def _(t):
            cols = block(t, 256)
            w = wd[:, :, :, :, :, cols].reshape(FF, 256)
            acc[:, cols] = mm(zed[...], w) + smallf[pl.ds(BD, 1), cols]

        def step(i, sums):
            r = block(i, 64)
            h = acc[r, :] + y1[r, :]
            centre = h - row_mean(h)
            rs = lax.rsqrt(row_mean(centre * centre) + EPSILON)
            xh = centre * rs
            gain = smallf[pl.ds(G2, 1), :]
            valid = (lax.broadcasted_iota(jnp.int32, (64, D), 0) + i * 64) < len_s
            res = jnp.where(valid, xh * gain + smallf[pl.ds(B2, 1), :], 0.0).astype(BF)
            OUTV[pl.ds(i * 4, 4)] = res.reshape(4, 16, D)
            up = jnp.where(valid, gs[pl.ds(i * 4, 4)].reshape(64, D).astype(F32), 0.0)
            dx = up * gain
            dh = rs * (dx - row_mean(dx) - xh * row_mean(dx * xh))
            low = dh.astype(BF)
            acc[r, :] = dh
            dfb[r, :] = low
            sg, sb, sd = sums
            return (
                sg + jnp.sum(up * xh, axis=0, keepdims=True),
                sb + jnp.sum(up, axis=0, keepdims=True),
                sd + jnp.sum(low.astype(F32), axis=0, keepdims=True),
            )

        zero = jnp.zeros((1, D), F32)
        sg, sb, sd = lax.fori_loop(0, L // 64, step, (zero, zero, zero))
        sgrad[pl.ds(G2, 1), :] = sg
        sgrad[pl.ds(B2, 1), :] = sb
        sgrad[pl.ds(BD, 1), :] = sd

    def ff_back():
        tr[...] = y1b[...].T

        @pl.loop(0, FF // D)
        def _(i):
            cols = block(i, D)
            down = wd.at[pl.ds(i * Z // 4, Z // 4)]
            dz = mm_nt(dfb[...], down[...].reshape(D, D))
            dgate = (dz * slope_up[:, cols].astype(F32)).astype(BF)
            dup = (dz * act[:, cols].astype(F32)).astype(BF)
            acc[...] += mm_nt(dgate, w_all(4 + 2 * i)) + mm_nt(dup, w_all(5 + 2 * i))
            down[...] = mm_tn(zed[:, cols], dfb[...]).astype(BF).reshape(down.shape)
            wa[4 + 2 * i] = mm(tr[...], dgate).astype(BF).reshape(w_pc)
            wa[5 + 2 * i] = mm(tr[...], dup).astype(BF).reshape(w_pc)

    def first_norm_back():
        def step(i, sums):
            r = block(i, 64)
            up = acc[r, :]
            xh = xhat[r, :]
            dx = up * smallf[pl.ds(G1, 1), :]
            dh = rstd[r, :][:, :1] * (dx - row_mean(dx) - xh * row_mean(dx * xh))
            low = dh.astype(BF)
            xhat[r, :] = dh
            dfb[r, :] = low
            sg, sb, sd = sums
            return (
                sg + jnp.sum(up * xh, axis=0, keepdims=True),
                sb + jnp.sum(up, axis=0, keepdims=True),
                sd + jnp.sum(low.astype(F32), axis=0, keepdims=True),
            )

        zero = jnp.zeros((1, D), F32)
        sg, sb, sd = lax.fori_loop(0, L // 64, step, (zero, zero, zero))
        sgrad[pl.ds(G1, 1), :] = sg
        sgrad[pl.ds(B1, 1), :] = sb
        sgrad[pl.ds(BO, 1), :] = sd

    def out_back():
        @pl.loop(0, 1)
        def _(t):
            y1b[...] = mm_nt(dfb[...], w_all(3)).astype(BF)
            wa[3] = mm_tn(ctxt[...], dfb[...]).astype(BF).reshape(w_pc)

    OUTV = sems[13]
    sgrad = sems[14]

    def keep(src, dst, k):
        c = pltpu.make_async_copy(src, dst, osem.at[k])
        c.start()
        kept.append(c)

    kept = []

    pc.barrier()
    ex_x.start()
    for k in range(1, fsdp):
        pass

    me_small = small.at[pc.f]
    loc = pltpu.make_async_copy(small_in, me_small, esems[2].at[2])
    loc.start()

    @pl.loop(1, fsdp)
    def _(k):
        f = lax.rem(pc.f + k, fsdp)
        remote(small_in, me_small, esems[0].at[2], esems[1].at[2], (pc.x, f)).start()

    small_all = remote(
        small.at[pl.ds(0, fsdp - 1)], small.at[pl.ds(0, fsdp - 1)], esems[0].at[2], esems[1].at[2],
        pc.dev(c=1 - pc.c),
    )

    def after_core(p):
        if p == 2:
            ex_x.wait()
            small_all.wait_recv()
            loc.wait()
            sum_small()
            prepare()
            for i in range(3):
                project(i)
            keep(xs, X, 0)
            keep(wa.at[pl.ds(0, 3)], WQKV, 1)
            keep(qkv, QKV, 2)
            pl.loop(0, 2)(attend)
        elif p == 3:
            pl.loop(2, 5)(attend)
        elif p == 4:
            attend(5)
            first_norm()
        elif 5 <= p < 12 and p % 2 == 1:
            for s in range(3):
                gated((p - 5) // 2, s)

    for t in range(PIECES + 8):
        if t < PIECES:
            g.start(t)
        if t == 4:
            ex_g.start()
        for h in range(1, Z):
            if 0 <= t - h < PIECES:
                g.hop(t - h, h)
        if 0 <= t - 4 < PIECES:
            g.row(t - 4)
        if 0 <= t - 6 < PIECES:
            g.plane(t - 6)
        if 0 <= t - 8 < PIECES:
            g.core(t - 8)
            after_core(t - 8)
    ex_g.wait()
    pc.finish()
    second_norm()
    keep(OUTV, OUT, 3)
    ff_back()
    keep(wa.at[pl.ds(4, 8)], DWA.at[pl.ds(1, 8)], 4)
    keep(wd, DWD, 5)
    first_norm_back()
    out_back()
    keep(wa.at[3], DWA.at[0], 6)
    keep(y1b, DO, 7)
    keep(xhat, H1G, 8)
    keep(lse, LSE, 9)
    sgrad[pl.ds(BQ, 1), :] = jnp.zeros((1, D), F32)
    sgrad[pl.ds(BV, 1), :] = jnp.zeros((1, D), F32)
    keep(sgrad, SMALLG, 10)
    ex_x.done()
    ex_g.done()
    small_all.wait_send()
    for c in kept:
        c.wait()


def backward_kernel(
    fsdp, rows,
    length, slopes, x_in, qkv_in, do_in, lse_in, h1_in, out_in, wqkv_in, dwa, dwd, small_in,
    GQ, GW, GG, GD, OUT, DX, SMALLG,
    xs, qkv, dob, lse, h1, wqkv, dist, dqkv, dwq, dxv, sgrad, gsum, *rest,
):
    pc = Place(fsdp)
    bufs, rest = rest[:6], rest[6:]
    ssems, esems, isem = rest[:11], rest[11:14], rest[14]
    L = xs.shape[0] * xs.shape[1]
    sc = Scatter(pc, *bufs, ssems)
    order = [12, 13, 14, 15] + list(range(4, 12)) + [3, 0, 1, 2]

    def terms(p):
        if p >= 12:
            return lambda c: dwd.at[:, :, c, p - 12]
        if p >= 3:
            return lambda c: dwa.at[p - 3, :, :, c]
        return lambda c: dwq.at[p, :, :, c]

    def out_of(p):
        if p >= 12:
            return GD.at[pl.ds(rows * (p - 12), rows)]
        if p == 3:
            return GW
        if p < 3:
            return GQ.at[:, pl.ds(D * p, D)]
        i, j = (p - 4) // 2, (p - 4) % 2
        return GG.at[:, pl.ds(FF * j + D * i, D)]

    loads = [
        pltpu.make_async_copy(s, d, isem.at[k])
        for k, (s, d) in enumerate(
            ((x_in, xs), (qkv_in, qkv), (do_in, dob), (lse_in, lse), (h1_in, h1), (wqkv_in, wqkv), (small_in, sgrad))
        )
    ]
    for c in loads:
        c.start()
    len_s = length[0]
    k = lax.broadcasted_iota(jnp.int32, (L, L), 0)
    q = lax.broadcasted_iota(jnp.int32, (L, L), 1)
    dist[...] = jnp.where(k < len_s, jnp.abs(k - q).astype(F32), -NEGATIVE)

    def attend_back(j):
        cols = block(j, 128)
        lane = lax.broadcasted_iota(jnp.int32, (L, 128), 1)
        q2, k2, v2 = (qkv[i, :, cols] for i in range(3))
        do2 = dob[:, cols]
        kt = k2.T
        dv = dk = None
        for q in range(L // 256):
            qr = pl.ds(256 * q, 256)
            qs = slice(256 * q, 256 * q + 256)
            parts = []
            for s in range(2):
                half = (lane < 64) if s == 0 else (lane >= 64)
                qm = jnp.where(half, q2, jnp.zeros_like(q2))[qs]
                dm = jnp.where(half, do2, jnp.zeros_like(do2))[qs]
                st = mm_nt(k2, qm) * (0.125 * LOG2E) - dist[:, qr] * slopes[2 * j + s]
                pr = jnp.exp2(st - lse[2 * j + s, :, qr])
                dp = mm_nt(v2, dm)
                ds = (pr * (dp - jnp.sum(pr * dp, axis=0, keepdims=True))).astype(BF)
                a, b = mm(pr.astype(BF), dm), mm(ds, qm)
                dv = a if dv is None else dv + a
                dk = b if dk is None else dk + b
                parts.append(mm(kt[64 * s : 64 * s + 64], ds))
            dqkv[0, qr, cols] = (jnp.concatenate(parts, axis=0).T * 0.125).astype(BF)
        dqkv[1, :, cols] = (dk * 0.125).astype(BF)
        dqkv[2, :, cols] = dv.astype(BF)

    def weights_back(p):
        x = xs[...].reshape(L, D)
        dwq[p] = mm_tn(x, dqkv[p]).astype(BF).reshape(dwq.shape[1:])
        if p != 1:
            r = BQ if p == 0 else BV
            sgrad[pl.ds(r, 1), :] = jnp.sum(dqkv[p].astype(F32), axis=0, keepdims=True)

    def tokens_back():
        @pl.loop(0, L // 128)
        def _(i):
            r = block(i, 128)
            v = h1[r, :]
            for p in range(3):
                v = v + mm_nt(dqkv[p, r, :], wqkv[p].reshape(D, D))
            dxv[pl.ds(i * 8, 8)] = v.astype(BF).reshape(8, 16, D)

    ex_o = Exchange(pc, out_in, OUT, esems, 0)
    ex_d = Exchange(pc, dxv, DX, esems, 1)
    ex_s = Exchange(pc, sgrad, gsum, esems, 2, one=True)

    pc.barrier()
    for n in range(13):
        sc.load(order[n], terms(order[n])).start()
    stages = (("core", 1), ("plane", 3), ("row", 5), ("middle", 6), ("line", 8), ("last", 10))
    for t in range(PIECES + 10):
        if t < PIECES:
            p = order[t]
            if p < 3:
                sc.load(p, terms(p)).start()
            sc.start(p, terms(p))
        if t == 1:
            ex_o.start()
        for name, off in stages:
            if 0 <= t - off < PIECES:
                p = order[t - off]
                if name == "core":
                    sc.load(p, terms(p)).wait()
                if name == "last":
                    sc.last(p, out_of(p))
                else:
                    getattr(sc, name)(p)
        if t == 2:
            for c in loads:
                c.wait()
        if 2 <= t < 8:
            attend_back(t - 2)
        if t == 8:
            tokens_back()
            ex_d.start()
        if t == 9:
            for p in range(3):
                weights_back(p)
            ex_s.start()
    ex_s.wait()

    def add(i, v):
        return v + gsum[i]

    SMALLG[...] = lax.fori_loop(1, pc.total, add, gsum[0])
    ex_o.wait()
    ex_d.wait()
    for e in (ex_o, ex_d, ex_s):
        e.done()
    pc.finish()


def per_device(
    tokens_in, out_grad, seq_lengths, order, w_qkv, bias_q, bias_v, w_out, bias_out, ln1_gain, ln1_bias, w_gate_up,
    w_down, bias_down, ln2_gain, ln2_bias,
):
    fsdp = lax.axis_size("fsdp")
    total = 2 * fsdp
    rows = w_out.shape[0]
    slots_here = tokens_in.shape[2]
    L = slots_here * total
    Z = fsdp // 4
    f = lax.axis_index("fsdp")
    m = lax.axis_index("ctx")
    dealt = jnp.take_along_axis(tokens_in, order[:, :, None, None], axis=1).reshape(total, slots_here, D)
    grads = out_grad.reshape(total, slots_here, D)
    length = seq_lengths[m, order[m, f]].reshape(1)
    slopes = jnp.array(slope_list(HEADS), F32) * LOG2E
    small = jnp.stack([bias_q, bias_v, bias_out, ln1_gain, ln1_bias, bias_down, ln2_gain, ln2_bias])
    small = lax.dynamic_update_slice(jnp.zeros((16, D), BF), small, (0, f * rows))
    hbm = pl.BlockSpec(memory_space=pl.ANY)
    smem = pl.BlockSpec(memory_space=pltpu.SMEM)
    vmem = pl.BlockSpec(memory_space=pltpu.VMEM)
    S = jax.ShapeDtypeStruct
    T = pltpu.SemaphoreType.DMA
    V = pltpu.VMEM
    fw_outs = [
        S((total, slots_here, D), BF), S((3, L, D), BF), S((L, D), BF), S((HEADS, 1, L), F32), S((L, D), F32),
        S((total, slots_here, D), BF), S((3, Z, 2, 2, rows, D), BF), S((9, Z, 2, 2, rows, D), BF),
        S((Z, 2, 2, 4, rows, D), BF), S((8, D), F32),
    ]
    fw = pl.pallas_call(
        functools.partial(forward_kernel, fsdp, rows),
        out_shape=fw_outs,
        in_specs=[smem, smem] + [hbm] * 7,
        out_specs=[hbm] * len(fw_outs),
        scratch_shapes=[
            V((12, Z, 2, 2, rows, D), BF), V((Z, 2, 2, 4, rows, D), BF),
            V((total, slots_here, D), BF), V((total, slots_here, D), BF),
            V((fsdp, 16, D), BF), V((16, D), F32), V((3, L, D), BF), V((L, L), F32), V((HEADS, 1, L), F32),
            V((L, D), BF), V((L, D), F32), V((L, D), BF), V((L, D), F32), V((L, 128), F32),
            V((L, FF), BF), V((L, FF), BF), V((L, FF), BF), V((L, D), F32), V((L, D), BF), V((D, L), BF),
            *Gather.sems(Z), T((3,)), T((3,)), T((3,)), T((11,)), V((total, slots_here, D), BF), V((8, D), F32),
        ],
        compiler_params=pltpu.CompilerParams(collective_id=0, has_side_effects=True, vmem_limit_bytes=VMEM_LIMIT),
        name="gather_and_forward",
    )(length, slopes, dealt, grads, small, w_qkv, w_out, w_gate_up, w_down)
    x, qkv, dob, lse, h1, out, wqkv, dwa, dwd, smallg = fw
    bw_outs = [
        S((rows, 3 * D), F32), S((rows, D), F32), S((rows, 2 * FF), F32), S((4 * rows, D), F32),
        S((total, slots_here, D), BF), S((total, slots_here, D), BF), S((8, D), F32),
    ]
    gq, gw, gg, gd, output, dealt_grads, small_sum = pl.pallas_call(
        functools.partial(backward_kernel, fsdp, rows),
        out_shape=bw_outs,
        in_specs=[smem, smem] + [hbm] * 10,
        out_specs=[vmem] * 4 + [hbm] * 2 + [vmem],
        scratch_shapes=[
            V((total, slots_here, D), BF), V((3, L, D), BF), V((L, D), BF), V((HEADS, 1, L), F32), V((L, D), F32),
            V((3, Z, 2, 2, rows, D), BF), V((L, L), F32), V((3, L, D), BF), V((3, Z, 2, 2, rows, D), BF),
            V((total, slots_here, D), BF), V((8, D), F32), V((total, 8, D), F32),
            *Scatter.buffers(Z, rows), *Scatter.sems(), T((3,)), T((3,)), T((3,)), T((7,)),
        ],
        compiler_params=pltpu.CompilerParams(collective_id=1, has_side_effects=True, vmem_limit_bytes=VMEM_LIMIT),
        name="backward_and_scatter",
    )(length, slopes, x, qkv, dob, lse, h1, out, wqkv, dwa, dwd, smallg)
    inverse = jnp.argsort(order, axis=1)
    input_grad = jnp.take_along_axis(
        dealt_grads.reshape(tokens_in.shape), inverse[:, :, None, None], axis=1
    )
    mine = lax.dynamic_slice(small_sum, (0, f * rows), (8, rows))
    return (
        output.reshape(tokens_in.shape), input_grad, gq, mine[BQ], mine[BV], gw, mine[BO], mine[G1], mine[B1], gg, gd,
        mine[BD], mine[G2], mine[B2],
    )


def solution(mesh):
    fsdp = mesh.shape["fsdp"]
    rows = D // fsdp
    kernels = mesh.shape["ctx"] == M and fsdp == 16 and rows % 16 == 0
    return jax.shard_map(
        per_device if kernels else per_device_plain,
        mesh=mesh,
        in_specs=(
            P(None, None, ("ctx", "fsdp"), None),
            P(None, None, ("ctx", "fsdp"), None),
            P(),
            P(),
            P("fsdp", None),
            P("fsdp"),
            P("fsdp"),
            P("fsdp", None),
            P("fsdp"),
            P("fsdp"),
            P("fsdp"),
            P("fsdp", None),
            P("fsdp", None),
            P("fsdp"),
            P("fsdp"),
            P("fsdp"),
        ),
        out_specs=(
            P(None, None, ("ctx", "fsdp"), None),
            P(None, None, ("ctx", "fsdp"), None),
            P("fsdp", None),
            P("fsdp"),
            P("fsdp"),
            P("fsdp", None),
            P("fsdp"),
            P("fsdp"),
            P("fsdp"),
            P("fsdp", None),
            P("fsdp", None),
            P("fsdp"),
            P("fsdp"),
            P("fsdp"),
        ),
        check_vma=False,
    )
```

```python
import functools
import math

import jax
import jax.numpy as jnp
from jax import lax
from jax.experimental import pallas as pl
from jax.experimental.pallas import tpu as pltpu
from jax.sharding import PartitionSpec as P

D = 768
HEADS = 12
HEAD_DIM = 64
FF = 3072
M = 2
EPSILON = 1e-12
NEGATIVE = -1e30
MESH = pl.DeviceIdType.MESH
BF = jnp.bfloat16
F32 = jnp.float32
LOG2E = math.log2(math.e)
VMEM_LIMIT = 62 << 20


def slope_list(head_count):

    def powers(number):
        anchor = 2.0 ** (-(2.0 ** (-(math.log2(number) - 3))))
        return [anchor ** (power_index + 1) for power_index in range(number)]

    closest = 2 ** int(math.floor(math.log2(head_count)))
    return powers(closest) + powers(2 * closest)[0::2][: head_count - closest]


def layer_norm(inputs, gain_row, offset_row):
    centre = inputs - jnp.mean(inputs, axis=-1, keepdims=True)
    spread = jnp.mean(centre * centre, axis=-1, keepdims=True)
    return centre * lax.rsqrt(spread + EPSILON) * gain_row + offset_row


def gated_unit(gate_up):
    return jax.nn.gelu(gate_up[:, :FF], approximate=False) * gate_up[:, FF:]


def rows_product(former, latter):
    return lax.dot_general(
        former, latter, (((0,), (0,)), ((), ())), preferred_element_type=jnp.float32
    )


def by_transpose(former, latter):
    return lax.dot_general(
        former, latter, (((1,), (1,)), ((), ())), preferred_element_type=jnp.float32
    )


def plain_product(former, latter):
    return jnp.dot(former, latter, preferred_element_type=jnp.float32)


def masked_scores(heads_q, heads_k, position, key_place, length, slopes):
    raw_scores = (
        jnp.einsum("qhd,khd->hqk", heads_q, heads_k, preferred_element_type=jnp.float32) * 0.125
    )
    distance = jnp.abs(position[:, None] - key_place[None, :]).astype(jnp.float32)
    raw_scores = raw_scores - slopes[:, None, None] * distance[None]
    return jnp.where((key_place < length)[None, None, :], raw_scores, NEGATIVE)


def fetch_weights(shards):
    return (
        lax.all_gather(shards[0], "fsdp", axis=0, tiled=True),
        lax.all_gather(shards[1], "fsdp", axis=0, tiled=True),
        lax.all_gather(shards[2], "fsdp", axis=0, tiled=True),
        lax.all_gather(shards[3], "fsdp", axis=0, tiled=True),
        lax.all_gather(shards[4], "fsdp", axis=0, tiled=True),
        lax.all_gather(shards[5], "fsdp", axis=0, tiled=True),
        lax.all_gather(shards[6], "fsdp", axis=0, tiled=True),
        lax.all_gather(shards[7], "fsdp", axis=0, tiled=True),
        lax.all_gather(shards[8], "fsdp", axis=0, tiled=True),
        lax.all_gather(shards[9], "fsdp", axis=0, tiled=True),
        lax.all_gather(shards[10], "fsdp", axis=0, tiled=True),
        lax.all_gather(shards[11], "fsdp", axis=0, tiled=True),
    )


def reduce_grads(grad_terms):
    shard_sums = (
        lax.psum_scatter(grad_terms[0], "fsdp", scatter_dimension=0, tiled=True),
        lax.psum_scatter(grad_terms[1], "fsdp", scatter_dimension=0, tiled=True),
        lax.psum_scatter(grad_terms[2], "fsdp", scatter_dimension=0, tiled=True),
        lax.psum_scatter(grad_terms[3], "fsdp", scatter_dimension=0, tiled=True),
        lax.psum_scatter(grad_terms[4], "fsdp", scatter_dimension=0, tiled=True),
        lax.psum_scatter(grad_terms[5], "fsdp", scatter_dimension=0, tiled=True),
        lax.psum_scatter(grad_terms[6], "fsdp", scatter_dimension=0, tiled=True),
        lax.psum_scatter(grad_terms[7], "fsdp", scatter_dimension=0, tiled=True),
        lax.psum_scatter(grad_terms[8], "fsdp", scatter_dimension=0, tiled=True),
        lax.psum_scatter(grad_terms[9], "fsdp", scatter_dimension=0, tiled=True),
        lax.psum_scatter(grad_terms[10], "fsdp", scatter_dimension=0, tiled=True),
        lax.psum_scatter(grad_terms[11], "fsdp", scatter_dimension=0, tiled=True),
    )
    return (
        lax.psum(shard_sums[0].astype(jnp.bfloat16), "ctx").astype(jnp.float32),
        lax.psum(shard_sums[1].astype(jnp.bfloat16), "ctx").astype(jnp.float32),
        lax.psum(shard_sums[2].astype(jnp.bfloat16), "ctx").astype(jnp.float32),
        lax.psum(shard_sums[3].astype(jnp.bfloat16), "ctx").astype(jnp.float32),
        lax.psum(shard_sums[4].astype(jnp.bfloat16), "ctx").astype(jnp.float32),
        lax.psum(shard_sums[5].astype(jnp.bfloat16), "ctx").astype(jnp.float32),
        lax.psum(shard_sums[6].astype(jnp.bfloat16), "ctx").astype(jnp.float32),
        lax.psum(shard_sums[7].astype(jnp.bfloat16), "ctx").astype(jnp.float32),
        lax.psum(shard_sums[8].astype(jnp.bfloat16), "ctx").astype(jnp.float32),
        lax.psum(shard_sums[9].astype(jnp.bfloat16), "ctx").astype(jnp.float32),
        lax.psum(shard_sums[10].astype(jnp.bfloat16), "ctx").astype(jnp.float32),
        lax.psum(shard_sums[11].astype(jnp.bfloat16), "ctx").astype(jnp.float32),
    )


def per_device_plain(
    tokens_in,
    out_grad,
    seq_lengths,
    order,
    w_qkv,
    bias_q,
    bias_v,
    w_out,
    bias_out,
    ln1_gain,
    ln1_bias,
    w_gate_up,
    w_down,
    bias_down,
    ln2_gain,
    ln2_bias,
):
    shards = (
        w_qkv,
        bias_q,
        bias_v,
        w_out,
        bias_out,
        ln1_gain,
        ln1_bias,
        w_gate_up,
        w_down,
        bias_down,
        ln2_gain,
        ln2_bias,
    )
    group_index = lax.axis_index("fsdp")
    ctx_index = lax.axis_index("ctx")
    dealt_tokens = jnp.take_along_axis(tokens_in, order[:, :, None, None], axis=1)
    tokens_grp, grads_grp = (
        lax.all_to_all(dealt_tokens, "fsdp", split_axis=1, concat_axis=2, tiled=True),
        lax.all_to_all(out_grad, "fsdp", split_axis=1, concat_axis=2, tiled=True),
    )
    dealt_lengths = jnp.take_along_axis(seq_lengths, order, axis=1)
    local_rows = tokens_grp.shape[2]
    key_place = jnp.arange(local_rows * lax.axis_size("ctx"))
    position = ctx_index * local_rows + jnp.arange(local_rows)
    slopes = jnp.array(slope_list(HEADS), jnp.float32)
    output_list = []
    input_list = []
    running = None
    for micro_batch in range(M):
        weights = fetch_weights(shards)
        (
            full_qkv,
            full_bias_q,
            full_bias_v,
            full_out,
            full_bias_out,
            full_ln1_gain,
            full_ln1_bias,
            full_gate_up,
            full_down,
            full_bias_down,
            full_ln2_gain,
            full_ln2_bias,
        ) = weights
        tokens = tokens_grp[micro_batch, 0]
        cotangent = grads_grp[micro_batch, 0]
        length = lax.dynamic_index_in_dim(
            dealt_lengths[micro_batch], group_index, 0, keepdims=False
        )
        valid_rows = position < length
        projected = plain_product(tokens, full_qkv)
        queries = (projected[:, :D] + full_bias_q.astype(jnp.float32)).astype(jnp.bfloat16)
        key_rows = projected[:, D : 2 * D].astype(jnp.bfloat16)
        values = (projected[:, 2 * D :] + full_bias_v.astype(jnp.float32)).astype(jnp.bfloat16)
        keys_all, values_all = (
            lax.all_gather(key_rows, "ctx", axis=0, tiled=True),
            lax.all_gather(values, "ctx", axis=0, tiled=True),
        )
        heads_q = queries.reshape(local_rows, HEADS, HEAD_DIM)
        heads_k = keys_all.reshape(-1, HEADS, HEAD_DIM)
        heads_v = values_all.reshape(-1, HEADS, HEAD_DIM)
        scores = masked_scores(heads_q, heads_k, position, key_place, length, slopes)
        row_max = jnp.max(scores, axis=-1, keepdims=True)
        exp_terms = jnp.exp(scores - row_max)
        row_total = jnp.sum(exp_terms, axis=-1, keepdims=True)
        log_total = row_max + jnp.log(row_total)
        attn_probs = (exp_terms / row_total).astype(jnp.bfloat16)
        context = (
            jnp.einsum("hqk,khd->qhd", attn_probs, heads_v, preferred_element_type=jnp.float32)
            .reshape(local_rows, D)
            .astype(jnp.bfloat16)
        )
        attn_out = plain_product(context, full_out) + full_bias_out.astype(jnp.float32)
        first_sum = tokens.astype(jnp.float32) + attn_out
        normed_one, norm_one_pull = jax.vjp(
            layer_norm,
            first_sum,
            full_ln1_gain.astype(jnp.float32),
            full_ln1_bias.astype(jnp.float32),
        )
        normed_low = normed_one.astype(jnp.bfloat16)
        gate_up = plain_product(normed_low, full_gate_up)
        hidden, gated_pull = jax.vjp(gated_unit, gate_up)
        hidden_low = hidden.astype(jnp.bfloat16)
        branch = plain_product(hidden_low, full_down) + full_bias_down.astype(jnp.float32)
        result, norm_two_pull = jax.vjp(
            layer_norm,
            normed_one + branch,
            full_ln2_gain.astype(jnp.float32),
            full_ln2_bias.astype(jnp.float32),
        )
        output_list.append(jnp.where(valid_rows[:, None], result, 0.0).astype(jnp.bfloat16))
        grad_result = jnp.where(valid_rows[:, None], cotangent.astype(jnp.float32), 0.0)
        grad_second, grad_ln2_gain, grad_ln2_bias = norm_two_pull(grad_result)
        grad_branch = grad_second.astype(jnp.bfloat16)
        grad_bias_down = jnp.sum(grad_branch.astype(jnp.float32), axis=0)
        grad_w_down = rows_product(hidden_low, grad_branch)
        grad_hidden = by_transpose(grad_branch, full_down)
        (grad_gate_up,) = gated_pull(grad_hidden)
        grad_gate_low = grad_gate_up.astype(jnp.bfloat16)
        grad_w_gate_up = rows_product(normed_low, grad_gate_low)
        grad_normed = grad_second + by_transpose(grad_gate_low, full_gate_up)
        grad_first, grad_ln1_gain, grad_ln1_bias = norm_one_pull(grad_normed)
        grad_attn = grad_first.astype(jnp.bfloat16)
        grad_bias_out = jnp.sum(grad_attn.astype(jnp.float32), axis=0)
        grad_w_out = rows_product(context, grad_attn)
        grad_context = (
            by_transpose(grad_attn, full_out)
            .astype(jnp.bfloat16)
            .reshape(local_rows, HEADS, HEAD_DIM)
        )
        scores = masked_scores(heads_q, heads_k, position, key_place, length, slopes)
        attn_exact = jnp.exp(scores - log_total)
        grad_values_term = jnp.einsum(
            "hqk,qhd->khd",
            attn_exact.astype(jnp.bfloat16),
            grad_context,
            preferred_element_type=jnp.float32,
        )
        grad_probs = jnp.einsum(
            "qhd,khd->hqk", grad_context, heads_v, preferred_element_type=jnp.float32
        )
        grad_scores = (
            attn_exact * (grad_probs - jnp.sum(attn_exact * grad_probs, axis=-1, keepdims=True))
        ).astype(jnp.bfloat16)
        grad_queries = (
            jnp.einsum("hqk,khd->qhd", grad_scores, heads_k, preferred_element_type=jnp.float32)
            * 0.125
        ).reshape(local_rows, D)
        grad_keys_term = (
            jnp.einsum("hqk,qhd->khd", grad_scores, heads_q, preferred_element_type=jnp.float32)
            * 0.125
        )
        grad_keys, grad_values = (
            lax.psum_scatter(
                grad_keys_term.reshape(-1, D).astype(jnp.bfloat16),
                "ctx",
                scatter_dimension=0,
                tiled=True,
            ).astype(jnp.float32),
            lax.psum_scatter(
                grad_values_term.reshape(-1, D).astype(jnp.bfloat16),
                "ctx",
                scatter_dimension=0,
                tiled=True,
            ).astype(jnp.float32),
        )
        grad_qkv = jnp.concatenate(
            [
                grad_queries.astype(jnp.bfloat16),
                grad_keys.astype(jnp.bfloat16),
                grad_values.astype(jnp.bfloat16),
            ],
            axis=1,
        )
        grad_w_qkv = rows_product(tokens, grad_qkv)
        grad_bias_q = jnp.sum(grad_qkv[:, :D].astype(jnp.float32), axis=0)
        grad_bias_v = jnp.sum(grad_qkv[:, 2 * D :].astype(jnp.float32), axis=0)
        grad_tokens = grad_first + by_transpose(grad_qkv, full_qkv)
        input_list.append(grad_tokens.astype(jnp.bfloat16))
        grad_terms = (
            grad_w_qkv,
            grad_bias_q,
            grad_bias_v,
            grad_w_out,
            grad_bias_out,
            grad_ln1_gain,
            grad_ln1_bias,
            grad_w_gate_up,
            grad_w_down,
            grad_bias_down,
            grad_ln2_gain,
            grad_ln2_bias,
        )
        reduced = reduce_grads(grad_terms)
        if micro_batch == 0:
            running = reduced
        else:
            running = tuple((left_sum + right_sum for left_sum, right_sum in zip(running, reduced)))
    output_stack = jnp.stack(output_list, axis=0)[:, None]
    input_stack = jnp.stack(input_list, axis=0)[:, None]
    output, dealt_grads = (
        lax.all_to_all(output_stack, "fsdp", split_axis=2, concat_axis=1, tiled=True),
        lax.all_to_all(input_stack, "fsdp", split_axis=2, concat_axis=1, tiled=True),
    )
    inverse = jnp.argsort(order, axis=1)
    input_grad = jnp.take_along_axis(dealt_grads, inverse[:, :, None, None], axis=1)
    return (
        output,
        input_grad,
        running[0],
        running[1],
        running[2],
        running[3],
        running[4],
        running[5],
        running[6],
        running[7],
        running[8],
        running[9],
        running[10],
        running[11],
    )


W0 = 256
W1 = 256
WIN = W0 + W1
PIECES = 16
RING = 4


def mm(a, b):
    return jnp.dot(a, b, preferred_element_type=F32)


def mm_nt(a, b):
    return lax.dot_general(a, b, (((1,), (1,)), ((), ())), preferred_element_type=F32)


def mm_tn(a, b):
    return lax.dot_general(a, b, (((0,), (0,)), ((), ())), preferred_element_type=F32)


def block(i, size):
    if isinstance(i, int):
        return pl.ds(i * size, size)
    return pl.ds(pl.multiple_of(i * size, size), size)


class Place:
    def __init__(self, fsdp):
        self.fsdp = fsdp
        self.total = 2 * fsdp
        self.Z = fsdp // 4
        self.x = lax.axis_index("ctx")
        self.f = lax.axis_index("fsdp")
        self.z = self.f // 4
        self.y = lax.rem(self.f // 2, 2)
        self.c = lax.rem(self.f, 2)
        self.me = self.x * fsdp + self.f
        self.cols = pl.ds(pl.multiple_of(self.x * W1, 128), WIN)
        self.give = pl.ds(pl.multiple_of(self.x * WIN, 128), W1)
        self.take = pl.ds(pl.multiple_of((1 - self.x) * WIN, 128), W1)
        self.pending = []

    def dev(self, x=None, z=None, y=None, c=None):
        x = self.x if x is None else x
        z = self.z if z is None else z
        y = self.y if y is None else y
        c = self.c if c is None else c
        return (x, z * 4 + y * 2 + c)

    def at(self, d):
        return (d // self.fsdp, lax.rem(d, self.fsdp))

    def signal(self):
        sem = pltpu.get_barrier_semaphore()

        @pl.loop(1, self.total)
        def _(k):
            d = lax.rem(self.me + k, self.total)
            pl.semaphore_signal(sem, inc=1, device_id=self.at(d), device_id_type=MESH)

    def wait(self):
        pl.semaphore_wait(pltpu.get_barrier_semaphore(), self.total - 1)

    def go(self, copy, cond=None):
        if cond is None:
            copy.start()
        else:
            pl.when(cond)(copy.start)
        self.pending.append((cond, copy))

    def finish(self):
        for cond, copy in self.pending:
            if cond is None:
                copy.wait_send()
            else:
                pl.when(cond)(copy.wait_send)
        self.pending = []


def remote(src, dst, send, recv, device):
    return pltpu.make_async_remote_copy(
        src_ref=src, dst_ref=dst, send_sem=send, recv_sem=recv, device_id=device, device_id_type=MESH
    )


class Exchange:
    def __init__(self, pc, src, dst, sems, k, one=False):
        self.pc, self.src, self.dst, self.one = pc, src, dst, one
        self.send, self.recv, self.local = sems[0].at[k], sems[1].at[k], sems[2].at[k]

    def part(self, d):
        return self.src if self.one else self.src.at[d]

    def own(self):
        return pltpu.make_async_copy(self.part(self.pc.me), self.dst.at[self.pc.me], self.local)

    def start(self):
        pc = self.pc
        self.own().start()

        @pl.loop(1, pc.total)
        def _(k):
            d = lax.rem(pc.me + k, pc.total)
            remote(self.part(d), self.dst.at[pc.me], self.send, self.recv, pc.at(d)).start()

    def whole(self):
        blocks = pl.ds(0, self.pc.total - 1)
        dst = self.dst.at[blocks]
        src = dst if self.one else self.src.at[blocks]
        return remote(src, dst, self.send, self.recv, self.pc.dev(c=1 - self.pc.c))

    def wait(self):
        self.own().wait()
        self.whole().wait_recv()

    def done(self):
        self.whole().wait_send()


class Gather:
    def __init__(self, pc, own, slots, sems):
        self.pc, self.own, self.slots = pc, own, slots
        self.zs, self.zr, self.ys, self.yr, self.xs, self.xr, self.cs, self.cr, self.ls = sems

    @staticmethod
    def sems(Z):
        T = pltpu.SemaphoreType.DMA
        n = PIECES
        return [
            T((n, 2 * Z - 2)), T((n, 2 * Z - 2)), T((n, 2 * Z - 1)), T((n,)),
            T((n,)), T((n,)), T((n, 2)), T((n, 2)), T((n,)),
        ]

    def up(self):
        return jnp.minimum(self.pc.z + 1, self.pc.Z - 1)

    def down(self):
        return jnp.maximum(self.pc.z - 1, 0)

    def mine(self, p):
        pc = self.pc
        src = self.own(p, pc.cols)
        dst = self.slots(p, pc.z, pc.y, pc.c, pc.cols)
        return pltpu.make_async_copy(src, dst, self.ls.at[p])

    def start(self, p):
        pc = self.pc
        Z = pc.Z
        src = self.own(p, pc.cols)
        dst = self.slots(p, pc.z, pc.y, pc.c, pc.cols)
        self.mine(p).start()
        pc.go(remote(src, dst, self.zs.at[p, 0], self.zr.at[p, 0], pc.dev(z=self.up())), pc.z < Z - 1)
        k = Z - 1
        pc.go(remote(src, dst, self.zs.at[p, k], self.zr.at[p, k], pc.dev(z=self.down())), pc.z > 0)
        pc.go(remote(src, dst, self.ys.at[p, 0], self.yr.at[p], pc.dev(y=1 - pc.y)))

    def hop(self, p, h):
        pc = self.pc
        Z = pc.Z
        for upward in (True, False):
            k = (0 if upward else Z - 1) + h - 1
            if upward:
                z, here, onward, to = jnp.maximum(pc.z - h, 0), pc.z >= h, pc.z < Z - 1, self.up()
            else:
                z, here, onward, to = jnp.minimum(pc.z + h, Z - 1), pc.z + h < Z, pc.z > 0, self.down()
            ref = self.slots(p, z, pc.y, pc.c, pc.cols)
            pl.when(here)(remote(ref, ref, self.zs.at[p, k], self.zr.at[p, k], pc.dev(z=to)).wait_recv)
            if h < Z - 1:
                pc.go(
                    remote(ref, ref, self.zs.at[p, k + 1], self.zr.at[p, k + 1], pc.dev(z=to)),
                    jnp.logical_and(here, onward),
                )
            pc.go(remote(ref, ref, self.ys.at[p, 1 + k], self.yr.at[p], pc.dev(y=1 - pc.y)), here)

    def row(self, p):
        pc = self.pc
        ref = self.slots(p, slice(None), 1 - pc.y, pc.c, pc.cols)
        remote(ref, ref, self.ys.at[p, 0], self.yr.at[p], pc.dev(y=1 - pc.y)).wait_recv()
        self.mine(p).wait()
        ref = self.slots(p, slice(None), slice(None), pc.c, pc.give)
        pc.go(remote(ref, ref, self.xs.at[p], self.xr.at[p], pc.dev(x=1 - pc.x)))
        ref = self.slots(p, slice(None), slice(None), pc.c, pc.cols)
        pc.go(remote(ref, ref, self.cs.at[p, 0], self.cr.at[p, 0], pc.dev(c=1 - pc.c)))

    def plane(self, p):
        pc = self.pc
        ref = self.slots(p, slice(None), slice(None), pc.c, pc.take)
        remote(ref, ref, self.xs.at[p], self.xr.at[p], pc.dev(x=1 - pc.x)).wait_recv()
        pc.go(remote(ref, ref, self.cs.at[p, 1], self.cr.at[p, 1], pc.dev(c=1 - pc.c)))

    def core(self, p):
        pc = self.pc
        for k, cols in ((0, pc.cols), (1, pc.take)):
            ref = self.slots(p, slice(None), slice(None), 1 - pc.c, cols)
            remote(ref, ref, self.cs.at[p, k], self.cr.at[p, k], pc.dev(c=1 - pc.c)).wait_recv()


class Scatter:
    def __init__(self, pc, terms, get, put, from_c, from_x, from_y, from_z, from_f, sems):
        self.pc, self.terms, self.get, self.put = pc, terms, get, put
        self.from_c, self.from_x, self.from_y, self.from_z, self.from_f = from_c, from_x, from_y, from_z, from_f
        self.cs, self.cr, self.xs, self.xr, self.ys, self.yr, self.zs, self.zr, self.fs, self.fr, self.free = sems
        self.sent = 0
        self.summed = 0
        z = pc.z
        self.inner = jnp.logical_or(z == 1, z == 2)
        self.outer = jnp.logical_not(self.inner)
        self.mate = z + 1 - 2 * lax.rem(z, 2)
        self.far_in = jnp.where(z < 2, 2, 1)
        self.far_out = jnp.where(z < 2, 3, 0)

    @staticmethod
    def sems():
        T = pltpu.SemaphoreType.DMA
        n = PIECES
        return [
            T((n,)), T((n,)), T((n,)), T((n,)), T((n,)), T((n,)), T((n, 5)), T((n, 4)), T((n,)), T((n,)),
            pltpu.SemaphoreType.REGULAR((n,)),
        ]

    @staticmethod
    def buffers(Z, rows):
        n = PIECES
        return [
            pltpu.VMEM((RING, Z, 2, rows, D), BF),
            pltpu.VMEM((n, Z, 2, rows, W1), BF),
            pltpu.VMEM((n, Z, rows, WIN), BF),
            pltpu.VMEM((n, 4, rows, WIN), BF),
            pltpu.VMEM((n, rows, WIN), BF),
        ]

    def start(self, p):
        pc = self.pc
        if self.sent >= RING:
            pl.semaphore_wait(self.free.at[self.sent], 1)
        src = self.terms(p, slice(None), slice(None), 1 - pc.c, slice(None))
        dst = self.from_c.at[self.sent % RING]
        pc.go(remote(src, dst, self.cs.at[p], self.cr.at[p], pc.dev(c=1 - pc.c)))
        self.sent += 1

    def core(self, p):
        pc = self.pc
        slot = self.summed % RING
        ref = self.from_c.at[slot]
        remote(ref, ref, self.cs.at[p], self.cr.at[p], pc.dev(c=1 - pc.c)).wait_recv()

        for z, y in ((z, y) for z in range(pc.Z) for y in range(2)):
            at = (p, z, y, pc.c, slice(None))
            self.put(*at, self.get(*at) + self.from_c[slot, z, y])

        self.summed += 1
        if self.summed + RING <= PIECES:
            pl.semaphore_signal(self.free.at[self.summed + RING - 1], inc=1, device_id=pc.dev(c=1 - pc.c), device_id_type=MESH)
        src = self.terms(p, slice(None), slice(None), pc.c, pc.take)
        pc.go(remote(src, self.from_x.at[p], self.xs.at[p], self.xr.at[p], pc.dev(x=1 - pc.x)))

    def plane(self, p):
        pc = self.pc
        ref = self.from_x.at[p]
        remote(ref, ref, self.xs.at[p], self.xr.at[p], pc.dev(x=1 - pc.x)).wait_recv()

        for z, y in ((z, y) for z in range(pc.Z) for y in range(2)):
            at = (p, z, y, pc.c, pc.give)
            self.put(*at, self.get(*at) + self.from_x[p, z, y])

        src = self.terms(p, slice(None), 1 - pc.y, pc.c, pc.cols)
        pc.go(remote(src, self.from_y.at[p], self.ys.at[p], self.yr.at[p], pc.dev(y=1 - pc.y)))

    def row(self, p):
        pc = self.pc
        ref = self.from_y.at[p]
        remote(ref, ref, self.ys.at[p], self.yr.at[p], pc.dev(y=1 - pc.y)).wait_recv()

        for z in range(pc.Z):
            at = (p, z, pc.y, pc.c, pc.cols)
            self.put(*at, self.get(*at) + self.from_y[p, z])

        for k, z in enumerate((self.mate, self.far_in, self.far_out)):
            src = self.terms(p, z, pc.y, pc.c, pc.cols)
            pc.go(
                remote(src, self.from_z.at[p, k], self.zs.at[p, k], self.zr.at[p, k], pc.dev(z=self.mate)),
                self.outer if k else None,
            )

    def middle(self, p):
        pc = self.pc
        far = ((1, self.far_in), (2, self.far_out))

        @pl.when(self.inner)
        def _():
            for k, z in far:
                ref = self.from_z.at[p, k]
                remote(ref, ref, self.zs.at[p, k], self.zr.at[p, k], pc.dev(z=self.mate)).wait_recv()
                at = (p, z, pc.y, pc.c, pc.cols)
                self.put(*at, self.get(*at) + self.from_z[p, k])

        for k, z in far:
            src = self.terms(p, z, pc.y, pc.c, pc.cols)
            pc.go(
                remote(src, self.from_z.at[p, 3], self.zs.at[p, 2 + k], self.zr.at[p, 3], pc.dev(z=z)), self.inner
            )

    def line(self, p):
        pc = self.pc
        at = (p, pc.z, pc.y, pc.c, pc.cols)
        for k in (0, 3):
            ref = self.from_z.at[p, k]
            remote(ref, ref, self.zs.at[p, k], self.zr.at[p, k], pc.dev(z=self.mate)).wait_recv()
            self.put(*at, self.get(*at) + self.from_z[p, k])
        pc.go(remote(self.terms(*at), self.from_f.at[p], self.fs.at[p], self.fr.at[p], pc.dev(x=1 - pc.x)))

    def last(self, p, out):
        pc = self.pc
        ref = self.from_f.at[p]
        remote(ref, ref, self.fs.at[p], self.fr.at[p], pc.dev(x=1 - pc.x)).wait_recv()

        def own(cols):
            return self.get(p, pc.z, pc.y, pc.c, cols).astype(F32)

        out[:, pc.give] = own(pc.give)
        theirs = pl.ds(pl.multiple_of((1 - pc.x) * W0, 128), W1)
        out[:, pc.take] = self.from_f[p, :, theirs].astype(F32)
        both = pl.ds(pl.multiple_of(pc.x * W1, 128), W0)
        shared = pl.ds(W1, W0)
        out[:, shared] = own(shared) + self.from_f[p, :, both].astype(F32)


def row_mean(v):
    return jnp.sum(v, axis=-1, keepdims=True) * (1.0 / D)


BQ, BV, BO, G1, B1, BD, G2, B2 = range(8)


def layer_kernel(
    fsdp, rows,
    order, lengths, slopes, tokens_in, grads_in, small_in, wq_in, wo_in, wg_in, wd_in,
    OUT, DX, GQ, GW, GG, GD, SMALLG,
    wa, wd, raw, outv, xs, gs, small, small_own, smallf, qkv, dist, lse, ctxt, y1, y1b, xhat, rstd, act, slope_up, zed, acc, dfb, tr,
    dxr, sgrad, gsum, from_c, from_x, from_y, from_z, from_f, *sems,
):
    pc = Place(fsdp)
    Z = pc.Z
    L = pc.total * raw.shape[1]
    gsems, ssems, esems, rsem = sems[:9], sems[9:20], sems[20:23], sems[23]
    w_pc = wa.shape[1:]

    def own(p, cols):
        if p < 3:
            return wq_in.at[:, pl.ds(pl.multiple_of(D * p + cols.start, 128), cols.size)]
        if p == 3:
            return wo_in.at[:, cols]
        if p < 12:
            i, j = (p - 4) // 2, (p - 4) % 2
            return wg_in.at[:, pl.ds(pl.multiple_of(FF * j + D * i + cols.start, 128), cols.size)]
        return wd_in.at[pl.ds(rows * (p - 12), rows), cols]

    def slots(p, z, y, c, cols):
        if p < 12:
            return wa.at[p, z, y, c, :, cols]
        return wd.at[z, y, c, p - 12, :, cols]

    def get(p, z, y, c, cols):
        if p < 12:
            return wa[p, z, y, c, :, cols]
        return wd[z, y, c, p - 12, :, cols]

    def put(p, z, y, c, cols, value):
        if p < 12:
            wa[p, z, y, c, :, cols] = value
        else:
            wd[z, y, c, p - 12, :, cols] = value

    def out_of(p):
        if p >= 12:
            return GD.at[pl.ds(rows * (p - 12), rows)]
        if p == 3:
            return GW
        if p < 3:
            return GQ.at[:, pl.ds(D * p, D)]
        i, j = (p - 4) // 2, (p - 4) % 2
        return GG.at[:, pl.ds(FF * j + D * i, D)]

    def w_cols(p, cols):
        return wa[p, :, :, :, :, cols].reshape(D, cols.size)

    def w_all(p):
        return wa[p].reshape(D, D)

    g = Gather(pc, own, slots, gsems)
    sc = Scatter(pc, slots, get, put, from_c, from_x, from_y, from_z, from_f, ssems)
    ex_x = Exchange(pc, outv, xs, esems, 0)
    ex_g = Exchange(pc, grads_in, gs, esems, 1)
    ex_o = Exchange(pc, outv, OUT, esems, 3)
    ex_d = Exchange(pc, raw, dxr, esems, 4)
    ex_s = Exchange(pc, sgrad, gsum, esems, 5, one=True)
    len_s = lengths[pc.x, order[pc.x, pc.f]]

    def tokens(r):
        n = r.size // 16
        return xs[pl.ds(r.start // 16, n)].reshape(r.size, D)

    def deal():
        @pl.loop(0, pc.total)
        def _(d):
            m = d // fsdp
            outv[d] = raw[m * fsdp + order[m, lax.rem(d, fsdp)]]

    def prepare():
        k = lax.broadcasted_iota(jnp.int32, (L, L), 0)
        q = lax.broadcasted_iota(jnp.int32, (L, L), 1)
        dist[...] = jnp.where(k < len_s, jnp.abs(k - q).astype(F32), -NEGATIVE)

    def place_small():
        k = lax.broadcasted_iota(jnp.int32, (rows, D), 0)
        col = lax.broadcasted_iota(jnp.int32, (rows, D), 1)
        at = jnp.where(col - pc.f * rows == k, 1.0, 0.0).astype(BF)
        small_own[...] = mm(small_in[...], at).astype(BF)

    def sum_small():
        def add(i, v):
            return v + small[i].astype(F32)

        smallf[...] = lax.fori_loop(1, fsdp, add, small[0].astype(F32))

    def project(p):
        @pl.loop(0, D // 256)
        def _(t):
            cols = block(t, 256)
            r = mm(xs[...].reshape(L, D), w_cols(p, cols))
            if p != 1:
                r = r + smallf[pl.ds(BQ if p == 0 else BV, 1), cols]
            qkv[p, :, cols] = r.astype(BF)

    def attend(j):
        cols = block(j, 128)
        lane = lax.broadcasted_iota(jnp.int32, (L, 128), 1)
        q2, k2 = qkv[0, :, cols], qkv[1, :, cols]
        vt = qkv[2, :, cols].T
        for q in range(L // 256):
            qr = pl.ds(256 * q, 256)
            parts = []
            for s in range(2):
                qm = jnp.where((lane < 64) if s == 0 else (lane >= 64), q2, jnp.zeros_like(q2))
                st = mm_nt(k2, qm[256 * q : 256 * q + 256])
                st = st * (0.125 * LOG2E) - dist[:, qr] * slopes[2 * j + s]
                top = jnp.max(st, axis=0, keepdims=True)
                e = jnp.exp2(st - top)
                total = jnp.sum(e, axis=0, keepdims=True)
                lse[2 * j + s, :, qr] = top + jnp.log2(total)
                pr = (e * (1.0 / total)).astype(BF)
                parts.append(mm(vt[64 * s : 64 * s + 64], pr))
            ctxt[qr, cols] = jnp.concatenate(parts, axis=0).T.astype(BF)

    def first_norm():
        @pl.loop(0, D // 256)
        def _(t):
            cols = block(t, 256)
            acc[:, cols] = mm(ctxt[...], w_cols(3, cols)) + smallf[pl.ds(BO, 1), cols]

        @pl.loop(0, L // 64)
        def _(i):
            r = block(i, 64)
            h = acc[r, :] + tokens(r).astype(F32)
            centre = h - row_mean(h)
            rs = lax.rsqrt(row_mean(centre * centre) + EPSILON)
            xh = centre * rs
            xhat[r, :] = xh
            rstd[r, :] = jnp.broadcast_to(rs, (64, 128))
            yy = xh * smallf[pl.ds(G1, 1), :] + smallf[pl.ds(B1, 1), :]
            y1[r, :] = yy
            y1b[r, :] = yy.astype(BF)

    def gated(i, s):
        wc = block(s, 256)
        cols = block(i * 3 + s, 256)
        a = mm(y1b[...], w_cols(4 + 2 * i, wc))
        u = mm(y1b[...], w_cols(5 + 2 * i, wc))
        cdf = 0.5 + 0.5 * lax.erf(a * math.sqrt(0.5))
        pdf = jnp.exp2(a * a * (-0.5 * LOG2E)) * (1.0 / math.sqrt(2.0 * math.pi))
        gelu = a * cdf
        zed[:, cols] = (gelu * u).astype(BF)
        act[:, cols] = gelu.astype(BF)
        slope_up[:, cols] = (u * (cdf + a * pdf)).astype(BF)

    def second_norm():
        @pl.loop(0, D // 256)
        def _(t):
            cols = block(t, 256)
            w = wd[:, :, :, :, :, cols].reshape(FF, 256)
            acc[:, cols] = mm(zed[...], w) + smallf[pl.ds(BD, 1), cols]

        def step(i, sums):
            r = block(i, 64)
            h = acc[r, :] + y1[r, :]
            centre = h - row_mean(h)
            rs = lax.rsqrt(row_mean(centre * centre) + EPSILON)
            xh = centre * rs
            gain = smallf[pl.ds(G2, 1), :]
            valid = (lax.broadcasted_iota(jnp.int32, (64, D), 0) + i * 64) < len_s
            res = jnp.where(valid, xh * gain + smallf[pl.ds(B2, 1), :], 0.0).astype(BF)
            outv[pl.ds(i * 4, 4)] = res.reshape(4, 16, D)
            up = jnp.where(valid, gs[pl.ds(i * 4, 4)].reshape(64, D).astype(F32), 0.0)
            dx = up * gain
            dh = rs * (dx - row_mean(dx) - xh * row_mean(dx * xh))
            low = dh.astype(BF)
            acc[r, :] = dh
            dfb[r, :] = low
            sg, sb, sd = sums
            return (
                sg + jnp.sum(up * xh, axis=0, keepdims=True),
                sb + jnp.sum(up, axis=0, keepdims=True),
                sd + jnp.sum(low.astype(F32), axis=0, keepdims=True),
            )

        zero = jnp.zeros((1, D), F32)
        sg, sb, sd = lax.fori_loop(0, L // 64, step, (zero, zero, zero))
        sgrad[pl.ds(G2, 1), :] = sg
        sgrad[pl.ds(B2, 1), :] = sb
        sgrad[pl.ds(BD, 1), :] = sd

    def ff_back(i):
        cols = block(i, D)
        part = pl.ds(i * Z // 4, Z // 4)
        dz = mm_nt(dfb[...], wd[part].reshape(D, D))
        dgate = (dz * slope_up[:, cols].astype(F32)).astype(BF)
        dup = (dz * act[:, cols].astype(F32)).astype(BF)
        acc[...] += mm_nt(dgate, w_all(4 + 2 * i)) + mm_nt(dup, w_all(5 + 2 * i))
        wa[4 + 2 * i] = mm(tr[...], dgate).astype(BF).reshape(w_pc)
        wa[5 + 2 * i] = mm(tr[...], dup).astype(BF).reshape(w_pc)
        wd[part] = mm_tn(zed[:, cols], dfb[...]).astype(BF).reshape((Z // 4,) + wd.shape[1:])

    def first_norm_back():
        def step(i, sums):
            r = block(i, 64)
            up = acc[r, :]
            xh = xhat[r, :]
            dx = up * smallf[pl.ds(G1, 1), :]
            dh = rstd[r, :][:, :1] * (dx - row_mean(dx) - xh * row_mean(dx * xh))
            low = dh.astype(BF)
            xhat[r, :] = dh
            dfb[r, :] = low
            sg, sb, sd = sums
            return (
                sg + jnp.sum(up * xh, axis=0, keepdims=True),
                sb + jnp.sum(up, axis=0, keepdims=True),
                sd + jnp.sum(low.astype(F32), axis=0, keepdims=True),
            )

        zero = jnp.zeros((1, D), F32)
        sg, sb, sd = lax.fori_loop(0, L // 64, step, (zero, zero, zero))
        sgrad[pl.ds(G1, 1), :] = sg
        sgrad[pl.ds(B1, 1), :] = sb
        sgrad[pl.ds(BO, 1), :] = sd

    def out_back():
        y1b[...] = mm_nt(dfb[...], w_all(3)).astype(BF)
        wa[3] = mm_tn(ctxt[...], dfb[...]).astype(BF).reshape(w_pc)

    def dqkv(p):
        return act.at[:, pl.ds(D * p, D)]

    def attend_back(j):
        cols = block(j, 128)
        lane = lax.broadcasted_iota(jnp.int32, (L, 128), 1)
        q2, k2, v2 = (qkv[i, :, cols] for i in range(3))
        do2 = y1b[:, cols]
        kt = k2.T
        dv = dk = None
        for q in range(L // 256):
            qr = pl.ds(256 * q, 256)
            qs = slice(256 * q, 256 * q + 256)
            parts = []
            for s in range(2):
                half = (lane < 64) if s == 0 else (lane >= 64)
                qm = jnp.where(half, q2, jnp.zeros_like(q2))[qs]
                dm = jnp.where(half, do2, jnp.zeros_like(do2))[qs]
                st = mm_nt(k2, qm) * (0.125 * LOG2E) - dist[:, qr] * slopes[2 * j + s]
                pr = jnp.exp2(st - lse[2 * j + s, :, qr])
                dp = mm_nt(v2, dm)
                ds = (pr * (dp - jnp.sum(pr * dp, axis=0, keepdims=True))).astype(BF)
                a, b = mm(pr.astype(BF), dm), mm(ds, qm)
                dv = a if dv is None else dv + a
                dk = b if dk is None else dk + b
                parts.append(mm(kt[64 * s : 64 * s + 64], ds))
            dqkv(0)[qr, cols] = (jnp.concatenate(parts, axis=0).T * 0.125).astype(BF)
        dqkv(1)[:, cols] = (dk * 0.125).astype(BF)
        dqkv(2)[:, cols] = dv.astype(BF)

    def weights_back(p):
        x = xs[...].reshape(L, D)
        d = dqkv(p)
        wa[p] = mm_tn(x, d[...]).astype(BF).reshape(w_pc)
        if p != 1:
            r = BQ if p == 0 else BV
            sgrad[pl.ds(r, 1), :] = jnp.sum(d[...].astype(F32), axis=0, keepdims=True)

    def tokens_back():
        @pl.loop(0, L // 128)
        def _(i):
            r = block(i, 128)
            v = xhat[r, :]
            for p in range(3):
                v = v + mm_nt(dqkv(p)[r, :], w_all(p))
            raw[pl.ds(i * 8, 8)] = v.astype(BF).reshape(8, 16, D)

    def undeal():
        @pl.loop(0, pc.total)
        def _(k):
            m, n = k // fsdp, lax.rem(k, fsdp)

            def find(f, at):
                return jnp.where(order[m, f] == n, f, at)

            DX[k] = dxr[m * fsdp + lax.fori_loop(0, fsdp, find, 0)]

    take_raw = pltpu.make_async_copy(tokens_in, raw, rsem)
    take_raw.start()
    pc.signal()
    place_small()
    prepare()
    take_raw.wait()
    deal()
    pc.wait()

    me_small = small.at[pc.f]
    keep_small = pltpu.make_async_copy(small_own, me_small, esems[2].at[2])
    keep_small.start()

    @pl.loop(1, fsdp)
    def _(k):
        f = lax.rem(pc.f + k, fsdp)
        remote(small_own, me_small, esems[0].at[2], esems[1].at[2], (pc.x, f)).start()

    small_all = remote(
        small.at[pl.ds(0, fsdp - 1)], small.at[pl.ds(0, fsdp - 1)], esems[0].at[2], esems[1].at[2],
        pc.dev(c=1 - pc.c),
    )

    def after_core(p):
        if p == 2:
            ex_x.wait()
            small_all.wait_recv()
            keep_small.wait()
            sum_small()
            for i in range(3):
                project(i)
        if 2 <= p <= 4:
            pl.loop(2 * (p - 2), 2 * (p - 2) + 2)(attend)
        if p == 4:
            first_norm()
        if 5 <= p < 12 and p % 2 == 1:
            for s in range(3):
                gated((p - 5) // 2, s)

    for t in range(PIECES + 8):
        if t < PIECES:
            g.start(t)
        if t == 0:
            ex_x.start()
        if t == 6:
            ex_g.start()
        for h in range(1, Z):
            if 0 <= t - h < PIECES:
                g.hop(t - h, h)
        if 0 <= t - 4 < PIECES:
            g.row(t - 4)
        if 0 <= t - 6 < PIECES:
            g.plane(t - 6)
        if 0 <= t - 8 < PIECES:
            g.core(t - 8)
            after_core(t - 8)
    ex_g.wait()
    ex_x.done()
    second_norm()
    ex_o.start()
    tr[...] = y1b[...].T
    pc.finish()

    turns = list(range(4, 12)) + [12, 13, 14, 15, 3, 0, 1, 2]
    stages = (("core", 1), ("plane", 3), ("row", 5), ("middle", 6), ("line", 8), ("last", 10))
    for t in range(PIECES + 10):
        if t < 8 and t % 2 == 0:
            ff_back(t // 2)
        if t == 8:
            first_norm_back()
            out_back()
        if 9 <= t < 12:
            pl.loop(2 * (t - 9), 2 * (t - 9) + 2)(attend_back)
        if t == 12:
            tokens_back()
            ex_d.start()
            for p in range(3):
                weights_back(p)
            ex_s.start()
        if t < PIECES:
            sc.start(turns[t])
        for name, off in stages:
            if 0 <= t - off < PIECES:
                p = turns[t - off]
                if name == "last":
                    sc.last(p, out_of(p))
                else:
                    getattr(sc, name)(p)
    ex_s.wait()

    def add(i, v):
        return v + gsum[i]

    total = lax.fori_loop(1, pc.total, add, gsum[0])
    SMALLG[...] = pltpu.roll(total, D - pc.f * rows, axis=1)[:, :rows]
    ex_d.wait()
    undeal()
    ex_o.wait()
    for e in (ex_g, ex_o, ex_d, ex_s):
        e.done()
    small_all.wait_send()
    pc.finish()


def per_device(
    tokens_in, out_grad, seq_lengths, order, w_qkv, bias_q, bias_v, w_out, bias_out, ln1_gain, ln1_bias, w_gate_up,
    w_down, bias_down, ln2_gain, ln2_bias,
):
    fsdp = lax.axis_size("fsdp")
    total = 2 * fsdp
    rows = w_out.shape[0]
    here = tokens_in.shape[2]
    L = here * total
    Z = fsdp // 4
    zero = jnp.zeros((rows,), BF)
    small = jnp.stack([bias_q, bias_v, bias_out, ln1_gain, ln1_bias, bias_down, ln2_gain, ln2_bias] + [zero] * 8)
    slopes = jnp.array(slope_list(HEADS), F32) * LOG2E
    hbm = pl.BlockSpec(memory_space=pl.ANY)
    smem = pl.BlockSpec(memory_space=pltpu.SMEM)
    vmem = pl.BlockSpec(memory_space=pltpu.VMEM)
    S = jax.ShapeDtypeStruct
    T = pltpu.SemaphoreType.DMA
    V = pltpu.VMEM
    rows_of = (total, here, D)
    output, input_grad, gq, gw, gg, gd, mine = pl.pallas_call(
        functools.partial(layer_kernel, fsdp, rows),
        out_shape=[
            S(rows_of, BF), S(rows_of, BF), S((rows, 3 * D), F32), S((rows, D), F32), S((rows, 2 * FF), F32),
            S((4 * rows, D), F32), S((8, rows), F32),
        ],
        in_specs=[smem] * 3 + [hbm] * 2 + [vmem] + [hbm] * 4,
        out_specs=[hbm] + [vmem] * 6,
        scratch_shapes=[
            V((12, Z, 2, 2, rows, D), BF), V((Z, 2, 2, 4, rows, D), BF), V(rows_of, BF), V(rows_of, BF),
            V(rows_of, BF), V(rows_of, BF), V((fsdp, 16, D), BF), V((16, D), BF), V((16, D), F32), V((3, L, D), BF), V((L, L), F32),
            V((HEADS, 1, L), F32), V((L, D), BF), V((L, D), F32), V((L, D), BF), V((L, D), F32), V((L, 128), F32),
            V((L, FF), BF), V((L, FF), BF), V((L, FF), BF), V((L, D), F32), V((L, D), BF), V((D, L), BF),
            V(rows_of, BF), V((8, D), F32), V((total, 8, D), F32),
            *Scatter.buffers(Z, rows), *Gather.sems(Z), *Scatter.sems(), T((6,)), T((6,)), T((6,)), T,
        ],
        compiler_params=pltpu.CompilerParams(collective_id=0, has_side_effects=True, vmem_limit_bytes=VMEM_LIMIT),
        name="layer",
    )(order, seq_lengths, slopes, tokens_in.reshape(rows_of), out_grad.reshape(rows_of), small, w_qkv, w_out, w_gate_up, w_down)
    return (
        output.reshape(tokens_in.shape), input_grad.reshape(tokens_in.shape), gq, mine[BQ], mine[BV], gw, mine[BO],
        mine[G1], mine[B1], gg, gd, mine[BD], mine[G2], mine[B2],
    )


def solution(mesh):
    fsdp = mesh.shape["fsdp"]
    rows = D // fsdp
    kernels = mesh.shape["ctx"] == M and fsdp == 16 and rows % 16 == 0
    return jax.shard_map(
        per_device if kernels else per_device_plain,
        mesh=mesh,
        in_specs=(
            P(None, None, ("ctx", "fsdp"), None),
            P(None, None, ("ctx", "fsdp"), None),
            P(),
            P(),
            P("fsdp", None),
            P("fsdp"),
            P("fsdp"),
            P("fsdp", None),
            P("fsdp"),
            P("fsdp"),
            P("fsdp"),
            P("fsdp", None),
            P("fsdp", None),
            P("fsdp"),
            P("fsdp"),
            P("fsdp"),
        ),
        out_specs=(
            P(None, None, ("ctx", "fsdp"), None),
            P(None, None, ("ctx", "fsdp"), None),
            P("fsdp", None),
            P("fsdp"),
            P("fsdp"),
            P("fsdp", None),
            P("fsdp"),
            P("fsdp"),
            P("fsdp"),
            P("fsdp", None),
            P("fsdp", None),
            P("fsdp"),
            P("fsdp"),
            P("fsdp"),
        ),
        check_vma=False,
    )
```

```python
import functools
import math

import jax
import jax.numpy as jnp
from jax import lax
from jax.experimental import pallas as pl
from jax.experimental.pallas import tpu as pltpu
from jax.sharding import PartitionSpec as P

D = 768
HEADS = 12
HEAD_DIM = 64
FF = 3072
M = 2
EPSILON = 1e-12
NEGATIVE = -1e30
MESH = pl.DeviceIdType.MESH
BF = jnp.bfloat16
F32 = jnp.float32
LOG2E = math.log2(math.e)
VMEM_LIMIT = 62 << 20


def slope_list(head_count):

    def powers(number):
        anchor = 2.0 ** (-(2.0 ** (-(math.log2(number) - 3))))
        return [anchor ** (power_index + 1) for power_index in range(number)]

    closest = 2 ** int(math.floor(math.log2(head_count)))
    return powers(closest) + powers(2 * closest)[0::2][: head_count - closest]


def layer_norm(inputs, gain_row, offset_row):
    centre = inputs - jnp.mean(inputs, axis=-1, keepdims=True)
    spread = jnp.mean(centre * centre, axis=-1, keepdims=True)
    return centre * lax.rsqrt(spread + EPSILON) * gain_row + offset_row


def gated_unit(gate_up):
    return jax.nn.gelu(gate_up[:, :FF], approximate=False) * gate_up[:, FF:]


def rows_product(former, latter):
    return lax.dot_general(
        former, latter, (((0,), (0,)), ((), ())), preferred_element_type=jnp.float32
    )


def by_transpose(former, latter):
    return lax.dot_general(
        former, latter, (((1,), (1,)), ((), ())), preferred_element_type=jnp.float32
    )


def plain_product(former, latter):
    return jnp.dot(former, latter, preferred_element_type=jnp.float32)


def masked_scores(heads_q, heads_k, position, key_place, length, slopes):
    raw_scores = (
        jnp.einsum("qhd,khd->hqk", heads_q, heads_k, preferred_element_type=jnp.float32) * 0.125
    )
    distance = jnp.abs(position[:, None] - key_place[None, :]).astype(jnp.float32)
    raw_scores = raw_scores - slopes[:, None, None] * distance[None]
    return jnp.where((key_place < length)[None, None, :], raw_scores, NEGATIVE)


def fetch_weights(shards):
    return (
        lax.all_gather(shards[0], "fsdp", axis=0, tiled=True),
        lax.all_gather(shards[1], "fsdp", axis=0, tiled=True),
        lax.all_gather(shards[2], "fsdp", axis=0, tiled=True),
        lax.all_gather(shards[3], "fsdp", axis=0, tiled=True),
        lax.all_gather(shards[4], "fsdp", axis=0, tiled=True),
        lax.all_gather(shards[5], "fsdp", axis=0, tiled=True),
        lax.all_gather(shards[6], "fsdp", axis=0, tiled=True),
        lax.all_gather(shards[7], "fsdp", axis=0, tiled=True),
        lax.all_gather(shards[8], "fsdp", axis=0, tiled=True),
        lax.all_gather(shards[9], "fsdp", axis=0, tiled=True),
        lax.all_gather(shards[10], "fsdp", axis=0, tiled=True),
        lax.all_gather(shards[11], "fsdp", axis=0, tiled=True),
    )


def reduce_grads(grad_terms):
    shard_sums = (
        lax.psum_scatter(grad_terms[0], "fsdp", scatter_dimension=0, tiled=True),
        lax.psum_scatter(grad_terms[1], "fsdp", scatter_dimension=0, tiled=True),
        lax.psum_scatter(grad_terms[2], "fsdp", scatter_dimension=0, tiled=True),
        lax.psum_scatter(grad_terms[3], "fsdp", scatter_dimension=0, tiled=True),
        lax.psum_scatter(grad_terms[4], "fsdp", scatter_dimension=0, tiled=True),
        lax.psum_scatter(grad_terms[5], "fsdp", scatter_dimension=0, tiled=True),
        lax.psum_scatter(grad_terms[6], "fsdp", scatter_dimension=0, tiled=True),
        lax.psum_scatter(grad_terms[7], "fsdp", scatter_dimension=0, tiled=True),
        lax.psum_scatter(grad_terms[8], "fsdp", scatter_dimension=0, tiled=True),
        lax.psum_scatter(grad_terms[9], "fsdp", scatter_dimension=0, tiled=True),
        lax.psum_scatter(grad_terms[10], "fsdp", scatter_dimension=0, tiled=True),
        lax.psum_scatter(grad_terms[11], "fsdp", scatter_dimension=0, tiled=True),
    )
    return (
        lax.psum(shard_sums[0].astype(jnp.bfloat16), "ctx").astype(jnp.float32),
        lax.psum(shard_sums[1].astype(jnp.bfloat16), "ctx").astype(jnp.float32),
        lax.psum(shard_sums[2].astype(jnp.bfloat16), "ctx").astype(jnp.float32),
        lax.psum(shard_sums[3].astype(jnp.bfloat16), "ctx").astype(jnp.float32),
        lax.psum(shard_sums[4].astype(jnp.bfloat16), "ctx").astype(jnp.float32),
        lax.psum(shard_sums[5].astype(jnp.bfloat16), "ctx").astype(jnp.float32),
        lax.psum(shard_sums[6].astype(jnp.bfloat16), "ctx").astype(jnp.float32),
        lax.psum(shard_sums[7].astype(jnp.bfloat16), "ctx").astype(jnp.float32),
        lax.psum(shard_sums[8].astype(jnp.bfloat16), "ctx").astype(jnp.float32),
        lax.psum(shard_sums[9].astype(jnp.bfloat16), "ctx").astype(jnp.float32),
        lax.psum(shard_sums[10].astype(jnp.bfloat16), "ctx").astype(jnp.float32),
        lax.psum(shard_sums[11].astype(jnp.bfloat16), "ctx").astype(jnp.float32),
    )


def per_device_plain(
    tokens_in,
    out_grad,
    seq_lengths,
    order,
    w_qkv,
    bias_q,
    bias_v,
    w_out,
    bias_out,
    ln1_gain,
    ln1_bias,
    w_gate_up,
    w_down,
    bias_down,
    ln2_gain,
    ln2_bias,
):
    shards = (
        w_qkv,
        bias_q,
        bias_v,
        w_out,
        bias_out,
        ln1_gain,
        ln1_bias,
        w_gate_up,
        w_down,
        bias_down,
        ln2_gain,
        ln2_bias,
    )
    group_index = lax.axis_index("fsdp")
    ctx_index = lax.axis_index("ctx")
    dealt_tokens = jnp.take_along_axis(tokens_in, order[:, :, None, None], axis=1)
    tokens_grp, grads_grp = (
        lax.all_to_all(dealt_tokens, "fsdp", split_axis=1, concat_axis=2, tiled=True),
        lax.all_to_all(out_grad, "fsdp", split_axis=1, concat_axis=2, tiled=True),
    )
    dealt_lengths = jnp.take_along_axis(seq_lengths, order, axis=1)
    local_rows = tokens_grp.shape[2]
    key_place = jnp.arange(local_rows * lax.axis_size("ctx"))
    position = ctx_index * local_rows + jnp.arange(local_rows)
    slopes = jnp.array(slope_list(HEADS), jnp.float32)
    output_list = []
    input_list = []
    running = None
    for micro_batch in range(M):
        weights = fetch_weights(shards)
        (
            full_qkv,
            full_bias_q,
            full_bias_v,
            full_out,
            full_bias_out,
            full_ln1_gain,
            full_ln1_bias,
            full_gate_up,
            full_down,
            full_bias_down,
            full_ln2_gain,
            full_ln2_bias,
        ) = weights
        tokens = tokens_grp[micro_batch, 0]
        cotangent = grads_grp[micro_batch, 0]
        length = lax.dynamic_index_in_dim(
            dealt_lengths[micro_batch], group_index, 0, keepdims=False
        )
        valid_rows = position < length
        projected = plain_product(tokens, full_qkv)
        queries = (projected[:, :D] + full_bias_q.astype(jnp.float32)).astype(jnp.bfloat16)
        key_rows = projected[:, D : 2 * D].astype(jnp.bfloat16)
        values = (projected[:, 2 * D :] + full_bias_v.astype(jnp.float32)).astype(jnp.bfloat16)
        keys_all, values_all = (
            lax.all_gather(key_rows, "ctx", axis=0, tiled=True),
            lax.all_gather(values, "ctx", axis=0, tiled=True),
        )
        heads_q = queries.reshape(local_rows, HEADS, HEAD_DIM)
        heads_k = keys_all.reshape(-1, HEADS, HEAD_DIM)
        heads_v = values_all.reshape(-1, HEADS, HEAD_DIM)
        scores = masked_scores(heads_q, heads_k, position, key_place, length, slopes)
        row_max = jnp.max(scores, axis=-1, keepdims=True)
        exp_terms = jnp.exp(scores - row_max)
        row_total = jnp.sum(exp_terms, axis=-1, keepdims=True)
        log_total = row_max + jnp.log(row_total)
        attn_probs = (exp_terms / row_total).astype(jnp.bfloat16)
        context = (
            jnp.einsum("hqk,khd->qhd", attn_probs, heads_v, preferred_element_type=jnp.float32)
            .reshape(local_rows, D)
            .astype(jnp.bfloat16)
        )
        attn_out = plain_product(context, full_out) + full_bias_out.astype(jnp.float32)
        first_sum = tokens.astype(jnp.float32) + attn_out
        normed_one, norm_one_pull = jax.vjp(
            layer_norm,
            first_sum,
            full_ln1_gain.astype(jnp.float32),
            full_ln1_bias.astype(jnp.float32),
        )
        normed_low = normed_one.astype(jnp.bfloat16)
        gate_up = plain_product(normed_low, full_gate_up)
        hidden, gated_pull = jax.vjp(gated_unit, gate_up)
        hidden_low = hidden.astype(jnp.bfloat16)
        branch = plain_product(hidden_low, full_down) + full_bias_down.astype(jnp.float32)
        result, norm_two_pull = jax.vjp(
            layer_norm,
            normed_one + branch,
            full_ln2_gain.astype(jnp.float32),
            full_ln2_bias.astype(jnp.float32),
        )
        output_list.append(jnp.where(valid_rows[:, None], result, 0.0).astype(jnp.bfloat16))
        grad_result = jnp.where(valid_rows[:, None], cotangent.astype(jnp.float32), 0.0)
        grad_second, grad_ln2_gain, grad_ln2_bias = norm_two_pull(grad_result)
        grad_branch = grad_second.astype(jnp.bfloat16)
        grad_bias_down = jnp.sum(grad_branch.astype(jnp.float32), axis=0)
        grad_w_down = rows_product(hidden_low, grad_branch)
        grad_hidden = by_transpose(grad_branch, full_down)
        (grad_gate_up,) = gated_pull(grad_hidden)
        grad_gate_low = grad_gate_up.astype(jnp.bfloat16)
        grad_w_gate_up = rows_product(normed_low, grad_gate_low)
        grad_normed = grad_second + by_transpose(grad_gate_low, full_gate_up)
        grad_first, grad_ln1_gain, grad_ln1_bias = norm_one_pull(grad_normed)
        grad_attn = grad_first.astype(jnp.bfloat16)
        grad_bias_out = jnp.sum(grad_attn.astype(jnp.float32), axis=0)
        grad_w_out = rows_product(context, grad_attn)
        grad_context = (
            by_transpose(grad_attn, full_out)
            .astype(jnp.bfloat16)
            .reshape(local_rows, HEADS, HEAD_DIM)
        )
        scores = masked_scores(heads_q, heads_k, position, key_place, length, slopes)
        attn_exact = jnp.exp(scores - log_total)
        grad_values_term = jnp.einsum(
            "hqk,qhd->khd",
            attn_exact.astype(jnp.bfloat16),
            grad_context,
            preferred_element_type=jnp.float32,
        )
        grad_probs = jnp.einsum(
            "qhd,khd->hqk", grad_context, heads_v, preferred_element_type=jnp.float32
        )
        grad_scores = (
            attn_exact * (grad_probs - jnp.sum(attn_exact * grad_probs, axis=-1, keepdims=True))
        ).astype(jnp.bfloat16)
        grad_queries = (
            jnp.einsum("hqk,khd->qhd", grad_scores, heads_k, preferred_element_type=jnp.float32)
            * 0.125
        ).reshape(local_rows, D)
        grad_keys_term = (
            jnp.einsum("hqk,qhd->khd", grad_scores, heads_q, preferred_element_type=jnp.float32)
            * 0.125
        )
        grad_keys, grad_values = (
            lax.psum_scatter(
                grad_keys_term.reshape(-1, D).astype(jnp.bfloat16),
                "ctx",
                scatter_dimension=0,
                tiled=True,
            ).astype(jnp.float32),
            lax.psum_scatter(
                grad_values_term.reshape(-1, D).astype(jnp.bfloat16),
                "ctx",
                scatter_dimension=0,
                tiled=True,
            ).astype(jnp.float32),
        )
        grad_qkv = jnp.concatenate(
            [
                grad_queries.astype(jnp.bfloat16),
                grad_keys.astype(jnp.bfloat16),
                grad_values.astype(jnp.bfloat16),
            ],
            axis=1,
        )
        grad_w_qkv = rows_product(tokens, grad_qkv)
        grad_bias_q = jnp.sum(grad_qkv[:, :D].astype(jnp.float32), axis=0)
        grad_bias_v = jnp.sum(grad_qkv[:, 2 * D :].astype(jnp.float32), axis=0)
        grad_tokens = grad_first + by_transpose(grad_qkv, full_qkv)
        input_list.append(grad_tokens.astype(jnp.bfloat16))
        grad_terms = (
            grad_w_qkv,
            grad_bias_q,
            grad_bias_v,
            grad_w_out,
            grad_bias_out,
            grad_ln1_gain,
            grad_ln1_bias,
            grad_w_gate_up,
            grad_w_down,
            grad_bias_down,
            grad_ln2_gain,
            grad_ln2_bias,
        )
        reduced = reduce_grads(grad_terms)
        if micro_batch == 0:
            running = reduced
        else:
            running = tuple((left_sum + right_sum for left_sum, right_sum in zip(running, reduced)))
    output_stack = jnp.stack(output_list, axis=0)[:, None]
    input_stack = jnp.stack(input_list, axis=0)[:, None]
    output, dealt_grads = (
        lax.all_to_all(output_stack, "fsdp", split_axis=2, concat_axis=1, tiled=True),
        lax.all_to_all(input_stack, "fsdp", split_axis=2, concat_axis=1, tiled=True),
    )
    inverse = jnp.argsort(order, axis=1)
    input_grad = jnp.take_along_axis(dealt_grads, inverse[:, :, None, None], axis=1)
    return (
        output,
        input_grad,
        running[0],
        running[1],
        running[2],
        running[3],
        running[4],
        running[5],
        running[6],
        running[7],
        running[8],
        running[9],
        running[10],
        running[11],
    )


PIECES = 16
RING = 4


def whole(p, w=256):
    return [(p, 0, D, w)]


def halves(p, w=128):
    return [(p, 384 * i, 384, w) for i in range(2)]


GATHER_UNITS = sum([whole(p) for p in range(PIECES)], [])
SCATTER_UNITS = sum([whole(p) for p in [*range(4, 16), 3, 0, 1, 2]], [])
STAGES = ()
AHEAD = 0
ROW_AT = 4
PLANE_AT = 6
CORE_AT = 8
X_AT = (0, 4)
G_AT = (6, 8)
O_AT = (0, 8)
D_AT = (12, 4)


def mm(a, b):
    return jnp.dot(a, b, preferred_element_type=F32)


def mm_nt(a, b):
    return lax.dot_general(a, b, (((1,), (1,)), ((), ())), preferred_element_type=F32)


def mm_tn(a, b):
    return lax.dot_general(a, b, (((0,), (0,)), ((), ())), preferred_element_type=F32)


def block(i, size):
    if isinstance(i, int):
        return pl.ds(i * size, size)
    return pl.ds(pl.multiple_of(i * size, size), size)


class Place:
    def __init__(self, fsdp):
        self.fsdp = fsdp
        self.total = 2 * fsdp
        self.Z = fsdp // 4
        self.x = lax.axis_index("ctx")
        self.f = lax.axis_index("fsdp")
        self.z = self.f // 4
        self.y = lax.rem(self.f // 2, 2)
        self.c = lax.rem(self.f, 2)
        self.me = self.x * fsdp + self.f
        self.pending = []

    def dev(self, x=None, z=None, y=None, c=None):
        x = self.x if x is None else x
        z = self.z if z is None else z
        y = self.y if y is None else y
        c = self.c if c is None else c
        return (x, z * 4 + y * 2 + c)

    def cols(self, unit):
        p, lo, n, w = unit
        return pl.ds(pl.multiple_of(lo + self.x * w, 128), n - w)

    def give(self, unit):
        p, lo, n, w = unit
        return pl.ds(pl.multiple_of(lo + self.x * (n - w), 128), w)

    def take(self, unit):
        p, lo, n, w = unit
        return pl.ds(pl.multiple_of(lo + (1 - self.x) * (n - w), 128), w)

    def at(self, d):
        return (d // self.fsdp, lax.rem(d, self.fsdp))

    def signal(self):
        sem = pltpu.get_barrier_semaphore()

        @pl.loop(1, self.total)
        def _(k):
            d = lax.rem(self.me + k, self.total)
            pl.semaphore_signal(sem, inc=1, device_id=self.at(d), device_id_type=MESH)

    def wait(self):
        pl.semaphore_wait(pltpu.get_barrier_semaphore(), self.total - 1)

    def go(self, copy, cond=None):
        if cond is None:
            copy.start()
        else:
            pl.when(cond)(copy.start)
        self.pending.append((cond, copy))

    def finish(self):
        for cond, copy in self.pending:
            if cond is None:
                copy.wait_send()
            else:
                pl.when(cond)(copy.wait_send)
        self.pending = []


def remote(src, dst, send, recv, device):
    return pltpu.make_async_remote_copy(
        src_ref=src, dst_ref=dst, send_sem=send, recv_sem=recv, device_id=device, device_id_type=MESH
    )


class Exchange:
    def __init__(self, pc, src, dst, sems, k):
        self.pc, self.src, self.dst = pc, src, dst
        self.send, self.recv, self.local = sems[0].at[k], sems[1].at[k], sems[2].at[k]

    def own(self):
        return pltpu.make_async_copy(self.src.at[self.pc.me], self.dst.at[self.pc.me], self.local)

    def start(self, turn=0, turns=1):
        pc = self.pc
        if turn == 0:
            self.own().start()
        per = -(-(pc.total - 1) // turns)

        @pl.loop(1 + turn * per, min(1 + (turn + 1) * per, pc.total))
        def _(k):
            d = lax.rem(pc.me + k, pc.total)
            remote(self.src.at[d], self.dst.at[pc.me], self.send, self.recv, pc.at(d)).start()

    def whole(self):
        blocks = pl.ds(0, self.pc.total - 1)
        return remote(self.src.at[blocks], self.dst.at[blocks], self.send, self.recv, self.pc.dev(c=1 - self.pc.c))

    def wait(self):
        self.own().wait()
        self.whole().wait_recv()

    def done(self):
        self.whole().wait_send()


class Gather:
    def __init__(self, pc, own, slots, sems):
        self.pc, self.own = pc, own
        self.place = slots
        self.zs, self.zr, self.ys, self.yr, self.xs, self.xr, self.cs, self.cr, self.ls = sems

    @staticmethod
    def sems(Z):
        T = pltpu.SemaphoreType.DMA
        n = len(GATHER_UNITS)
        return [
            T((n, 2 * Z - 2)), T((n, 2 * Z - 2)), T((n, 2 * Z - 1)), T((n,)),
            T((n, 2)), T((n, 2)), T((n, 2)), T((n, 2)), T((n,)),
        ]

    def up(self):
        return jnp.minimum(self.pc.z + 1, self.pc.Z - 1)

    def down(self):
        return jnp.maximum(self.pc.z - 1, 0)

    def slots(self, u, z, y, cols):
        return self.place(GATHER_UNITS[u][0], z, y, self.pc.c, cols)

    def cols(self, u):
        return self.pc.cols(GATHER_UNITS[u])

    def mine(self, u):
        pc = self.pc
        src = self.own(GATHER_UNITS[u][0], self.cols(u))
        return pltpu.make_async_copy(src, self.slots(u, pc.z, pc.y, self.cols(u)), self.ls.at[u])

    def start(self, u):
        pc = self.pc
        Z = pc.Z
        src = self.own(GATHER_UNITS[u][0], self.cols(u))
        dst = self.slots(u, pc.z, pc.y, self.cols(u))
        self.mine(u).start()
        pc.go(remote(src, dst, self.zs.at[u, 0], self.zr.at[u, 0], pc.dev(z=self.up())), pc.z < Z - 1)
        k = Z - 1
        pc.go(remote(src, dst, self.zs.at[u, k], self.zr.at[u, k], pc.dev(z=self.down())), pc.z > 0)
        pc.go(remote(src, dst, self.ys.at[u, 0], self.yr.at[u], pc.dev(y=1 - pc.y)))

    def hop(self, u, h):
        pc = self.pc
        Z = pc.Z
        for upward in (True, False):
            k = (0 if upward else Z - 1) + h - 1
            if upward:
                z, here, onward, to = jnp.maximum(pc.z - h, 0), pc.z >= h, pc.z < Z - 1, self.up()
            else:
                z, here, onward, to = jnp.minimum(pc.z + h, Z - 1), pc.z + h < Z, pc.z > 0, self.down()
            ref = self.slots(u, z, pc.y, self.cols(u))
            pl.when(here)(remote(ref, ref, self.zs.at[u, k], self.zr.at[u, k], pc.dev(z=to)).wait_recv)
            if h < Z - 1:
                pc.go(
                    remote(ref, ref, self.zs.at[u, k + 1], self.zr.at[u, k + 1], pc.dev(z=to)),
                    jnp.logical_and(here, onward),
                )
            pc.go(remote(ref, ref, self.ys.at[u, 1 + k], self.yr.at[u], pc.dev(y=1 - pc.y)), here)
        if h == Z - 1:
            self.mine(u).wait()
            self.across(u, pc.y, 0)

    def across(self, u, y, k):
        pc = self.pc
        if GATHER_UNITS[u][3]:
            ref = self.slots(u, slice(None), y, pc.give(GATHER_UNITS[u]))
            pc.go(remote(ref, ref, self.xs.at[u, k], self.xr.at[u, k], pc.dev(x=1 - pc.x)))

    def row(self, u):
        pc = self.pc
        ref = self.slots(u, slice(None), 1 - pc.y, self.cols(u))
        remote(ref, ref, self.ys.at[u, 0], self.yr.at[u], pc.dev(y=1 - pc.y)).wait_recv()
        self.across(u, 1 - pc.y, 1)
        ref = self.slots(u, slice(None), slice(None), self.cols(u))
        pc.go(remote(ref, ref, self.cs.at[u, 0], self.cr.at[u, 0], pc.dev(c=1 - pc.c)))

    def plane(self, u):
        pc = self.pc
        if not GATHER_UNITS[u][3]:
            return
        take = pc.take(GATHER_UNITS[u])
        for k, y in enumerate((pc.y, 1 - pc.y)):
            ref = self.slots(u, slice(None), y, take)
            remote(ref, ref, self.xs.at[u, k], self.xr.at[u, k], pc.dev(x=1 - pc.x)).wait_recv()
        ref = self.slots(u, slice(None), slice(None), take)
        pc.go(remote(ref, ref, self.cs.at[u, 1], self.cr.at[u, 1], pc.dev(c=1 - pc.c)))

    def core(self, u):
        pc = self.pc
        parts = [pc.cols(GATHER_UNITS[u])] + ([pc.take(GATHER_UNITS[u])] if GATHER_UNITS[u][3] else [])
        for k, cols in enumerate(parts):
            ref = self.place(GATHER_UNITS[u][0], slice(None), slice(None), 1 - pc.c, cols)
            remote(ref, ref, self.cs.at[u, k], self.cr.at[u, k], pc.dev(c=1 - pc.c)).wait_recv()


class Scatter:
    def __init__(self, pc, terms, get, put, from_c, from_x, from_y, from_z, from_f, sems):
        self.pc, self.terms, self.get, self.put = pc, terms, get, put
        self.from_c, self.from_x, self.from_y, self.from_z, self.from_f = from_c, from_x, from_y, from_z, from_f
        self.cs, self.cr, self.xs, self.xr, self.ys, self.yr, self.zs, self.zr, self.fs, self.fr, self.free = sems
        z = pc.z
        self.inner = jnp.logical_or(z == 1, z == 2)
        self.outer = jnp.logical_not(self.inner)
        self.mate = z + 1 - 2 * lax.rem(z, 2)
        self.far_in = jnp.where(z < 2, 2, 1)
        self.far_out = jnp.where(z < 2, 3, 0)
        self.x_lo, self.y_lo = [], []
        used = {}
        for p, lo, n, w in SCATTER_UNITS:
            a, b = used.get(p, (0, 0))
            self.x_lo.append(a)
            self.y_lo.append(b)
            used[p] = (a + w, b + n - w)

    @staticmethod
    def sems():
        T = pltpu.SemaphoreType.DMA
        n = len(SCATTER_UNITS)
        return [
            T((n,)), T((n,)), T((n,)), T((n,)), T((n,)), T((n,)), T((n, 5)), T((n, 4)), T((n,)), T((n,)),
            pltpu.SemaphoreType.REGULAR((n,)),
        ]

    @staticmethod
    def buffers(Z, rows):
        n = PIECES
        give, win = [0] * n, [0] * n
        for p, lo, k, w in SCATTER_UNITS:
            give[p] += w
            win[p] += k - w
        give, win = max(give), max(win)
        return [
            pltpu.VMEM((RING, Z, 2, rows, D), BF),
            pltpu.VMEM((n, Z, 2, rows, give), BF),
            pltpu.VMEM((n, Z, rows, win), BF),
            pltpu.VMEM((n, 4, rows, win), BF),
            pltpu.VMEM((n, rows, win), BF),
        ]

    def x_at(self, u):
        return pl.ds(self.x_lo[u], SCATTER_UNITS[u][3])

    def y_at(self, u):
        p, lo, n, w = SCATTER_UNITS[u]
        return pl.ds(self.y_lo[u], n - w)

    def add(self, u, z, y, cols, value):
        p = SCATTER_UNITS[u][0]
        c = self.pc.c
        self.put(p, z, y, c, cols, self.get(p, z, y, c, cols) + value)

    def part(self, u, z, y, cols):
        return self.terms(SCATTER_UNITS[u][0], z, y, self.pc.c, cols)

    def start(self, u):
        pc = self.pc
        p, lo, n, w = SCATTER_UNITS[u]
        if u >= RING:
            pl.semaphore_wait(self.free.at[u], 1)
        src = self.terms(p, slice(None), slice(None), 1 - pc.c, pl.ds(lo, n))
        dst = self.from_c.at[u % RING, :, :, :, pl.ds(0, n)]
        pc.go(remote(src, dst, self.cs.at[u], self.cr.at[u], pc.dev(c=1 - pc.c)))

    def core(self, u):
        pc = self.pc
        p, lo, n, w = SCATTER_UNITS[u]
        ref = self.from_c.at[u % RING, :, :, :, pl.ds(0, n)]
        remote(ref, ref, self.cs.at[u], self.cr.at[u], pc.dev(c=1 - pc.c)).wait_recv()
        for z in range(pc.Z):
            for y in range(2):
                self.add(u, z, y, pl.ds(lo, n), self.from_c[u % RING, z, y, :, pl.ds(0, n)])
        if u + RING < len(SCATTER_UNITS):
            pl.semaphore_signal(self.free.at[u + RING], inc=1, device_id=pc.dev(c=1 - pc.c), device_id_type=MESH)
        if w:
            src = self.part(u, slice(None), slice(None), pc.take(SCATTER_UNITS[u]))
            dst = self.from_x.at[p, :, :, :, self.x_at(u)]
            pc.go(remote(src, dst, self.xs.at[u], self.xr.at[u], pc.dev(x=1 - pc.x)))
        else:
            self.across(u)

    def plane(self, u):
        pc = self.pc
        p, lo, n, w = SCATTER_UNITS[u]
        if w:
            ref = self.from_x.at[p, :, :, :, self.x_at(u)]
            remote(ref, ref, self.xs.at[u], self.xr.at[u], pc.dev(x=1 - pc.x)).wait_recv()
            for z in range(pc.Z):
                for y in range(2):
                    self.add(u, z, y, pc.give(SCATTER_UNITS[u]), self.from_x[p, z, y, :, self.x_at(u)])
            self.across(u)

    def across(self, u):
        pc = self.pc
        src = self.part(u, slice(None), 1 - pc.y, pc.cols(SCATTER_UNITS[u]))
        dst = self.from_y.at[SCATTER_UNITS[u][0], :, :, self.y_at(u)]
        pc.go(remote(src, dst, self.ys.at[u], self.yr.at[u], pc.dev(y=1 - pc.y)))

    def z_ref(self, u, k):
        return self.from_z.at[SCATTER_UNITS[u][0], k, :, self.y_at(u)]

    def z_add(self, u, k, z):
        ref = self.z_ref(u, k)
        remote(ref, ref, self.zs.at[u, k], self.zr.at[u, k], self.pc.dev(z=self.mate)).wait_recv()
        value = self.from_z[SCATTER_UNITS[u][0], k, :, self.y_at(u)]
        self.add(u, z, self.pc.y, self.pc.cols(SCATTER_UNITS[u]), value)

    def row(self, u):
        pc = self.pc
        p = SCATTER_UNITS[u][0]
        cols = pc.cols(SCATTER_UNITS[u])
        ref = self.from_y.at[p, :, :, self.y_at(u)]
        remote(ref, ref, self.ys.at[u], self.yr.at[u], pc.dev(y=1 - pc.y)).wait_recv()
        for z in range(pc.Z):
            self.add(u, z, pc.y, cols, self.from_y[p, z, :, self.y_at(u)])
        for k, z in enumerate((self.mate, self.far_in, self.far_out)):
            copy = remote(
                self.part(u, z, pc.y, cols), self.z_ref(u, k), self.zs.at[u, k], self.zr.at[u, k], pc.dev(z=self.mate)
            )
            pc.go(copy, self.outer if k else None)

    def middle(self, u):
        pc = self.pc
        cols = pc.cols(SCATTER_UNITS[u])
        far = ((1, self.far_in), (2, self.far_out))

        @pl.when(self.inner)
        def _():
            for k, z in far:
                self.z_add(u, k, z)

        for k, z in far:
            src = self.part(u, z, pc.y, cols)
            pc.go(remote(src, self.z_ref(u, 3), self.zs.at[u, 2 + k], self.zr.at[u, 3], pc.dev(z=z)), self.inner)

    def f_ref(self, u):
        return self.from_f.at[SCATTER_UNITS[u][0], :, self.y_at(u)]

    def line(self, u):
        pc = self.pc
        for k in (0, 3):
            self.z_add(u, k, pc.z)
        src = self.part(u, pc.z, pc.y, pc.cols(SCATTER_UNITS[u]))
        pc.go(remote(src, self.f_ref(u), self.fs.at[u], self.fr.at[u], pc.dev(x=1 - pc.x)))

    def last(self, u, out):
        pc = self.pc
        unit = p, lo, n, w = SCATTER_UNITS[u]
        ref = self.f_ref(u)
        remote(ref, ref, self.fs.at[u], self.fr.at[u], pc.dev(x=1 - pc.x)).wait_recv()
        at = self.y_lo[u]

        def own(cols):
            return self.get(p, pc.z, pc.y, pc.c, cols).astype(F32)

        if w:
            out[:, pc.give(unit)] = own(pc.give(unit))
            theirs = pl.ds(pl.multiple_of(at + (1 - pc.x) * (n - 2 * w), 128), w)
            out[:, pc.take(unit)] = self.from_f[p, :, theirs].astype(F32)
        if n > 2 * w:
            both = pl.ds(pl.multiple_of(at + pc.x * w, 128), n - 2 * w)
            shared = pl.ds(lo + w, n - 2 * w)
            out[:, shared] = own(shared) + self.from_f[p, :, both].astype(F32)


def row_mean(v):
    return jnp.sum(v, axis=-1, keepdims=True) * (1.0 / D)


BQ, BV, BO, G1, B1, BD, G2, B2 = range(8)


def layer_kernel(
    fsdp, rows,
    order, lengths, slopes, tokens_in, grads_in, *refs,
):
    small_in, (wq_in, wo_in, wg_in, wd_in) = refs[:8], refs[8:12]
    OUT, DX, GQ, GW, GG, GD, SMALLG, *refs = refs[12:]
    (
    wa, wd, raw, outv, xs, gs, small, small_own, smallf, qkv, dist, lse, ctxt, y1, y1b, xhat, rstd, act, slope_up, zed, acc, dfb, tr,
    dxr, sgrad, sparts, gsum, from_c, from_x, from_y, from_z, from_f, *sems,
    ) = refs
    pc = Place(fsdp)
    Z = pc.Z
    L = pc.total * raw.shape[1]
    gsems, ssems, esems, rsem = sems[:9], sems[9:20], sems[20:23], sems[23]
    w_pc = wa.shape[1:]

    def own(p, cols):
        if p < 3:
            return wq_in.at[:, pl.ds(pl.multiple_of(D * p + cols.start, 128), cols.size)]
        if p == 3:
            return wo_in.at[:, cols]
        if p < 12:
            i, j = (p - 4) // 2, (p - 4) % 2
            return wg_in.at[:, pl.ds(pl.multiple_of(FF * j + D * i + cols.start, 128), cols.size)]
        return wd_in.at[pl.ds(rows * (p - 12), rows), cols]

    def slots(p, z, y, c, cols):
        if p < 12:
            return wa.at[p, z, y, c, :, cols]
        return wd.at[z, y, c, p - 12, :, cols]

    def get(p, z, y, c, cols):
        if p < 12:
            return wa[p, z, y, c, :, cols]
        return wd[z, y, c, p - 12, :, cols]

    def put(p, z, y, c, cols, value):
        if p < 12:
            wa[p, z, y, c, :, cols] = value
        else:
            wd[z, y, c, p - 12, :, cols] = value

    def out_of(p):
        if p >= 12:
            return GD.at[pl.ds(rows * (p - 12), rows)]
        if p == 3:
            return GW
        if p < 3:
            return GQ.at[:, pl.ds(D * p, D)]
        i, j = (p - 4) // 2, (p - 4) % 2
        return GG.at[:, pl.ds(FF * j + D * i, D)]

    def w_cols(p, cols):
        return wa[p, :, :, :, :, cols].reshape(D, cols.size)

    def w_all(p):
        return wa[p].reshape(D, D)

    g = Gather(pc, own, slots, gsems)
    sc = Scatter(pc, slots, get, put, from_c, from_x, from_y, from_z, from_f, ssems)
    ex_x = Exchange(pc, outv, xs, esems, 0)
    ex_g = Exchange(pc, grads_in, gs, esems, 1)
    ex_o = Exchange(pc, outv, OUT, esems, 3)
    ex_d = Exchange(pc, raw, dxr, esems, 4)
    ex_s = Exchange(pc, sparts, gsum, esems, 5)
    len_s = lengths[pc.x, order[pc.x, pc.f]]

    def tokens(r):
        n = r.size // 16
        return xs[pl.ds(r.start // 16, n)].reshape(r.size, D)

    def deal():
        @pl.loop(0, pc.total)
        def _(d):
            m = d // fsdp
            outv[d] = raw[m * fsdp + order[m, lax.rem(d, fsdp)]]

    def prepare():
        k = lax.broadcasted_iota(jnp.int32, (L, L), 0)
        q = lax.broadcasted_iota(jnp.int32, (L, L), 1)
        dist[...] = jnp.where(k < len_s, jnp.abs(k - q).astype(F32), -NEGATIVE)

    def place_small():
        for f in range(fsdp):
            smallf[:, pl.ds(f * rows, rows)] = small[f, :, pl.ds(0, rows)]

    def project(p):
        @pl.loop(0, D // 256)
        def _(t):
            cols = block(t, 256)
            r = mm(xs[...].reshape(L, D), w_cols(p, cols))
            if p != 1:
                r = r + smallf[pl.ds(BQ if p == 0 else BV, 1), cols]
            qkv[p, :, cols] = r.astype(BF)

    def attend(j):
        cols = block(j, 128)
        lane = lax.broadcasted_iota(jnp.int32, (L, 128), 1)
        q2, k2 = qkv[0, :, cols], qkv[1, :, cols]
        vt = qkv[2, :, cols].T
        for q in range(L // 256):
            qr = pl.ds(256 * q, 256)
            parts = []
            for s in range(2):
                qm = jnp.where((lane < 64) if s == 0 else (lane >= 64), q2, jnp.zeros_like(q2))
                st = mm_nt(k2, qm[256 * q : 256 * q + 256])
                st = st * (0.125 * LOG2E) - dist[:, qr] * slopes[2 * j + s]
                top = jnp.max(st, axis=0, keepdims=True)
                e = jnp.exp2(st - top)
                total = jnp.sum(e, axis=0, keepdims=True)
                lse[2 * j + s, :, qr] = top + jnp.log2(total)
                pr = (e * (1.0 / total)).astype(BF)
                parts.append(mm(vt[64 * s : 64 * s + 64], pr))
            ctxt[qr, cols] = jnp.concatenate(parts, axis=0).T.astype(BF)

    def first_norm():
        @pl.loop(0, D // 256)
        def _(t):
            cols = block(t, 256)
            acc[:, cols] = mm(ctxt[...], w_cols(3, cols)) + smallf[pl.ds(BO, 1), cols]

        @pl.loop(0, L // 64)
        def _(i):
            r = block(i, 64)
            h = acc[r, :] + tokens(r).astype(F32)
            centre = h - row_mean(h)
            rs = lax.rsqrt(row_mean(centre * centre) + EPSILON)
            xh = centre * rs
            xhat[r, :] = xh
            rstd[r, :] = jnp.broadcast_to(rs, (64, 128))
            yy = xh * smallf[pl.ds(G1, 1), :] + smallf[pl.ds(B1, 1), :]
            y1[r, :] = yy
            y1b[r, :] = yy.astype(BF)

    def gated(i, s):
        wc = block(s, 256)
        cols = block(i * 3 + s, 256)
        a = mm(y1b[...], w_cols(4 + 2 * i, wc))
        u = mm(y1b[...], w_cols(5 + 2 * i, wc))
        cdf = 0.5 + 0.5 * lax.erf(a * math.sqrt(0.5))
        pdf = jnp.exp2(a * a * (-0.5 * LOG2E)) * (1.0 / math.sqrt(2.0 * math.pi))
        gelu = a * cdf
        zed[:, cols] = (gelu * u).astype(BF)
        act[:, cols] = gelu.astype(BF)
        slope_up[:, cols] = (u * (cdf + a * pdf)).astype(BF)

    def second_norm():
        @pl.loop(0, D // 256)
        def _(t):
            cols = block(t, 256)
            w = wd[:, :, :, :, :, cols].reshape(FF, 256)
            acc[:, cols] = mm(zed[...], w) + smallf[pl.ds(BD, 1), cols]

        def step(i, sums):
            r = block(i, 64)
            h = acc[r, :] + y1[r, :]
            centre = h - row_mean(h)
            rs = lax.rsqrt(row_mean(centre * centre) + EPSILON)
            xh = centre * rs
            gain = smallf[pl.ds(G2, 1), :]
            valid = (lax.broadcasted_iota(jnp.int32, (64, D), 0) + i * 64) < len_s
            res = jnp.where(valid, xh * gain + smallf[pl.ds(B2, 1), :], 0.0).astype(BF)
            outv[pl.ds(i * 4, 4)] = res.reshape(4, 16, D)
            up = jnp.where(valid, gs[pl.ds(i * 4, 4)].reshape(64, D).astype(F32), 0.0)
            dx = up * gain
            dh = rs * (dx - row_mean(dx) - xh * row_mean(dx * xh))
            low = dh.astype(BF)
            acc[r, :] = dh
            dfb[r, :] = low
            sg, sb, sd = sums
            return (
                sg + jnp.sum(up * xh, axis=0, keepdims=True),
                sb + jnp.sum(up, axis=0, keepdims=True),
                sd + jnp.sum(low.astype(F32), axis=0, keepdims=True),
            )

        zero = jnp.zeros((1, D), F32)
        sg, sb, sd = lax.fori_loop(0, L // 64, step, (zero, zero, zero))
        sgrad[pl.ds(G2, 1), :] = sg
        sgrad[pl.ds(B2, 1), :] = sb
        sgrad[pl.ds(BD, 1), :] = sd

    def ff_back(i):
        cols = block(i, D)
        part = pl.ds(i * Z // 4, Z // 4)
        dz = mm_nt(dfb[...], wd[part].reshape(D, D))
        dgate = (dz * slope_up[:, cols].astype(F32)).astype(BF)
        dup = (dz * act[:, cols].astype(F32)).astype(BF)
        acc[...] += mm_nt(dgate, w_all(4 + 2 * i)) + mm_nt(dup, w_all(5 + 2 * i))
        wa[4 + 2 * i] = mm(tr[...], dgate).astype(BF).reshape(w_pc)
        wa[5 + 2 * i] = mm(tr[...], dup).astype(BF).reshape(w_pc)
        wd[part] = mm_tn(zed[:, cols], dfb[...]).astype(BF).reshape((Z // 4,) + wd.shape[1:])

    def first_norm_back():
        def step(i, sums):
            r = block(i, 64)
            up = acc[r, :]
            xh = xhat[r, :]
            dx = up * smallf[pl.ds(G1, 1), :]
            dh = rstd[r, :][:, :1] * (dx - row_mean(dx) - xh * row_mean(dx * xh))
            low = dh.astype(BF)
            xhat[r, :] = dh
            dfb[r, :] = low
            sg, sb, sd = sums
            return (
                sg + jnp.sum(up * xh, axis=0, keepdims=True),
                sb + jnp.sum(up, axis=0, keepdims=True),
                sd + jnp.sum(low.astype(F32), axis=0, keepdims=True),
            )

        zero = jnp.zeros((1, D), F32)
        sg, sb, sd = lax.fori_loop(0, L // 64, step, (zero, zero, zero))
        sgrad[pl.ds(G1, 1), :] = sg
        sgrad[pl.ds(B1, 1), :] = sb
        sgrad[pl.ds(BO, 1), :] = sd

    def out_back():
        y1b[...] = mm_nt(dfb[...], w_all(3)).astype(BF)
        wa[3] = mm_tn(ctxt[...], dfb[...]).astype(BF).reshape(w_pc)

    def dqkv(p):
        return act.at[:, pl.ds(D * p, D)]

    def attend_back(j):
        cols = block(j, 128)
        lane = lax.broadcasted_iota(jnp.int32, (L, 128), 1)
        q2, k2, v2 = (qkv[i, :, cols] for i in range(3))
        do2 = y1b[:, cols]
        kt = k2.T
        dv = dk = None
        for q in range(L // 256):
            qr = pl.ds(256 * q, 256)
            qs = slice(256 * q, 256 * q + 256)
            parts = []
            for s in range(2):
                half = (lane < 64) if s == 0 else (lane >= 64)
                qm = jnp.where(half, q2, jnp.zeros_like(q2))[qs]
                dm = jnp.where(half, do2, jnp.zeros_like(do2))[qs]
                st = mm_nt(k2, qm) * (0.125 * LOG2E) - dist[:, qr] * slopes[2 * j + s]
                pr = jnp.exp2(st - lse[2 * j + s, :, qr])
                dp = mm_nt(v2, dm)
                ds = (pr * (dp - jnp.sum(pr * dp, axis=0, keepdims=True))).astype(BF)
                a, b = mm(pr.astype(BF), dm), mm(ds, qm)
                dv = a if dv is None else dv + a
                dk = b if dk is None else dk + b
                parts.append(mm(kt[64 * s : 64 * s + 64], ds))
            dqkv(0)[qr, cols] = (jnp.concatenate(parts, axis=0).T * 0.125).astype(BF)
        dqkv(1)[:, cols] = (dk * 0.125).astype(BF)
        dqkv(2)[:, cols] = dv.astype(BF)

    def weights_back(p):
        x = xs[...].reshape(L, D)
        d = dqkv(p)
        wa[p] = mm_tn(x, d[...]).astype(BF).reshape(w_pc)
        if p != 1:
            r = BQ if p == 0 else BV
            sgrad[pl.ds(r, 1), :] = jnp.sum(d[...].astype(F32), axis=0, keepdims=True)

    def tokens_back():
        @pl.loop(0, L // 128)
        def _(i):
            r = block(i, 128)
            v = xhat[r, :]
            for p in range(3):
                v = v + mm_nt(dqkv(p)[r, :], w_all(p))
            raw[pl.ds(i * 8, 8)] = v.astype(BF).reshape(8, 16, D)

    def split_small():
        sparts[...] = jnp.zeros_like(sparts)
        for d in range(pc.total):
            at = d % fsdp * rows
            sparts[d, :, pl.ds(0, rows)] = sgrad[:, pl.ds(at, rows)]

    def undeal():
        @pl.loop(0, pc.total)
        def _(k):
            m, n = k // fsdp, lax.rem(k, fsdp)

            def find(f, at):
                return jnp.where(order[m, f] == n, f, at)

            DX[k] = dxr[m * fsdp + lax.fori_loop(0, fsdp, find, 0)]

    def spread(ex, t, at):
        first, count = at
        if first <= t < first + count:
            ex.start(t - first, count)

    take_raw = pltpu.make_async_copy(tokens_in, raw, rsem)
    take_raw.start()
    pc.signal()
    small_own[...] = jnp.zeros_like(small_own)
    for i, ref in enumerate(small_in):
        small_own[pl.ds(i, 1), pl.ds(0, rows)] = ref[...].astype(F32)
    prepare()
    take_raw.wait()
    deal()
    pc.wait()

    me_small = small.at[pc.f]
    keep_small = pltpu.make_async_copy(small_own, me_small, esems[2].at[2])
    keep_small.start()

    @pl.loop(1, fsdp)
    def _(k):
        f = lax.rem(pc.f + k, fsdp)
        remote(small_own, me_small, esems[0].at[2], esems[1].at[2], (pc.x, f)).start()

    small_all = remote(
        small.at[pl.ds(0, fsdp - 1)], small.at[pl.ds(0, fsdp - 1)], esems[0].at[2], esems[1].at[2],
        pc.dev(c=1 - pc.c),
    )

    def after_core(p):
        if p == 2:
            ex_x.wait()
            small_all.wait_recv()
            keep_small.wait()
            place_small()
            for i in range(3):
                project(i)
        if 2 <= p <= 4:
            pl.loop(2 * (p - 2), 2 * (p - 2) + 2)(attend)
        if p == 4:
            first_norm()
            tr[...] = y1b[...].T
        if 5 <= p < 12 and p % 2 == 1:
            for s in range(3):
                gated((p - 5) // 2, s)

    units = len(GATHER_UNITS)
    finished = [max(u for u in range(units) if GATHER_UNITS[u][0] == p) for p in range(PIECES)]
    for t in range(units + CORE_AT):
        spread(ex_x, t, X_AT)
        spread(ex_g, t, G_AT)
        for u in range(units):
            if t == max(0, u - AHEAD):
                g.start(u)
        for h in range(1, Z):
            for u in range(units):
                if t == max(0, u - AHEAD) + h:
                    g.hop(u, h)
        if 0 <= t - ROW_AT < units:
            g.row(t - ROW_AT)
        if 0 <= t - PLANE_AT < units:
            g.plane(t - PLANE_AT)
        if 0 <= t - CORE_AT < units:
            u = t - CORE_AT
            g.core(u)
            for p in range(PIECES):
                if finished[p] == u:
                    after_core(p)
    ex_g.wait()
    ex_x.done()
    second_norm()
    pc.finish()

    units = len(SCATTER_UNITS)
    stages = STAGES if STAGES else (("core", 1), ("plane", 3), ("row", 5), ("middle", 6), ("line", 8), ("last", 10))
    for t in range(units + 10):
        if t < 8 and t % 2 == 0:
            ff_back(t // 2)
        if t == 8:
            first_norm_back()
            out_back()
        if 9 <= t < 12:
            pl.loop(2 * (t - 9), 2 * (t - 9) + 2)(attend_back)
        if t == 12:
            tokens_back()
            for p in range(3):
                weights_back(p)
            split_small()
            ex_s.start()
        spread(ex_o, t, O_AT)
        spread(ex_d, t, D_AT)
        if t < units:
            sc.start(t)
        for name, off in stages:
            if 0 <= t - off < units:
                u = t - off
                if name == "last":
                    sc.last(u, out_of(SCATTER_UNITS[u][0]))
                else:
                    getattr(sc, name)(u)
    ex_s.wait()

    def add(i, v):
        return v + gsum[i]

    total = lax.fori_loop(1, pc.total, add, gsum[0])
    SMALLG[...] = total[:, :rows]
    ex_d.wait()
    undeal()
    ex_o.wait()
    for e in (ex_g, ex_o, ex_d, ex_s):
        e.done()
    small_all.wait_send()
    pc.finish()


def hand_over(*refs):
    src, small, dst, parts, sem = refs[:6], refs[6], refs[7:13], refs[13:21], refs[21]
    copies = [pltpu.make_async_copy(a, b, sem.at[k]) for k, (a, b) in enumerate(zip(src, dst))]
    for c in copies:
        c.start()
    for k, ref in enumerate(parts):
        ref[...] = small[pl.ds(k, 1), :]
    for c in copies:
        c.wait()


def per_device(
    tokens_in, out_grad, seq_lengths, order, w_qkv, bias_q, bias_v, w_out, bias_out, ln1_gain, ln1_bias, w_gate_up,
    w_down, bias_down, ln2_gain, ln2_bias,
):
    fsdp = lax.axis_size("fsdp")
    total = 2 * fsdp
    rows = w_out.shape[0]
    here = tokens_in.shape[2]
    L = here * total
    Z = fsdp // 4
    small = [v.reshape(1, rows) for v in (bias_q, bias_v, bias_out, ln1_gain, ln1_bias, bias_down, ln2_gain, ln2_bias)]
    slopes = jnp.array(slope_list(HEADS), F32) * LOG2E
    hbm = pl.BlockSpec(memory_space=pl.ANY)
    smem = pl.BlockSpec(memory_space=pltpu.SMEM)
    vmem = pl.BlockSpec(memory_space=pltpu.VMEM)
    S = jax.ShapeDtypeStruct
    T = pltpu.SemaphoreType.DMA
    V = pltpu.VMEM
    rows_of = (total, here, D)
    results = pl.pallas_call(
        functools.partial(layer_kernel, fsdp, rows),
        out_shape=[
            S(rows_of, BF), S(rows_of, BF), S((rows, 3 * D), F32), S((rows, D), F32), S((rows, 2 * FF), F32),
            S((4 * rows, D), F32), S((8, rows), F32),
        ],
        in_specs=[smem] * 3 + [hbm] * 2 + [vmem] * 8 + [hbm] * 4,
        out_specs=[hbm] + [vmem] * 6,
        scratch_shapes=[
            V((12, Z, 2, 2, rows, D), BF), V((Z, 2, 2, 4, rows, D), BF), V(rows_of, BF), V(rows_of, BF),
            V(rows_of, BF), V(rows_of, BF), V((fsdp, 8, 128), F32), V((8, 128), F32), V((8, D), F32), V((3, L, D), BF), V((L, L), F32),
            V((HEADS, 1, L), F32), V((L, D), BF), V((L, D), F32), V((L, D), BF), V((L, D), F32), V((L, 128), F32),
            V((L, FF), BF), V((L, FF), BF), V((L, FF), BF), V((L, D), F32), V((L, D), BF), V((D, L), BF),
            V(rows_of, BF), V((8, D), F32), V((total, 8, 128), F32), V((total, 8, 128), F32),
            *Scatter.buffers(Z, rows), *Gather.sems(Z), *Scatter.sems(), T((6,)), T((6,)), T((6,)), T,
        ],
        compiler_params=pltpu.CompilerParams(collective_id=0, has_side_effects=True, vmem_limit_bytes=VMEM_LIMIT),
        name="layer",
    )(order, seq_lengths, slopes, tokens_in.reshape(rows_of), out_grad.reshape(rows_of), *small, w_qkv, w_out, w_gate_up, w_down)
    output, input_grad, gq, gw, gg, gd, *mine = pl.pallas_call(
        hand_over,
        out_shape=[S(r.shape, r.dtype) for r in results[:6]] + [S((1, rows), F32)] * 8,
        in_specs=[vmem] * 7,
        out_specs=[hbm] * 6 + [vmem] * 8,
        scratch_shapes=[T((6,))],
        name="hand_over",
    )(*results)
    mine = [v.reshape(rows) for v in mine]
    return (
        output.reshape(tokens_in.shape), input_grad.reshape(tokens_in.shape), gq, mine[BQ], mine[BV], gw, mine[BO],
        mine[G1], mine[B1], gg, gd, mine[BD], mine[G2], mine[B2],
    )


def solution(mesh):
    fsdp = mesh.shape["fsdp"]
    rows = D // fsdp
    kernels = mesh.shape["ctx"] == M and fsdp == 16 and rows % 16 == 0
    return jax.shard_map(
        per_device if kernels else per_device_plain,
        mesh=mesh,
        in_specs=(
            P(None, None, ("ctx", "fsdp"), None),
            P(None, None, ("ctx", "fsdp"), None),
            P(),
            P(),
            P("fsdp", None),
            P("fsdp"),
            P("fsdp"),
            P("fsdp", None),
            P("fsdp"),
            P("fsdp"),
            P("fsdp"),
            P("fsdp", None),
            P("fsdp", None),
            P("fsdp"),
            P("fsdp"),
            P("fsdp"),
        ),
        out_specs=(
            P(None, None, ("ctx", "fsdp"), None),
            P(None, None, ("ctx", "fsdp"), None),
            P("fsdp", None),
            P("fsdp"),
            P("fsdp"),
            P("fsdp", None),
            P("fsdp"),
            P("fsdp"),
            P("fsdp"),
            P("fsdp", None),
            P("fsdp", None),
            P("fsdp"),
            P("fsdp"),
            P("fsdp"),
        ),
        check_vma=False,
    )
```

```python
import functools
import math

import jax
import jax.numpy as jnp
from jax import lax
from jax.experimental import pallas as pl
from jax.experimental.pallas import tpu as pltpu
from jax.sharding import PartitionSpec as P

D = 768
HEADS = 12
HEAD_DIM = 64
FF = 3072
M = 2
EPSILON = 1e-12
NEGATIVE = -1e30
MESH = pl.DeviceIdType.MESH
BF = jnp.bfloat16
F32 = jnp.float32
LOG2E = math.log2(math.e)
VMEM_LIMIT = 62 << 20


def slope_list(head_count):

    def powers(number):
        anchor = 2.0 ** (-(2.0 ** (-(math.log2(number) - 3))))
        return [anchor ** (power_index + 1) for power_index in range(number)]

    closest = 2 ** int(math.floor(math.log2(head_count)))
    return powers(closest) + powers(2 * closest)[0::2][: head_count - closest]


def layer_norm(inputs, gain_row, offset_row):
    centre = inputs - jnp.mean(inputs, axis=-1, keepdims=True)
    spread = jnp.mean(centre * centre, axis=-1, keepdims=True)
    return centre * lax.rsqrt(spread + EPSILON) * gain_row + offset_row


def gated_unit(gate_up):
    return jax.nn.gelu(gate_up[:, :FF], approximate=False) * gate_up[:, FF:]


def rows_product(former, latter):
    return lax.dot_general(
        former, latter, (((0,), (0,)), ((), ())), preferred_element_type=jnp.float32
    )


def by_transpose(former, latter):
    return lax.dot_general(
        former, latter, (((1,), (1,)), ((), ())), preferred_element_type=jnp.float32
    )


def plain_product(former, latter):
    return jnp.dot(former, latter, preferred_element_type=jnp.float32)


def masked_scores(heads_q, heads_k, position, key_place, length, slopes):
    raw_scores = (
        jnp.einsum("qhd,khd->hqk", heads_q, heads_k, preferred_element_type=jnp.float32) * 0.125
    )
    distance = jnp.abs(position[:, None] - key_place[None, :]).astype(jnp.float32)
    raw_scores = raw_scores - slopes[:, None, None] * distance[None]
    return jnp.where((key_place < length)[None, None, :], raw_scores, NEGATIVE)


def fetch_weights(shards):
    return (
        lax.all_gather(shards[0], "fsdp", axis=0, tiled=True),
        lax.all_gather(shards[1], "fsdp", axis=0, tiled=True),
        lax.all_gather(shards[2], "fsdp", axis=0, tiled=True),
        lax.all_gather(shards[3], "fsdp", axis=0, tiled=True),
        lax.all_gather(shards[4], "fsdp", axis=0, tiled=True),
        lax.all_gather(shards[5], "fsdp", axis=0, tiled=True),
        lax.all_gather(shards[6], "fsdp", axis=0, tiled=True),
        lax.all_gather(shards[7], "fsdp", axis=0, tiled=True),
        lax.all_gather(shards[8], "fsdp", axis=0, tiled=True),
        lax.all_gather(shards[9], "fsdp", axis=0, tiled=True),
        lax.all_gather(shards[10], "fsdp", axis=0, tiled=True),
        lax.all_gather(shards[11], "fsdp", axis=0, tiled=True),
    )


def reduce_grads(grad_terms):
    shard_sums = (
        lax.psum_scatter(grad_terms[0], "fsdp", scatter_dimension=0, tiled=True),
        lax.psum_scatter(grad_terms[1], "fsdp", scatter_dimension=0, tiled=True),
        lax.psum_scatter(grad_terms[2], "fsdp", scatter_dimension=0, tiled=True),
        lax.psum_scatter(grad_terms[3], "fsdp", scatter_dimension=0, tiled=True),
        lax.psum_scatter(grad_terms[4], "fsdp", scatter_dimension=0, tiled=True),
        lax.psum_scatter(grad_terms[5], "fsdp", scatter_dimension=0, tiled=True),
        lax.psum_scatter(grad_terms[6], "fsdp", scatter_dimension=0, tiled=True),
        lax.psum_scatter(grad_terms[7], "fsdp", scatter_dimension=0, tiled=True),
        lax.psum_scatter(grad_terms[8], "fsdp", scatter_dimension=0, tiled=True),
        lax.psum_scatter(grad_terms[9], "fsdp", scatter_dimension=0, tiled=True),
        lax.psum_scatter(grad_terms[10], "fsdp", scatter_dimension=0, tiled=True),
        lax.psum_scatter(grad_terms[11], "fsdp", scatter_dimension=0, tiled=True),
    )
    return (
        lax.psum(shard_sums[0].astype(jnp.bfloat16), "ctx").astype(jnp.float32),
        lax.psum(shard_sums[1].astype(jnp.bfloat16), "ctx").astype(jnp.float32),
        lax.psum(shard_sums[2].astype(jnp.bfloat16), "ctx").astype(jnp.float32),
        lax.psum(shard_sums[3].astype(jnp.bfloat16), "ctx").astype(jnp.float32),
        lax.psum(shard_sums[4].astype(jnp.bfloat16), "ctx").astype(jnp.float32),
        lax.psum(shard_sums[5].astype(jnp.bfloat16), "ctx").astype(jnp.float32),
        lax.psum(shard_sums[6].astype(jnp.bfloat16), "ctx").astype(jnp.float32),
        lax.psum(shard_sums[7].astype(jnp.bfloat16), "ctx").astype(jnp.float32),
        lax.psum(shard_sums[8].astype(jnp.bfloat16), "ctx").astype(jnp.float32),
        lax.psum(shard_sums[9].astype(jnp.bfloat16), "ctx").astype(jnp.float32),
        lax.psum(shard_sums[10].astype(jnp.bfloat16), "ctx").astype(jnp.float32),
        lax.psum(shard_sums[11].astype(jnp.bfloat16), "ctx").astype(jnp.float32),
    )


def per_device_plain(
    tokens_in,
    out_grad,
    seq_lengths,
    order,
    w_qkv,
    bias_q,
    bias_v,
    w_out,
    bias_out,
    ln1_gain,
    ln1_bias,
    w_gate_up,
    w_down,
    bias_down,
    ln2_gain,
    ln2_bias,
):
    shards = (
        w_qkv,
        bias_q,
        bias_v,
        w_out,
        bias_out,
        ln1_gain,
        ln1_bias,
        w_gate_up,
        w_down,
        bias_down,
        ln2_gain,
        ln2_bias,
    )
    group_index = lax.axis_index("fsdp")
    ctx_index = lax.axis_index("ctx")
    dealt_tokens = jnp.take_along_axis(tokens_in, order[:, :, None, None], axis=1)
    tokens_grp, grads_grp = (
        lax.all_to_all(dealt_tokens, "fsdp", split_axis=1, concat_axis=2, tiled=True),
        lax.all_to_all(out_grad, "fsdp", split_axis=1, concat_axis=2, tiled=True),
    )
    dealt_lengths = jnp.take_along_axis(seq_lengths, order, axis=1)
    local_rows = tokens_grp.shape[2]
    key_place = jnp.arange(local_rows * lax.axis_size("ctx"))
    position = ctx_index * local_rows + jnp.arange(local_rows)
    slopes = jnp.array(slope_list(HEADS), jnp.float32)
    output_list = []
    input_list = []
    running = None
    for micro_batch in range(M):
        weights = fetch_weights(shards)
        (
            full_qkv,
            full_bias_q,
            full_bias_v,
            full_out,
            full_bias_out,
            full_ln1_gain,
            full_ln1_bias,
            full_gate_up,
            full_down,
            full_bias_down,
            full_ln2_gain,
            full_ln2_bias,
        ) = weights
        tokens = tokens_grp[micro_batch, 0]
        cotangent = grads_grp[micro_batch, 0]
        length = lax.dynamic_index_in_dim(
            dealt_lengths[micro_batch], group_index, 0, keepdims=False
        )
        valid_rows = position < length
        projected = plain_product(tokens, full_qkv)
        queries = (projected[:, :D] + full_bias_q.astype(jnp.float32)).astype(jnp.bfloat16)
        key_rows = projected[:, D : 2 * D].astype(jnp.bfloat16)
        values = (projected[:, 2 * D :] + full_bias_v.astype(jnp.float32)).astype(jnp.bfloat16)
        keys_all, values_all = (
            lax.all_gather(key_rows, "ctx", axis=0, tiled=True),
            lax.all_gather(values, "ctx", axis=0, tiled=True),
        )
        heads_q = queries.reshape(local_rows, HEADS, HEAD_DIM)
        heads_k = keys_all.reshape(-1, HEADS, HEAD_DIM)
        heads_v = values_all.reshape(-1, HEADS, HEAD_DIM)
        scores = masked_scores(heads_q, heads_k, position, key_place, length, slopes)
        row_max = jnp.max(scores, axis=-1, keepdims=True)
        exp_terms = jnp.exp(scores - row_max)
        row_total = jnp.sum(exp_terms, axis=-1, keepdims=True)
        log_total = row_max + jnp.log(row_total)
        attn_probs = (exp_terms / row_total).astype(jnp.bfloat16)
        context = (
            jnp.einsum("hqk,khd->qhd", attn_probs, heads_v, preferred_element_type=jnp.float32)
            .reshape(local_rows, D)
            .astype(jnp.bfloat16)
        )
        attn_out = plain_product(context, full_out) + full_bias_out.astype(jnp.float32)
        first_sum = tokens.astype(jnp.float32) + attn_out
        normed_one, norm_one_pull = jax.vjp(
            layer_norm,
            first_sum,
            full_ln1_gain.astype(jnp.float32),
            full_ln1_bias.astype(jnp.float32),
        )
        normed_low = normed_one.astype(jnp.bfloat16)
        gate_up = plain_product(normed_low, full_gate_up)
        hidden, gated_pull = jax.vjp(gated_unit, gate_up)
        hidden_low = hidden.astype(jnp.bfloat16)
        branch = plain_product(hidden_low, full_down) + full_bias_down.astype(jnp.float32)
        result, norm_two_pull = jax.vjp(
            layer_norm,
            normed_one + branch,
            full_ln2_gain.astype(jnp.float32),
            full_ln2_bias.astype(jnp.float32),
        )
        output_list.append(jnp.where(valid_rows[:, None], result, 0.0).astype(jnp.bfloat16))
        grad_result = jnp.where(valid_rows[:, None], cotangent.astype(jnp.float32), 0.0)
        grad_second, grad_ln2_gain, grad_ln2_bias = norm_two_pull(grad_result)
        grad_branch = grad_second.astype(jnp.bfloat16)
        grad_bias_down = jnp.sum(grad_branch.astype(jnp.float32), axis=0)
        grad_w_down = rows_product(hidden_low, grad_branch)
        grad_hidden = by_transpose(grad_branch, full_down)
        (grad_gate_up,) = gated_pull(grad_hidden)
        grad_gate_low = grad_gate_up.astype(jnp.bfloat16)
        grad_w_gate_up = rows_product(normed_low, grad_gate_low)
        grad_normed = grad_second + by_transpose(grad_gate_low, full_gate_up)
        grad_first, grad_ln1_gain, grad_ln1_bias = norm_one_pull(grad_normed)
        grad_attn = grad_first.astype(jnp.bfloat16)
        grad_bias_out = jnp.sum(grad_attn.astype(jnp.float32), axis=0)
        grad_w_out = rows_product(context, grad_attn)
        grad_context = (
            by_transpose(grad_attn, full_out)
            .astype(jnp.bfloat16)
            .reshape(local_rows, HEADS, HEAD_DIM)
        )
        scores = masked_scores(heads_q, heads_k, position, key_place, length, slopes)
        attn_exact = jnp.exp(scores - log_total)
        grad_values_term = jnp.einsum(
            "hqk,qhd->khd",
            attn_exact.astype(jnp.bfloat16),
            grad_context,
            preferred_element_type=jnp.float32,
        )
        grad_probs = jnp.einsum(
            "qhd,khd->hqk", grad_context, heads_v, preferred_element_type=jnp.float32
        )
        grad_scores = (
            attn_exact * (grad_probs - jnp.sum(attn_exact * grad_probs, axis=-1, keepdims=True))
        ).astype(jnp.bfloat16)
        grad_queries = (
            jnp.einsum("hqk,khd->qhd", grad_scores, heads_k, preferred_element_type=jnp.float32)
            * 0.125
        ).reshape(local_rows, D)
        grad_keys_term = (
            jnp.einsum("hqk,qhd->khd", grad_scores, heads_q, preferred_element_type=jnp.float32)
            * 0.125
        )
        grad_keys, grad_values = (
            lax.psum_scatter(
                grad_keys_term.reshape(-1, D).astype(jnp.bfloat16),
                "ctx",
                scatter_dimension=0,
                tiled=True,
            ).astype(jnp.float32),
            lax.psum_scatter(
                grad_values_term.reshape(-1, D).astype(jnp.bfloat16),
                "ctx",
                scatter_dimension=0,
                tiled=True,
            ).astype(jnp.float32),
        )
        grad_qkv = jnp.concatenate(
            [
                grad_queries.astype(jnp.bfloat16),
                grad_keys.astype(jnp.bfloat16),
                grad_values.astype(jnp.bfloat16),
            ],
            axis=1,
        )
        grad_w_qkv = rows_product(tokens, grad_qkv)
        grad_bias_q = jnp.sum(grad_qkv[:, :D].astype(jnp.float32), axis=0)
        grad_bias_v = jnp.sum(grad_qkv[:, 2 * D :].astype(jnp.float32), axis=0)
        grad_tokens = grad_first + by_transpose(grad_qkv, full_qkv)
        input_list.append(grad_tokens.astype(jnp.bfloat16))
        grad_terms = (
            grad_w_qkv,
            grad_bias_q,
            grad_bias_v,
            grad_w_out,
            grad_bias_out,
            grad_ln1_gain,
            grad_ln1_bias,
            grad_w_gate_up,
            grad_w_down,
            grad_bias_down,
            grad_ln2_gain,
            grad_ln2_bias,
        )
        reduced = reduce_grads(grad_terms)
        if micro_batch == 0:
            running = reduced
        else:
            running = tuple((left_sum + right_sum for left_sum, right_sum in zip(running, reduced)))
    output_stack = jnp.stack(output_list, axis=0)[:, None]
    input_stack = jnp.stack(input_list, axis=0)[:, None]
    output, dealt_grads = (
        lax.all_to_all(output_stack, "fsdp", split_axis=2, concat_axis=1, tiled=True),
        lax.all_to_all(input_stack, "fsdp", split_axis=2, concat_axis=1, tiled=True),
    )
    inverse = jnp.argsort(order, axis=1)
    input_grad = jnp.take_along_axis(dealt_grads, inverse[:, :, None, None], axis=1)
    return (
        output,
        input_grad,
        running[0],
        running[1],
        running[2],
        running[3],
        running[4],
        running[5],
        running[6],
        running[7],
        running[8],
        running[9],
        running[10],
        running[11],
    )


PIECES = 16
RING = 4


def whole(p, w=256):
    return [(p, 0, D, w)]


def halves(p, w=128):
    return [(p, 384 * i, 384, w) for i in range(2)]


GATHER_UNITS = sum([whole(p, 384 if p in (6, 10) else 256) for p in range(PIECES)], [])
SCATTER_UNITS = sum([whole(p, 256 if i % 3 else 128) for i, p in enumerate([*range(4, 16), 3, 0, 1, 2])], [])
STAGES = ()
AHEAD = 0
ROW_AT = 4
PLANE_AT = 6
CORE_AT = 8
X_AT = (0, 7)
G_AT = (7, 9)
O_AT = (0, 8)
O_FIRST = True
D_AT = (13, 7)


def mm(a, b):
    return jnp.dot(a, b, preferred_element_type=F32)


def mm_nt(a, b):
    return lax.dot_general(a, b, (((1,), (1,)), ((), ())), preferred_element_type=F32)


def mm_tn(a, b):
    return lax.dot_general(a, b, (((0,), (0,)), ((), ())), preferred_element_type=F32)


def block(i, size):
    if isinstance(i, int):
        return pl.ds(i * size, size)
    return pl.ds(pl.multiple_of(i * size, size), size)


class Place:
    def __init__(self, fsdp):
        self.fsdp = fsdp
        self.total = 2 * fsdp
        self.Z = fsdp // 4
        self.x = lax.axis_index("ctx")
        self.f = lax.axis_index("fsdp")
        self.z = self.f // 4
        self.y = lax.rem(self.f // 2, 2)
        self.c = lax.rem(self.f, 2)
        self.me = self.x * fsdp + self.f
        self.pending = []

    def dev(self, x=None, z=None, y=None, c=None):
        x = self.x if x is None else x
        z = self.z if z is None else z
        y = self.y if y is None else y
        c = self.c if c is None else c
        return (x, z * 4 + y * 2 + c)

    def cols(self, unit):
        p, lo, n, w = unit
        return pl.ds(pl.multiple_of(lo + self.x * w, 128), n - w)

    def give(self, unit):
        p, lo, n, w = unit
        return pl.ds(pl.multiple_of(lo + self.x * (n - w), 128), w)

    def take(self, unit):
        p, lo, n, w = unit
        return pl.ds(pl.multiple_of(lo + (1 - self.x) * (n - w), 128), w)

    def at(self, d):
        return (d // self.fsdp, lax.rem(d, self.fsdp))

    def signal(self):
        sem = pltpu.get_barrier_semaphore()

        @pl.loop(1, self.total)
        def _(k):
            d = lax.rem(self.me + k, self.total)
            pl.semaphore_signal(sem, inc=1, device_id=self.at(d), device_id_type=MESH)

    def wait(self):
        pl.semaphore_wait(pltpu.get_barrier_semaphore(), self.total - 1)

    def go(self, copy, cond=None):
        if cond is None:
            copy.start()
        else:
            pl.when(cond)(copy.start)
        self.pending.append((cond, copy))

    def finish(self):
        for cond, copy in self.pending:
            if cond is None:
                copy.wait_send()
            else:
                pl.when(cond)(copy.wait_send)
        self.pending = []


def remote(src, dst, send, recv, device):
    return pltpu.make_async_remote_copy(
        src_ref=src, dst_ref=dst, send_sem=send, recv_sem=recv, device_id=device, device_id_type=MESH
    )


class Exchange:
    def __init__(self, pc, src, dst, sems, k):
        self.pc, self.src, self.dst = pc, src, dst
        self.send, self.recv, self.local = sems[0].at[k], sems[1].at[k], sems[2].at[k]

    def own(self):
        return pltpu.make_async_copy(self.src.at[self.pc.me], self.dst.at[self.pc.me], self.local)

    def start(self, turn=0, turns=1):
        pc = self.pc
        if turn == 0:
            self.own().start()
        near = [(x, 0, y, c) for x in range(2) for y in range(2) for c in range(2) if x + y + c]
        far = [(x, z, y, c) for x in range(2) for y in range(2) for c in range(2) for z in (2, 3, 1)]
        if turns > 1:
            per = -(-len(far) // (turns - 1))
            picked = far[(turn - 1) * per : turn * per] if turn else near
        else:
            picked = near + far
        for x, z, y, c in picked:
            to = pc.dev(
                x=(1 - pc.x) if x else None,
                y=(1 - pc.y) if y else None,
                c=(1 - pc.c) if c else None,
                z=(None, pc.z + 1 - 2 * lax.rem(pc.z, 2), lax.rem(pc.z + 2, 4), 3 - pc.z)[z],
            )
            d = to[0] * pc.fsdp + to[1]
            remote(self.src.at[d], self.dst.at[pc.me], self.send, self.recv, to).start()

    def whole(self):
        blocks = pl.ds(0, self.pc.total - 1)
        return remote(self.src.at[blocks], self.dst.at[blocks], self.send, self.recv, self.pc.dev(c=1 - self.pc.c))

    def wait(self):
        self.own().wait()
        self.whole().wait_recv()

    def done(self):
        self.whole().wait_send()


class Gather:
    def __init__(self, pc, own, slots, sems):
        self.pc, self.own = pc, own
        self.place = slots
        self.zs, self.zr, self.ys, self.yr, self.xs, self.xr, self.cs, self.cr, self.ls = sems

    @staticmethod
    def sems(Z):
        T = pltpu.SemaphoreType.DMA
        n = len(GATHER_UNITS)
        return [
            T((n, 2 * Z - 2)), T((n, 2 * Z - 2)), T((n, 2 * Z - 1)), T((n,)),
            T((n, 2 * Z - 1)), T((n, 2 * Z - 1)), T((n, 2)), T((n, 2)), T((n,)),
        ]

    def up(self):
        return jnp.minimum(self.pc.z + 1, self.pc.Z - 1)

    def down(self):
        return jnp.maximum(self.pc.z - 1, 0)

    def slots(self, u, z, y, cols):
        return self.place(GATHER_UNITS[u][0], z, y, self.pc.c, cols)

    def cols(self, u):
        return self.pc.cols(GATHER_UNITS[u])

    def mine(self, u):
        pc = self.pc
        p, lo, n, w = GATHER_UNITS[u]
        return pltpu.make_async_copy(self.own(p, pl.ds(lo, n)), self.slots(u, pc.z, pc.y, pl.ds(lo, n)), self.ls.at[u])

    def start(self, u):
        pc = self.pc
        Z = pc.Z
        src = self.own(GATHER_UNITS[u][0], self.cols(u))
        dst = self.slots(u, pc.z, pc.y, self.cols(u))
        self.mine(u).start()
        pc.go(remote(src, dst, self.zs.at[u, 0], self.zr.at[u, 0], pc.dev(z=self.up())), pc.z < Z - 1)
        k = Z - 1
        pc.go(remote(src, dst, self.zs.at[u, k], self.zr.at[u, k], pc.dev(z=self.down())), pc.z > 0)
        pc.go(remote(src, dst, self.ys.at[u, 0], self.yr.at[u], pc.dev(y=1 - pc.y)))

    def hops(self, h):
        pc = self.pc
        Z = pc.Z
        return (
            (jnp.maximum(pc.z - h, 0), pc.z >= h, pc.z < Z - 1, self.up(), h - 1),
            (jnp.minimum(pc.z + h, Z - 1), pc.z + h < Z, pc.z > 0, self.down(), Z + h - 2),
        )

    def hop(self, u, h):
        pc = self.pc
        for z, here, onward, to, k in self.hops(h):
            ref = self.slots(u, z, pc.y, self.cols(u))
            pl.when(here)(remote(ref, ref, self.zs.at[u, k], self.zr.at[u, k], pc.dev(z=to)).wait_recv)
            if h < pc.Z - 1:
                pc.go(
                    remote(ref, ref, self.zs.at[u, k + 1], self.zr.at[u, k + 1], pc.dev(z=to)),
                    jnp.logical_and(here, onward),
                )
            pc.go(remote(ref, ref, self.ys.at[u, 1 + k], self.yr.at[u], pc.dev(y=1 - pc.y)), here)
            if GATHER_UNITS[u][3]:
                ref = self.slots(u, z, pc.y, pc.give(GATHER_UNITS[u]))
                pc.go(remote(ref, ref, self.xs.at[u, k], self.xr.at[u, k], pc.dev(x=1 - pc.x)), here)

    def row(self, u):
        pc = self.pc
        unit = GATHER_UNITS[u]
        ref = self.slots(u, slice(None), 1 - pc.y, self.cols(u))
        remote(ref, ref, self.ys.at[u, 0], self.yr.at[u], pc.dev(y=1 - pc.y)).wait_recv()
        if unit[3]:
            k = 2 * pc.Z - 2
            ref = self.slots(u, slice(None), 1 - pc.y, pc.give(unit))
            pc.go(remote(ref, ref, self.xs.at[u, k], self.xr.at[u, k], pc.dev(x=1 - pc.x)))
        self.mine(u).wait()
        ref = self.slots(u, slice(None), slice(None), self.cols(u))
        pc.go(remote(ref, ref, self.cs.at[u, 0], self.cr.at[u, 0], pc.dev(c=1 - pc.c)))

    def plane(self, u):
        pc = self.pc
        unit = GATHER_UNITS[u]
        if not unit[3]:
            return
        take = pc.take(unit)
        for h in range(1, pc.Z):
            for z, here, onward, to, k in self.hops(h):
                ref = self.slots(u, z, pc.y, take)
                pl.when(here)(remote(ref, ref, self.xs.at[u, k], self.xr.at[u, k], pc.dev(x=1 - pc.x)).wait_recv)
        k = 2 * pc.Z - 2
        ref = self.slots(u, slice(None), 1 - pc.y, take)
        remote(ref, ref, self.xs.at[u, k], self.xr.at[u, k], pc.dev(x=1 - pc.x)).wait_recv()
        ref = self.slots(u, slice(None), slice(None), take)
        pc.go(remote(ref, ref, self.cs.at[u, 1], self.cr.at[u, 1], pc.dev(c=1 - pc.c)))

    def core(self, u):
        pc = self.pc
        parts = [pc.cols(GATHER_UNITS[u])] + ([pc.take(GATHER_UNITS[u])] if GATHER_UNITS[u][3] else [])
        for k, cols in enumerate(parts):
            ref = self.place(GATHER_UNITS[u][0], slice(None), slice(None), 1 - pc.c, cols)
            remote(ref, ref, self.cs.at[u, k], self.cr.at[u, k], pc.dev(c=1 - pc.c)).wait_recv()


class Scatter:
    def __init__(self, pc, terms, get, put, from_c, from_x, from_y, from_z, from_f, sems):
        self.pc, self.terms, self.get, self.put = pc, terms, get, put
        self.from_c, self.from_x, self.from_y, self.from_z, self.from_f = from_c, from_x, from_y, from_z, from_f
        self.cs, self.cr, self.xs, self.xr, self.ys, self.yr, self.zs, self.zr, self.fs, self.fr, self.free = sems
        z = pc.z
        self.inner = jnp.logical_or(z == 1, z == 2)
        self.outer = jnp.logical_not(self.inner)
        self.mate = z + 1 - 2 * lax.rem(z, 2)
        self.far_in = jnp.where(z < 2, 2, 1)
        self.far_out = jnp.where(z < 2, 3, 0)
        self.x_lo, self.y_lo = [], []
        used = {}
        for p, lo, n, w in SCATTER_UNITS:
            a, b = used.get(p, (0, 0))
            self.x_lo.append(a)
            self.y_lo.append(b)
            used[p] = (a + w, b + n - w)

    @staticmethod
    def sems():
        T = pltpu.SemaphoreType.DMA
        n = len(SCATTER_UNITS)
        return [
            T((n,)), T((n,)), T((n,)), T((n,)), T((n,)), T((n,)), T((n, 5)), T((n, 4)), T((n,)), T((n,)),
            pltpu.SemaphoreType.REGULAR((n,)),
        ]

    @staticmethod
    def buffers(Z, rows):
        n = PIECES
        give, win = [0] * n, [0] * n
        for p, lo, k, w in SCATTER_UNITS:
            give[p] += w
            win[p] += k - w
        give, win = max(give), max(win)
        return [
            pltpu.VMEM((RING, Z, 2, rows, D), BF),
            pltpu.VMEM((n, Z, 2, rows, give), BF),
            pltpu.VMEM((n, Z, rows, win), BF),
            pltpu.VMEM((n, 4, rows, win), BF),
            pltpu.VMEM((n, rows, win), BF),
        ]

    def x_at(self, u):
        return pl.ds(self.x_lo[u], SCATTER_UNITS[u][3])

    def y_at(self, u):
        p, lo, n, w = SCATTER_UNITS[u]
        return pl.ds(self.y_lo[u], n - w)

    def add(self, u, z, y, cols, value):
        p = SCATTER_UNITS[u][0]
        c = self.pc.c
        self.put(p, z, y, c, cols, self.get(p, z, y, c, cols) + value)

    def part(self, u, z, y, cols):
        return self.terms(SCATTER_UNITS[u][0], z, y, self.pc.c, cols)

    def start(self, u):
        pc = self.pc
        p, lo, n, w = SCATTER_UNITS[u]
        if u >= RING:
            pl.semaphore_wait(self.free.at[u], 1)
        src = self.terms(p, slice(None), slice(None), 1 - pc.c, pl.ds(lo, n))
        dst = self.from_c.at[u % RING, :, :, :, pl.ds(0, n)]
        pc.go(remote(src, dst, self.cs.at[u], self.cr.at[u], pc.dev(c=1 - pc.c)))

    def core(self, u):
        pc = self.pc
        p, lo, n, w = SCATTER_UNITS[u]
        ref = self.from_c.at[u % RING, :, :, :, pl.ds(0, n)]
        remote(ref, ref, self.cs.at[u], self.cr.at[u], pc.dev(c=1 - pc.c)).wait_recv()
        for z in range(pc.Z):
            for y in range(2):
                self.add(u, z, y, pl.ds(lo, n), self.from_c[u % RING, z, y, :, pl.ds(0, n)])
        if u + RING < len(SCATTER_UNITS):
            pl.semaphore_signal(self.free.at[u + RING], inc=1, device_id=pc.dev(c=1 - pc.c), device_id_type=MESH)
        if w:
            src = self.part(u, slice(None), slice(None), pc.take(SCATTER_UNITS[u]))
            dst = self.from_x.at[p, :, :, :, self.x_at(u)]
            pc.go(remote(src, dst, self.xs.at[u], self.xr.at[u], pc.dev(x=1 - pc.x)))
        else:
            self.across(u)

    def plane(self, u):
        pc = self.pc
        p, lo, n, w = SCATTER_UNITS[u]
        if w:
            ref = self.from_x.at[p, :, :, :, self.x_at(u)]
            remote(ref, ref, self.xs.at[u], self.xr.at[u], pc.dev(x=1 - pc.x)).wait_recv()
            for z in range(pc.Z):
                for y in range(2):
                    self.add(u, z, y, pc.give(SCATTER_UNITS[u]), self.from_x[p, z, y, :, self.x_at(u)])
            self.across(u)

    def across(self, u):
        pc = self.pc
        src = self.part(u, slice(None), 1 - pc.y, pc.cols(SCATTER_UNITS[u]))
        dst = self.from_y.at[SCATTER_UNITS[u][0], :, :, self.y_at(u)]
        pc.go(remote(src, dst, self.ys.at[u], self.yr.at[u], pc.dev(y=1 - pc.y)))

    def z_ref(self, u, k):
        return self.from_z.at[SCATTER_UNITS[u][0], k, :, self.y_at(u)]

    def z_add(self, u, k, z):
        ref = self.z_ref(u, k)
        remote(ref, ref, self.zs.at[u, k], self.zr.at[u, k], self.pc.dev(z=self.mate)).wait_recv()
        value = self.from_z[SCATTER_UNITS[u][0], k, :, self.y_at(u)]
        self.add(u, z, self.pc.y, self.pc.cols(SCATTER_UNITS[u]), value)

    def row(self, u):
        pc = self.pc
        p = SCATTER_UNITS[u][0]
        cols = pc.cols(SCATTER_UNITS[u])
        ref = self.from_y.at[p, :, :, self.y_at(u)]
        remote(ref, ref, self.ys.at[u], self.yr.at[u], pc.dev(y=1 - pc.y)).wait_recv()
        for z in range(pc.Z):
            self.add(u, z, pc.y, cols, self.from_y[p, z, :, self.y_at(u)])
        for k, z in enumerate((self.mate, self.far_in, self.far_out)):
            copy = remote(
                self.part(u, z, pc.y, cols), self.z_ref(u, k), self.zs.at[u, k], self.zr.at[u, k], pc.dev(z=self.mate)
            )
            pc.go(copy, self.outer if k else None)

    def middle(self, u):
        pc = self.pc
        cols = pc.cols(SCATTER_UNITS[u])
        far = ((1, self.far_in), (2, self.far_out))

        @pl.when(self.inner)
        def _():
            for k, z in far:
                self.z_add(u, k, z)

        for k, z in far:
            src = self.part(u, z, pc.y, cols)
            pc.go(remote(src, self.z_ref(u, 3), self.zs.at[u, 2 + k], self.zr.at[u, 3], pc.dev(z=z)), self.inner)

    def f_ref(self, u):
        return self.from_f.at[SCATTER_UNITS[u][0], :, self.y_at(u)]

    def line(self, u):
        pc = self.pc
        for k in (0, 3):
            self.z_add(u, k, pc.z)
        src = self.part(u, pc.z, pc.y, pc.cols(SCATTER_UNITS[u]))
        pc.go(remote(src, self.f_ref(u), self.fs.at[u], self.fr.at[u], pc.dev(x=1 - pc.x)))

    def last(self, u, out):
        pc = self.pc
        unit = p, lo, n, w = SCATTER_UNITS[u]
        ref = self.f_ref(u)
        remote(ref, ref, self.fs.at[u], self.fr.at[u], pc.dev(x=1 - pc.x)).wait_recv()
        at = self.y_lo[u]

        def own(cols):
            return self.get(p, pc.z, pc.y, pc.c, cols).astype(F32)

        if w:
            out[:, pc.give(unit)] = own(pc.give(unit))
            theirs = pl.ds(pl.multiple_of(at + (1 - pc.x) * (n - 2 * w), 128), w)
            out[:, pc.take(unit)] = self.from_f[p, :, theirs].astype(F32)
        if n > 2 * w:
            both = pl.ds(pl.multiple_of(at + pc.x * w, 128), n - 2 * w)
            shared = pl.ds(lo + w, n - 2 * w)
            out[:, shared] = own(shared) + self.from_f[p, :, both].astype(F32)


def row_mean(v):
    return jnp.sum(v, axis=-1, keepdims=True) * (1.0 / D)


BQ, BV, BO, G1, B1, BD, G2, B2 = range(8)


def layer_kernel(
    fsdp, rows,
    order, lengths, slopes, tokens_in, grads_in, *refs,
):
    small_in, (wq_in, wo_in, wg_in, wd_in) = refs[:8], refs[8:12]
    OUT, DX, GQ, GW, GG, GD, SMALLG, *refs = refs[12:]
    (
    wa, wd, raw, outv, xs, gs, small, small_own, smallf, qkv, dist, lse, ctxt, y1, y1b, xhat, rstd, act, slope_up, zed, acc, dfb, tr,
    dxr, sgrad, sparts, gsum, from_c, from_x, from_y, from_z, from_f, *sems,
    ) = refs
    pc = Place(fsdp)
    Z = pc.Z
    L = pc.total * raw.shape[1]
    gsems, ssems, esems, rsem = sems[:9], sems[9:20], sems[20:23], sems[23]
    w_pc = wa.shape[1:]

    def own(p, cols):
        if p < 3:
            return wq_in.at[:, pl.ds(pl.multiple_of(D * p + cols.start, 128), cols.size)]
        if p == 3:
            return wo_in.at[:, cols]
        if p < 12:
            i, j = (p - 4) // 2, (p - 4) % 2
            return wg_in.at[:, pl.ds(pl.multiple_of(FF * j + D * i + cols.start, 128), cols.size)]
        return wd_in.at[pl.ds(rows * (p - 12), rows), cols]

    def slots(p, z, y, c, cols):
        if p < 12:
            return wa.at[p, z, y, c, :, cols]
        return wd.at[z, y, c, p - 12, :, cols]

    def get(p, z, y, c, cols):
        if p < 12:
            return wa[p, z, y, c, :, cols]
        return wd[z, y, c, p - 12, :, cols]

    def put(p, z, y, c, cols, value):
        if p < 12:
            wa[p, z, y, c, :, cols] = value
        else:
            wd[z, y, c, p - 12, :, cols] = value

    def out_of(p):
        if p >= 12:
            return GD.at[pl.ds(rows * (p - 12), rows)]
        if p == 3:
            return GW
        if p < 3:
            return GQ.at[:, pl.ds(D * p, D)]
        i, j = (p - 4) // 2, (p - 4) % 2
        return GG.at[:, pl.ds(FF * j + D * i, D)]

    def w_cols(p, cols):
        return wa[p, :, :, :, :, cols].reshape(D, cols.size)

    def w_all(p):
        return wa[p].reshape(D, D)

    g = Gather(pc, own, slots, gsems)
    sc = Scatter(pc, slots, get, put, from_c, from_x, from_y, from_z, from_f, ssems)
    ex_x = Exchange(pc, outv, xs, esems, 0)
    ex_g = Exchange(pc, grads_in, gs, esems, 1)
    ex_o = Exchange(pc, outv, OUT, esems, 3)
    ex_d = Exchange(pc, raw, dxr, esems, 4)
    ex_s = Exchange(pc, sparts, gsum, esems, 5)
    len_s = lengths[pc.x, order[pc.x, pc.f]]

    def tokens(r):
        n = r.size // 16
        return xs[pl.ds(r.start // 16, n)].reshape(r.size, D)

    def deal():
        @pl.loop(0, pc.total)
        def _(d):
            m = d // fsdp
            outv[d] = raw[m * fsdp + order[m, lax.rem(d, fsdp)]]

    def prepare():
        k = lax.broadcasted_iota(jnp.int32, (L, L), 0)
        q = lax.broadcasted_iota(jnp.int32, (L, L), 1)
        dist[...] = jnp.where(k < len_s, jnp.abs(k - q).astype(F32), -NEGATIVE)

    def place_small():
        for f in range(fsdp):
            smallf[:, pl.ds(f * rows, rows)] = small[f, :, pl.ds(0, rows)]

    def project(p):
        @pl.loop(0, D // 256)
        def _(t):
            cols = block(t, 256)
            r = mm(xs[...].reshape(L, D), w_cols(p, cols))
            if p != 1:
                r = r + smallf[pl.ds(BQ if p == 0 else BV, 1), cols]
            qkv[p, :, cols] = r.astype(BF)

    def attend(j):
        cols = block(j, 128)
        lane = lax.broadcasted_iota(jnp.int32, (L, 128), 1)
        q2, k2 = qkv[0, :, cols], qkv[1, :, cols]
        vt = qkv[2, :, cols].T
        for q in range(L // 256):
            qr = pl.ds(256 * q, 256)
            parts = []
            for s in range(2):
                qm = jnp.where((lane < 64) if s == 0 else (lane >= 64), q2, jnp.zeros_like(q2))
                st = mm_nt(k2, qm[256 * q : 256 * q + 256])
                st = st * (0.125 * LOG2E) - dist[:, qr] * slopes[2 * j + s]
                top = jnp.max(st, axis=0, keepdims=True)
                e = jnp.exp2(st - top)
                total = jnp.sum(e, axis=0, keepdims=True)
                lse[2 * j + s, :, qr] = top + jnp.log2(total)
                pr = (e * (1.0 / total)).astype(BF)
                parts.append(mm(vt[64 * s : 64 * s + 64], pr))
            ctxt[qr, cols] = jnp.concatenate(parts, axis=0).T.astype(BF)

    def first_sum():
        @pl.loop(0, D // 256)
        def _(t):
            cols = block(t, 256)
            acc[:, cols] = mm(ctxt[...], w_cols(3, cols)) + smallf[pl.ds(BO, 1), cols]

    def first_norm():
        @pl.loop(0, L // 64)
        def _(i):
            r = block(i, 64)
            h = acc[r, :] + tokens(r).astype(F32)
            centre = h - row_mean(h)
            rs = lax.rsqrt(row_mean(centre * centre) + EPSILON)
            xh = centre * rs
            xhat[r, :] = xh
            rstd[r, :] = jnp.broadcast_to(rs, (64, 128))
            yy = xh * smallf[pl.ds(G1, 1), :] + smallf[pl.ds(B1, 1), :]
            y1[r, :] = yy
            y1b[r, :] = yy.astype(BF)

        tr[...] = y1b[...].T

    def gated(i):
        for s in range(D // 256):
            gated_part(i, s)

    def gated_part(i, s):
        wc = block(s, 256)
        cols = block(i * 3 + s, 256)
        a = mm(y1b[...], w_cols(4 + 2 * i, wc))
        u = mm(y1b[...], w_cols(5 + 2 * i, wc))
        cdf = 0.5 + 0.5 * lax.erf(a * math.sqrt(0.5))
        pdf = jnp.exp2(a * a * (-0.5 * LOG2E)) * (1.0 / math.sqrt(2.0 * math.pi))
        gelu = a * cdf
        zed[:, cols] = (gelu * u).astype(BF)
        act[:, cols] = gelu.astype(BF)
        slope_up[:, cols] = (u * (cdf + a * pdf)).astype(BF)

    def second_norm():
        @pl.loop(0, D // 256)
        def _(t):
            cols = block(t, 256)
            w = wd[:, :, :, :, :, cols].reshape(FF, 256)
            acc[:, cols] = mm(zed[...], w) + smallf[pl.ds(BD, 1), cols]

        def step(i, sums):
            r = block(i, 64)
            h = acc[r, :] + y1[r, :]
            centre = h - row_mean(h)
            rs = lax.rsqrt(row_mean(centre * centre) + EPSILON)
            xh = centre * rs
            gain = smallf[pl.ds(G2, 1), :]
            valid = (lax.broadcasted_iota(jnp.int32, (64, D), 0) + i * 64) < len_s
            res = jnp.where(valid, xh * gain + smallf[pl.ds(B2, 1), :], 0.0).astype(BF)
            outv[pl.ds(i * 4, 4)] = res.reshape(4, 16, D)
            up = jnp.where(valid, gs[pl.ds(i * 4, 4)].reshape(64, D).astype(F32), 0.0)
            dx = up * gain
            dh = rs * (dx - row_mean(dx) - xh * row_mean(dx * xh))
            low = dh.astype(BF)
            acc[r, :] = dh
            dfb[r, :] = low
            sg, sb, sd = sums
            return (
                sg + jnp.sum(up * xh, axis=0, keepdims=True),
                sb + jnp.sum(up, axis=0, keepdims=True),
                sd + jnp.sum(low.astype(F32), axis=0, keepdims=True),
            )

        zero = jnp.zeros((1, D), F32)
        sg, sb, sd = lax.fori_loop(0, L // 64, step, (zero, zero, zero))
        sgrad[pl.ds(G2, 1), :] = sg
        sgrad[pl.ds(B2, 1), :] = sb
        sgrad[pl.ds(BD, 1), :] = sd

    def ff_back(i):
        cols = block(i, D)
        dz = mm_nt(dfb[...], wd[pl.ds(i * Z // 4, Z // 4)].reshape(D, D))
        dgate = (dz * slope_up[:, cols].astype(F32)).astype(BF)
        dup = (dz * act[:, cols].astype(F32)).astype(BF)
        act[:, cols] = dup
        acc[...] += mm_nt(dgate, w_all(4 + 2 * i)) + mm_nt(dup, w_all(5 + 2 * i))
        wa[4 + 2 * i] = mm(tr[...], dgate).astype(BF).reshape(w_pc)

    def ff_back_rest(i):
        cols = block(i, D)
        wa[5 + 2 * i] = mm(tr[...], act[:, cols]).astype(BF).reshape(w_pc)
        wd[pl.ds(i * Z // 4, Z // 4)] = mm_tn(zed[:, cols], dfb[...]).astype(BF).reshape((Z // 4,) + wd.shape[1:])

    def first_norm_back():
        def step(i, sums):
            r = block(i, 64)
            up = acc[r, :]
            xh = xhat[r, :]
            dx = up * smallf[pl.ds(G1, 1), :]
            dh = rstd[r, :][:, :1] * (dx - row_mean(dx) - xh * row_mean(dx * xh))
            low = dh.astype(BF)
            xhat[r, :] = dh
            dfb[r, :] = low
            sg, sb, sd = sums
            return (
                sg + jnp.sum(up * xh, axis=0, keepdims=True),
                sb + jnp.sum(up, axis=0, keepdims=True),
                sd + jnp.sum(low.astype(F32), axis=0, keepdims=True),
            )

        zero = jnp.zeros((1, D), F32)
        sg, sb, sd = lax.fori_loop(0, L // 64, step, (zero, zero, zero))
        sgrad[pl.ds(G1, 1), :] = sg
        sgrad[pl.ds(B1, 1), :] = sb
        sgrad[pl.ds(BO, 1), :] = sd

    def out_back():
        y1b[...] = mm_nt(dfb[...], w_all(3)).astype(BF)
        wa[3] = mm_tn(ctxt[...], dfb[...]).astype(BF).reshape(w_pc)

    def dqkv(p):
        return act.at[:, pl.ds(D * p, D)]

    def attend_back(j):
        cols = block(j, 128)
        lane = lax.broadcasted_iota(jnp.int32, (L, 128), 1)
        q2, k2, v2 = (qkv[i, :, cols] for i in range(3))
        do2 = y1b[:, cols]
        kt = k2.T
        dv = dk = None
        for q in range(L // 256):
            qr = pl.ds(256 * q, 256)
            qs = slice(256 * q, 256 * q + 256)
            parts = []
            for s in range(2):
                half = (lane < 64) if s == 0 else (lane >= 64)
                qm = jnp.where(half, q2, jnp.zeros_like(q2))[qs]
                dm = jnp.where(half, do2, jnp.zeros_like(do2))[qs]
                st = mm_nt(k2, qm) * (0.125 * LOG2E) - dist[:, qr] * slopes[2 * j + s]
                pr = jnp.exp2(st - lse[2 * j + s, :, qr])
                dp = mm_nt(v2, dm)
                ds = (pr * (dp - jnp.sum(pr * dp, axis=0, keepdims=True))).astype(BF)
                a, b = mm(pr.astype(BF), dm), mm(ds, qm)
                dv = a if dv is None else dv + a
                dk = b if dk is None else dk + b
                parts.append(mm(kt[64 * s : 64 * s + 64], ds))
            dqkv(0)[qr, cols] = (jnp.concatenate(parts, axis=0).T * 0.125).astype(BF)
        dqkv(1)[:, cols] = (dk * 0.125).astype(BF)
        dqkv(2)[:, cols] = dv.astype(BF)

    def weights_back(p):
        x = xs[...].reshape(L, D)
        d = dqkv(p)
        wa[p] = mm_tn(x, d[...]).astype(BF).reshape(w_pc)
        if p != 1:
            r = BQ if p == 0 else BV
            sgrad[pl.ds(r, 1), :] = jnp.sum(d[...].astype(F32), axis=0, keepdims=True)

    def tokens_back():
        @pl.loop(0, L // 128)
        def _(i):
            r = block(i, 128)
            v = xhat[r, :]
            for p in range(3):
                v = v + mm_nt(dqkv(p)[r, :], w_all(p))
            raw[pl.ds(i * 8, 8)] = v.astype(BF).reshape(8, 16, D)

    def split_small():
        sparts[...] = jnp.zeros_like(sparts)
        for d in range(pc.total):
            at = d % fsdp * rows
            sparts[d, :, pl.ds(0, rows)] = sgrad[:, pl.ds(at, rows)]

    def undeal():
        @pl.loop(0, pc.total)
        def _(k):
            m, n = k // fsdp, lax.rem(k, fsdp)

            def find(f, at):
                return jnp.where(order[m, f] == n, f, at)

            DX[k] = dxr[m * fsdp + lax.fori_loop(0, fsdp, find, 0)]

    def spread(ex, t, at):
        first, count = at
        if first <= t < first + count:
            ex.start(t - first, count)

    take_raw = pltpu.make_async_copy(tokens_in, raw, rsem)
    take_raw.start()
    pc.signal()
    small_own[...] = jnp.zeros_like(small_own)
    for i, ref in enumerate(small_in):
        small_own[pl.ds(i, 1), pl.ds(0, rows)] = ref[...].astype(F32)
    prepare()
    take_raw.wait()
    deal()
    pc.wait()

    me_small = small.at[pc.f]
    keep_small = pltpu.make_async_copy(small_own, me_small, esems[2].at[2])
    keep_small.start()

    @pl.loop(1, fsdp)
    def _(k):
        f = lax.rem(pc.f + k, fsdp)
        remote(small_own, me_small, esems[0].at[2], esems[1].at[2], (pc.x, f)).start()

    small_all = remote(
        small.at[pl.ds(0, fsdp - 1)], small.at[pl.ds(0, fsdp - 1)], esems[0].at[2], esems[1].at[2],
        pc.dev(c=1 - pc.c),
    )

    def begin():
        ex_x.wait()
        small_all.wait_recv()
        keep_small.wait()
        place_small()
        for p in range(3):
            project(p)

    tasks = [(2, begin)]
    tasks += [(2, functools.partial(attend, j)) for j in range(HEADS // 2)]
    tasks += [(3, first_sum), (3, first_norm)]
    tasks += [(5 + 2 * i, functools.partial(gated, i)) for i in range(FF // D)]
    there = -1

    units = len(GATHER_UNITS)
    finished = [max(u for u in range(units) if GATHER_UNITS[u][0] == p) for p in range(PIECES)]
    for t in range(units + CORE_AT):
        spread(ex_x, t, X_AT)
        spread(ex_g, t, G_AT)
        for u in range(units):
            if t == max(0, u - AHEAD):
                g.start(u)
        for h in range(1, Z):
            for u in range(units):
                if t == max(0, u - AHEAD) + h:
                    g.hop(u, h)
        if 0 <= t - ROW_AT < units:
            g.row(t - ROW_AT)
        if 0 <= t - PLANE_AT < units:
            g.plane(t - PLANE_AT)
        if 0 <= t - CORE_AT < units:
            u = t - CORE_AT
            g.core(u)
            there = max([p for p in range(PIECES) if finished[p] <= u], default=-1)
            left = units + CORE_AT - 1 - t
            if tasks and tasks[0][0] <= there:
                tasks.pop(0)[1]()
            while len(tasks) > left and tasks[0][0] <= there:
                tasks.pop(0)[1]()
    ex_g.wait()
    ex_x.done()
    second_norm()
    if O_FIRST:
        ex_o.start()
    pc.finish()

    units = len(SCATTER_UNITS)
    stages = STAGES if STAGES else (("core", 1), ("plane", 3), ("row", 5), ("middle", 6), ("line", 8), ("last", 10))
    for t in range(units + stages[-1][1]):
        if t < 8:
            (ff_back_rest if t % 2 else ff_back)(t // 2)
        if t == 8:
            first_norm_back()
            out_back()
        if 9 <= t < 12:
            pl.loop(2 * (t - 9), 2 * (t - 9) + 2)(attend_back)
        if t == 12:
            tokens_back()
            for p in range(3):
                weights_back(p)
            split_small()
            ex_s.start()
        if not O_FIRST:
            spread(ex_o, t, O_AT)
        spread(ex_d, t, D_AT)
        if t < units:
            sc.start(t)
        for name, off in stages:
            if 0 <= t - off < units:
                u = t - off
                if name == "last":
                    sc.last(u, out_of(SCATTER_UNITS[u][0]))
                else:
                    getattr(sc, name)(u)
    ex_s.wait()

    def add(i, v):
        return v + gsum[i]

    total = lax.fori_loop(1, pc.total, add, gsum[0])
    SMALLG[...] = total[:, :rows]
    ex_d.wait()
    undeal()
    ex_o.wait()
    for e in (ex_g, ex_o, ex_d, ex_s):
        e.done()
    small_all.wait_send()
    pc.finish()


def hand_over(*refs):
    src, small, dst, parts, through, sem = refs[:6], refs[6], refs[7:13], refs[13:21], refs[21:27], refs[27]
    take = [pltpu.make_async_copy(a, b, sem.at[0, k]) for k, (a, b) in enumerate(zip(src, through))]
    give = [pltpu.make_async_copy(a, b, sem.at[1, k]) for k, (a, b) in enumerate(zip(through, dst))]
    for c in take:
        c.start()
    for k, ref in enumerate(parts):
        ref[...] = small[pl.ds(k, 1), :]
    for a, b in zip(take, give):
        a.wait()
        b.start()
    for c in give:
        c.wait()


def per_device(
    tokens_in, out_grad, seq_lengths, order, w_qkv, bias_q, bias_v, w_out, bias_out, ln1_gain, ln1_bias, w_gate_up,
    w_down, bias_down, ln2_gain, ln2_bias,
):
    fsdp = lax.axis_size("fsdp")
    total = 2 * fsdp
    rows = w_out.shape[0]
    here = tokens_in.shape[2]
    L = here * total
    Z = fsdp // 4
    small = [v.reshape(1, rows) for v in (bias_q, bias_v, bias_out, ln1_gain, ln1_bias, bias_down, ln2_gain, ln2_bias)]
    slopes = jnp.array(slope_list(HEADS), F32) * LOG2E
    hbm = pl.BlockSpec(memory_space=pl.ANY)
    smem = pl.BlockSpec(memory_space=pltpu.SMEM)
    vmem = pl.BlockSpec(memory_space=pltpu.VMEM)
    S = jax.ShapeDtypeStruct
    T = pltpu.SemaphoreType.DMA
    V = pltpu.VMEM
    rows_of = (total, here, D)
    results = pl.pallas_call(
        functools.partial(layer_kernel, fsdp, rows),
        out_shape=[
            S(rows_of, BF), S(rows_of, BF), S((rows, 3 * D), F32), S((rows, D), F32), S((rows, 2 * FF), F32),
            S((4 * rows, D), F32), S((8, rows), F32),
        ],
        in_specs=[smem] * 3 + [hbm] * 2 + [vmem] * 8 + [hbm] * 4,
        out_specs=[hbm] + [vmem] * 6,
        scratch_shapes=[
            V((12, Z, 2, 2, rows, D), BF), V((Z, 2, 2, 4, rows, D), BF), V(rows_of, BF), V(rows_of, BF),
            V(rows_of, BF), V(rows_of, BF), V((fsdp, 8, 128), F32), V((8, 128), F32), V((8, D), F32), V((3, L, D), BF), V((L, L), F32),
            V((HEADS, 1, L), F32), V((L, D), BF), V((L, D), F32), V((L, D), BF), V((L, D), F32), V((L, 128), F32),
            V((L, FF), BF), V((L, FF), BF), V((L, FF), BF), V((L, D), F32), V((L, D), BF), V((D, L), BF),
            V(rows_of, BF), V((8, D), F32), V((total, 8, 128), F32), V((total, 8, 128), F32),
            *Scatter.buffers(Z, rows), *Gather.sems(Z), *Scatter.sems(), T((6,)), T((6,)), T((6,)), T,
        ],
        compiler_params=pltpu.CompilerParams(collective_id=0, has_side_effects=True, vmem_limit_bytes=VMEM_LIMIT),
        name="layer",
    )(order, seq_lengths, slopes, tokens_in.reshape(rows_of), out_grad.reshape(rows_of), *small, w_qkv, w_out, w_gate_up, w_down)
    output, input_grad, gq, gw, gg, gd, *mine = pl.pallas_call(
        hand_over,
        out_shape=[S(r.shape, r.dtype) for r in results[:6]] + [S((1, rows), F32)] * 8,
        in_specs=[hbm] * 6 + [vmem],
        out_specs=[hbm] * 6 + [vmem] * 8,
        scratch_shapes=[V(r.shape, r.dtype) for r in results[:6]] + [T((2, 6))],
        name="hand_over",
    )(*results)
    mine = [v.reshape(rows) for v in mine]
    return (
        output.reshape(tokens_in.shape), input_grad.reshape(tokens_in.shape), gq, mine[BQ], mine[BV], gw, mine[BO],
        mine[G1], mine[B1], gg, gd, mine[BD], mine[G2], mine[B2],
    )


def solution(mesh):
    fsdp = mesh.shape["fsdp"]
    rows = D // fsdp
    kernels = mesh.shape["ctx"] == M and fsdp == 16 and rows % 16 == 0
    return jax.shard_map(
        per_device if kernels else per_device_plain,
        mesh=mesh,
        in_specs=(
            P(None, None, ("ctx", "fsdp"), None),
            P(None, None, ("ctx", "fsdp"), None),
            P(),
            P(),
            P("fsdp", None),
            P("fsdp"),
            P("fsdp"),
            P("fsdp", None),
            P("fsdp"),
            P("fsdp"),
            P("fsdp"),
            P("fsdp", None),
            P("fsdp", None),
            P("fsdp"),
            P("fsdp"),
            P("fsdp"),
        ),
        out_specs=(
            P(None, None, ("ctx", "fsdp"), None),
            P(None, None, ("ctx", "fsdp"), None),
            P("fsdp", None),
            P("fsdp"),
            P("fsdp"),
            P("fsdp", None),
            P("fsdp"),
            P("fsdp"),
            P("fsdp"),
            P("fsdp", None),
            P("fsdp", None),
            P("fsdp"),
            P("fsdp"),
            P("fsdp"),
        ),
        check_vma=False,
    )
```

```python
import functools
import math

import jax
import jax.numpy as jnp
from jax import lax
from jax.experimental import pallas as pl
from jax.experimental.pallas import tpu as pltpu
from jax.sharding import PartitionSpec as P

D = 768
HEADS = 12
HEAD_DIM = 64
FF = 3072
M = 2
EPSILON = 1e-12
NEGATIVE = -1e30
MESH = pl.DeviceIdType.MESH
BF = jnp.bfloat16
F32 = jnp.float32
LOG2E = math.log2(math.e)
VMEM_LIMIT = 62 << 20


def slope_list(head_count):

    def powers(number):
        anchor = 2.0 ** (-(2.0 ** (-(math.log2(number) - 3))))
        return [anchor ** (power_index + 1) for power_index in range(number)]

    closest = 2 ** int(math.floor(math.log2(head_count)))
    return powers(closest) + powers(2 * closest)[0::2][: head_count - closest]


def layer_norm(inputs, gain_row, offset_row):
    centre = inputs - jnp.mean(inputs, axis=-1, keepdims=True)
    spread = jnp.mean(centre * centre, axis=-1, keepdims=True)
    return centre * lax.rsqrt(spread + EPSILON) * gain_row + offset_row


def gated_unit(gate_up):
    return jax.nn.gelu(gate_up[:, :FF], approximate=False) * gate_up[:, FF:]


def rows_product(former, latter):
    return lax.dot_general(
        former, latter, (((0,), (0,)), ((), ())), preferred_element_type=jnp.float32
    )


def by_transpose(former, latter):
    return lax.dot_general(
        former, latter, (((1,), (1,)), ((), ())), preferred_element_type=jnp.float32
    )


def plain_product(former, latter):
    return jnp.dot(former, latter, preferred_element_type=jnp.float32)


def masked_scores(heads_q, heads_k, position, key_place, length, slopes):
    raw_scores = (
        jnp.einsum("qhd,khd->hqk", heads_q, heads_k, preferred_element_type=jnp.float32) * 0.125
    )
    distance = jnp.abs(position[:, None] - key_place[None, :]).astype(jnp.float32)
    raw_scores = raw_scores - slopes[:, None, None] * distance[None]
    return jnp.where((key_place < length)[None, None, :], raw_scores, NEGATIVE)


def fetch_weights(shards):
    return (
        lax.all_gather(shards[0], "fsdp", axis=0, tiled=True),
        lax.all_gather(shards[1], "fsdp", axis=0, tiled=True),
        lax.all_gather(shards[2], "fsdp", axis=0, tiled=True),
        lax.all_gather(shards[3], "fsdp", axis=0, tiled=True),
        lax.all_gather(shards[4], "fsdp", axis=0, tiled=True),
        lax.all_gather(shards[5], "fsdp", axis=0, tiled=True),
        lax.all_gather(shards[6], "fsdp", axis=0, tiled=True),
        lax.all_gather(shards[7], "fsdp", axis=0, tiled=True),
        lax.all_gather(shards[8], "fsdp", axis=0, tiled=True),
        lax.all_gather(shards[9], "fsdp", axis=0, tiled=True),
        lax.all_gather(shards[10], "fsdp", axis=0, tiled=True),
        lax.all_gather(shards[11], "fsdp", axis=0, tiled=True),
    )


def reduce_grads(grad_terms):
    shard_sums = (
        lax.psum_scatter(grad_terms[0], "fsdp", scatter_dimension=0, tiled=True),
        lax.psum_scatter(grad_terms[1], "fsdp", scatter_dimension=0, tiled=True),
        lax.psum_scatter(grad_terms[2], "fsdp", scatter_dimension=0, tiled=True),
        lax.psum_scatter(grad_terms[3], "fsdp", scatter_dimension=0, tiled=True),
        lax.psum_scatter(grad_terms[4], "fsdp", scatter_dimension=0, tiled=True),
        lax.psum_scatter(grad_terms[5], "fsdp", scatter_dimension=0, tiled=True),
        lax.psum_scatter(grad_terms[6], "fsdp", scatter_dimension=0, tiled=True),
        lax.psum_scatter(grad_terms[7], "fsdp", scatter_dimension=0, tiled=True),
        lax.psum_scatter(grad_terms[8], "fsdp", scatter_dimension=0, tiled=True),
        lax.psum_scatter(grad_terms[9], "fsdp", scatter_dimension=0, tiled=True),
        lax.psum_scatter(grad_terms[10], "fsdp", scatter_dimension=0, tiled=True),
        lax.psum_scatter(grad_terms[11], "fsdp", scatter_dimension=0, tiled=True),
    )
    return (
        lax.psum(shard_sums[0].astype(jnp.bfloat16), "ctx").astype(jnp.float32),
        lax.psum(shard_sums[1].astype(jnp.bfloat16), "ctx").astype(jnp.float32),
        lax.psum(shard_sums[2].astype(jnp.bfloat16), "ctx").astype(jnp.float32),
        lax.psum(shard_sums[3].astype(jnp.bfloat16), "ctx").astype(jnp.float32),
        lax.psum(shard_sums[4].astype(jnp.bfloat16), "ctx").astype(jnp.float32),
        lax.psum(shard_sums[5].astype(jnp.bfloat16), "ctx").astype(jnp.float32),
        lax.psum(shard_sums[6].astype(jnp.bfloat16), "ctx").astype(jnp.float32),
        lax.psum(shard_sums[7].astype(jnp.bfloat16), "ctx").astype(jnp.float32),
        lax.psum(shard_sums[8].astype(jnp.bfloat16), "ctx").astype(jnp.float32),
        lax.psum(shard_sums[9].astype(jnp.bfloat16), "ctx").astype(jnp.float32),
        lax.psum(shard_sums[10].astype(jnp.bfloat16), "ctx").astype(jnp.float32),
        lax.psum(shard_sums[11].astype(jnp.bfloat16), "ctx").astype(jnp.float32),
    )


def per_device_plain(
    tokens_in,
    out_grad,
    seq_lengths,
    order,
    w_qkv,
    bias_q,
    bias_v,
    w_out,
    bias_out,
    ln1_gain,
    ln1_bias,
    w_gate_up,
    w_down,
    bias_down,
    ln2_gain,
    ln2_bias,
):
    shards = (
        w_qkv,
        bias_q,
        bias_v,
        w_out,
        bias_out,
        ln1_gain,
        ln1_bias,
        w_gate_up,
        w_down,
        bias_down,
        ln2_gain,
        ln2_bias,
    )
    group_index = lax.axis_index("fsdp")
    ctx_index = lax.axis_index("ctx")
    dealt_tokens = jnp.take_along_axis(tokens_in, order[:, :, None, None], axis=1)
    tokens_grp, grads_grp = (
        lax.all_to_all(dealt_tokens, "fsdp", split_axis=1, concat_axis=2, tiled=True),
        lax.all_to_all(out_grad, "fsdp", split_axis=1, concat_axis=2, tiled=True),
    )
    dealt_lengths = jnp.take_along_axis(seq_lengths, order, axis=1)
    local_rows = tokens_grp.shape[2]
    key_place = jnp.arange(local_rows * lax.axis_size("ctx"))
    position = ctx_index * local_rows + jnp.arange(local_rows)
    slopes = jnp.array(slope_list(HEADS), jnp.float32)
    output_list = []
    input_list = []
    running = None
    for micro_batch in range(M):
        weights = fetch_weights(shards)
        (
            full_qkv,
            full_bias_q,
            full_bias_v,
            full_out,
            full_bias_out,
            full_ln1_gain,
            full_ln1_bias,
            full_gate_up,
            full_down,
            full_bias_down,
            full_ln2_gain,
            full_ln2_bias,
        ) = weights
        tokens = tokens_grp[micro_batch, 0]
        cotangent = grads_grp[micro_batch, 0]
        length = lax.dynamic_index_in_dim(
            dealt_lengths[micro_batch], group_index, 0, keepdims=False
        )
        valid_rows = position < length
        projected = plain_product(tokens, full_qkv)
        queries = (projected[:, :D] + full_bias_q.astype(jnp.float32)).astype(jnp.bfloat16)
        key_rows = projected[:, D : 2 * D].astype(jnp.bfloat16)
        values = (projected[:, 2 * D :] + full_bias_v.astype(jnp.float32)).astype(jnp.bfloat16)
        keys_all, values_all = (
            lax.all_gather(key_rows, "ctx", axis=0, tiled=True),
            lax.all_gather(values, "ctx", axis=0, tiled=True),
        )
        heads_q = queries.reshape(local_rows, HEADS, HEAD_DIM)
        heads_k = keys_all.reshape(-1, HEADS, HEAD_DIM)
        heads_v = values_all.reshape(-1, HEADS, HEAD_DIM)
        scores = masked_scores(heads_q, heads_k, position, key_place, length, slopes)
        row_max = jnp.max(scores, axis=-1, keepdims=True)
        exp_terms = jnp.exp(scores - row_max)
        row_total = jnp.sum(exp_terms, axis=-1, keepdims=True)
        log_total = row_max + jnp.log(row_total)
        attn_probs = (exp_terms / row_total).astype(jnp.bfloat16)
        context = (
            jnp.einsum("hqk,khd->qhd", attn_probs, heads_v, preferred_element_type=jnp.float32)
            .reshape(local_rows, D)
            .astype(jnp.bfloat16)
        )
        attn_out = plain_product(context, full_out) + full_bias_out.astype(jnp.float32)
        first_sum = tokens.astype(jnp.float32) + attn_out
        normed_one, norm_one_pull = jax.vjp(
            layer_norm,
            first_sum,
            full_ln1_gain.astype(jnp.float32),
            full_ln1_bias.astype(jnp.float32),
        )
        normed_low = normed_one.astype(jnp.bfloat16)
        gate_up = plain_product(normed_low, full_gate_up)
        hidden, gated_pull = jax.vjp(gated_unit, gate_up)
        hidden_low = hidden.astype(jnp.bfloat16)
        branch = plain_product(hidden_low, full_down) + full_bias_down.astype(jnp.float32)
        result, norm_two_pull = jax.vjp(
            layer_norm,
            normed_one + branch,
            full_ln2_gain.astype(jnp.float32),
            full_ln2_bias.astype(jnp.float32),
        )
        output_list.append(jnp.where(valid_rows[:, None], result, 0.0).astype(jnp.bfloat16))
        grad_result = jnp.where(valid_rows[:, None], cotangent.astype(jnp.float32), 0.0)
        grad_second, grad_ln2_gain, grad_ln2_bias = norm_two_pull(grad_result)
        grad_branch = grad_second.astype(jnp.bfloat16)
        grad_bias_down = jnp.sum(grad_branch.astype(jnp.float32), axis=0)
        grad_w_down = rows_product(hidden_low, grad_branch)
        grad_hidden = by_transpose(grad_branch, full_down)
        (grad_gate_up,) = gated_pull(grad_hidden)
        grad_gate_low = grad_gate_up.astype(jnp.bfloat16)
        grad_w_gate_up = rows_product(normed_low, grad_gate_low)
        grad_normed = grad_second + by_transpose(grad_gate_low, full_gate_up)
        grad_first, grad_ln1_gain, grad_ln1_bias = norm_one_pull(grad_normed)
        grad_attn = grad_first.astype(jnp.bfloat16)
        grad_bias_out = jnp.sum(grad_attn.astype(jnp.float32), axis=0)
        grad_w_out = rows_product(context, grad_attn)
        grad_context = (
            by_transpose(grad_attn, full_out)
            .astype(jnp.bfloat16)
            .reshape(local_rows, HEADS, HEAD_DIM)
        )
        scores = masked_scores(heads_q, heads_k, position, key_place, length, slopes)
        attn_exact = jnp.exp(scores - log_total)
        grad_values_term = jnp.einsum(
            "hqk,qhd->khd",
            attn_exact.astype(jnp.bfloat16),
            grad_context,
            preferred_element_type=jnp.float32,
        )
        grad_probs = jnp.einsum(
            "qhd,khd->hqk", grad_context, heads_v, preferred_element_type=jnp.float32
        )
        grad_scores = (
            attn_exact * (grad_probs - jnp.sum(attn_exact * grad_probs, axis=-1, keepdims=True))
        ).astype(jnp.bfloat16)
        grad_queries = (
            jnp.einsum("hqk,khd->qhd", grad_scores, heads_k, preferred_element_type=jnp.float32)
            * 0.125
        ).reshape(local_rows, D)
        grad_keys_term = (
            jnp.einsum("hqk,qhd->khd", grad_scores, heads_q, preferred_element_type=jnp.float32)
            * 0.125
        )
        grad_keys, grad_values = (
            lax.psum_scatter(
                grad_keys_term.reshape(-1, D).astype(jnp.bfloat16),
                "ctx",
                scatter_dimension=0,
                tiled=True,
            ).astype(jnp.float32),
            lax.psum_scatter(
                grad_values_term.reshape(-1, D).astype(jnp.bfloat16),
                "ctx",
                scatter_dimension=0,
                tiled=True,
            ).astype(jnp.float32),
        )
        grad_qkv = jnp.concatenate(
            [
                grad_queries.astype(jnp.bfloat16),
                grad_keys.astype(jnp.bfloat16),
                grad_values.astype(jnp.bfloat16),
            ],
            axis=1,
        )
        grad_w_qkv = rows_product(tokens, grad_qkv)
        grad_bias_q = jnp.sum(grad_qkv[:, :D].astype(jnp.float32), axis=0)
        grad_bias_v = jnp.sum(grad_qkv[:, 2 * D :].astype(jnp.float32), axis=0)
        grad_tokens = grad_first + by_transpose(grad_qkv, full_qkv)
        input_list.append(grad_tokens.astype(jnp.bfloat16))
        grad_terms = (
            grad_w_qkv,
            grad_bias_q,
            grad_bias_v,
            grad_w_out,
            grad_bias_out,
            grad_ln1_gain,
            grad_ln1_bias,
            grad_w_gate_up,
            grad_w_down,
            grad_bias_down,
            grad_ln2_gain,
            grad_ln2_bias,
        )
        reduced = reduce_grads(grad_terms)
        if micro_batch == 0:
            running = reduced
        else:
            running = tuple((left_sum + right_sum for left_sum, right_sum in zip(running, reduced)))
    output_stack = jnp.stack(output_list, axis=0)[:, None]
    input_stack = jnp.stack(input_list, axis=0)[:, None]
    output, dealt_grads = (
        lax.all_to_all(output_stack, "fsdp", split_axis=2, concat_axis=1, tiled=True),
        lax.all_to_all(input_stack, "fsdp", split_axis=2, concat_axis=1, tiled=True),
    )
    inverse = jnp.argsort(order, axis=1)
    input_grad = jnp.take_along_axis(dealt_grads, inverse[:, :, None, None], axis=1)
    return (
        output,
        input_grad,
        running[0],
        running[1],
        running[2],
        running[3],
        running[4],
        running[5],
        running[6],
        running[7],
        running[8],
        running[9],
        running[10],
        running[11],
    )


PIECES = 16
RING = 4


def whole(p, w=256):
    return [(p, 0, D, w)]


GATHER_UNITS = sum([whole(p, 0 if p == 15 else 384 if p in (6, 10) else 256) for p in range(PIECES)], [])
SCATTER_UNITS = sum([whole(p, 256 if i % 3 else 128) for i, p in enumerate([*range(4, 16), 3, 0, 1, 2])], [])
STAGES = ()
SETTLE = 4
AHEAD = 1
ROW_AT = 4
PLANE_AT = 6
CORE_AT = 7
X_AT = (0, 7)
G_AT = (7, 9)
O_AT = (0, 8)
O_FIRST = True
D_AT = (13, 7)


def mm(a, b):
    return jnp.dot(a, b, preferred_element_type=F32)


def mm_nt(a, b):
    return lax.dot_general(a, b, (((1,), (1,)), ((), ())), preferred_element_type=F32)


def mm_tn(a, b):
    return lax.dot_general(a, b, (((0,), (0,)), ((), ())), preferred_element_type=F32)


def block(i, size):
    if isinstance(i, int):
        return pl.ds(i * size, size)
    return pl.ds(pl.multiple_of(i * size, size), size)


class Place:
    def __init__(self, fsdp):
        self.fsdp = fsdp
        self.total = 2 * fsdp
        self.Z = fsdp // 4
        self.x = lax.axis_index("ctx")
        self.f = lax.axis_index("fsdp")
        self.z = self.f // 4
        self.y = lax.rem(self.f // 2, 2)
        self.c = lax.rem(self.f, 2)
        self.me = self.x * fsdp + self.f
        self.pending = []
        self.turn = 0

    def dev(self, x=None, z=None, y=None, c=None):
        x = self.x if x is None else x
        z = self.z if z is None else z
        y = self.y if y is None else y
        c = self.c if c is None else c
        return (x, z * 4 + y * 2 + c)

    def cols(self, unit):
        p, lo, n, w = unit
        return pl.ds(pl.multiple_of(lo + self.x * w, 128), n - w)

    def give(self, unit):
        p, lo, n, w = unit
        return pl.ds(pl.multiple_of(lo + self.x * (n - w), 128), w)

    def take(self, unit):
        p, lo, n, w = unit
        return pl.ds(pl.multiple_of(lo + (1 - self.x) * (n - w), 128), w)

    def at(self, d):
        return (d // self.fsdp, lax.rem(d, self.fsdp))

    def signal(self):
        sem = pltpu.get_barrier_semaphore()

        @pl.loop(1, self.total)
        def _(k):
            d = lax.rem(self.me + k, self.total)
            pl.semaphore_signal(sem, inc=1, device_id=self.at(d), device_id_type=MESH)

    def wait(self):
        pl.semaphore_wait(pltpu.get_barrier_semaphore(), self.total - 1)

    def go(self, copy, cond=None):
        if cond is None:
            copy.start()
        else:
            pl.when(cond)(copy.start)
        self.pending.append((self.turn, cond, copy))

    def finish(self, before=None):
        left = []
        for turn, cond, copy in self.pending:
            if before is not None and turn >= before:
                left.append((turn, cond, copy))
            elif cond is None:
                copy.wait_send()
            else:
                pl.when(cond)(copy.wait_send)
        self.pending = left


def remote(src, dst, send, recv, device):
    return pltpu.make_async_remote_copy(
        src_ref=src, dst_ref=dst, send_sem=send, recv_sem=recv, device_id=device, device_id_type=MESH
    )


class Exchange:
    def __init__(self, pc, src, dst, sems, k):
        self.pc, self.src, self.dst = pc, src, dst
        self.send, self.recv, self.local = sems[0].at[k], sems[1].at[k], sems[2].at[k]

    def own(self):
        return pltpu.make_async_copy(self.src.at[self.pc.me], self.dst.at[self.pc.me], self.local)

    def start(self, turn=0, turns=1):
        pc = self.pc
        if turn == 0:
            self.own().start()
        near = [(x, 0, y, c) for x in range(2) for y in range(2) for c in range(2) if x + y + c]
        far = [(x, z, y, c) for x in range(2) for y in range(2) for c in range(2) for z in (2, 3, 1)]
        if turns > 1:
            per = -(-len(far) // (turns - 1))
            picked = far[(turn - 1) * per : turn * per] if turn else near
        else:
            picked = near + far
        for x, z, y, c in picked:
            to = pc.dev(
                x=(1 - pc.x) if x else None,
                y=(1 - pc.y) if y else None,
                c=(1 - pc.c) if c else None,
                z=(None, pc.z + 1 - 2 * lax.rem(pc.z, 2), lax.rem(pc.z + 2, 4), 3 - pc.z)[z],
            )
            d = to[0] * pc.fsdp + to[1]
            remote(self.src.at[d], self.dst.at[pc.me], self.send, self.recv, to).start()

    def whole(self):
        blocks = pl.ds(0, self.pc.total - 1)
        return remote(self.src.at[blocks], self.dst.at[blocks], self.send, self.recv, self.pc.dev(c=1 - self.pc.c))

    def wait(self):
        self.own().wait()
        self.whole().wait_recv()

    def done(self):
        self.whole().wait_send()


class Gather:
    def __init__(self, pc, own, slots, sems):
        self.pc, self.own = pc, own
        self.place = slots
        self.zs, self.zr, self.ys, self.yr, self.xs, self.xr, self.cs, self.cr, self.ls = sems

    @staticmethod
    def sems(Z):
        T = pltpu.SemaphoreType.DMA
        n = len(GATHER_UNITS)
        return [
            T((n, 2 * Z - 2)), T((n, 2 * Z - 2)), T((n, 2 * Z - 1)), T((n,)),
            T((n, 2 * Z - 1)), T((n, 2 * Z - 1)), T((n, 2)), T((n, 2)), T((n,)),
        ]

    def up(self):
        return jnp.minimum(self.pc.z + 1, self.pc.Z - 1)

    def down(self):
        return jnp.maximum(self.pc.z - 1, 0)

    def slots(self, u, z, y, cols):
        return self.place(GATHER_UNITS[u][0], z, y, self.pc.c, cols)

    def cols(self, u):
        return self.pc.cols(GATHER_UNITS[u])

    def mine(self, u):
        pc = self.pc
        p, lo, n, w = GATHER_UNITS[u]
        return pltpu.make_async_copy(self.own(p, pl.ds(lo, n)), self.slots(u, pc.z, pc.y, pl.ds(lo, n)), self.ls.at[u])

    def start(self, u):
        pc = self.pc
        Z = pc.Z
        src = self.own(GATHER_UNITS[u][0], self.cols(u))
        dst = self.slots(u, pc.z, pc.y, self.cols(u))
        self.mine(u).start()
        pc.go(remote(src, dst, self.zs.at[u, 0], self.zr.at[u, 0], pc.dev(z=self.up())), pc.z < Z - 1)
        k = Z - 1
        pc.go(remote(src, dst, self.zs.at[u, k], self.zr.at[u, k], pc.dev(z=self.down())), pc.z > 0)
        pc.go(remote(src, dst, self.ys.at[u, 0], self.yr.at[u], pc.dev(y=1 - pc.y)))

    def hops(self, h):
        pc = self.pc
        Z = pc.Z
        return (
            (jnp.maximum(pc.z - h, 0), pc.z >= h, pc.z < Z - 1, self.up(), h - 1),
            (jnp.minimum(pc.z + h, Z - 1), pc.z + h < Z, pc.z > 0, self.down(), Z + h - 2),
        )

    def hop(self, u, h):
        pc = self.pc
        for z, here, onward, to, k in self.hops(h):
            ref = self.slots(u, z, pc.y, self.cols(u))
            pl.when(here)(remote(ref, ref, self.zs.at[u, k], self.zr.at[u, k], pc.dev(z=to)).wait_recv)
            if h < pc.Z - 1:
                pc.go(
                    remote(ref, ref, self.zs.at[u, k + 1], self.zr.at[u, k + 1], pc.dev(z=to)),
                    jnp.logical_and(here, onward),
                )
            pc.go(remote(ref, ref, self.ys.at[u, 1 + k], self.yr.at[u], pc.dev(y=1 - pc.y)), here)
            if GATHER_UNITS[u][3]:
                ref = self.slots(u, z, pc.y, pc.give(GATHER_UNITS[u]))
                pc.go(remote(ref, ref, self.xs.at[u, k], self.xr.at[u, k], pc.dev(x=1 - pc.x)), here)

    def row(self, u):
        pc = self.pc
        unit = GATHER_UNITS[u]
        ref = self.slots(u, slice(None), 1 - pc.y, self.cols(u))
        remote(ref, ref, self.ys.at[u, 0], self.yr.at[u], pc.dev(y=1 - pc.y)).wait_recv()
        if unit[3]:
            k = 2 * pc.Z - 2
            ref = self.slots(u, slice(None), 1 - pc.y, pc.give(unit))
            pc.go(remote(ref, ref, self.xs.at[u, k], self.xr.at[u, k], pc.dev(x=1 - pc.x)))
        self.mine(u).wait()
        ref = self.slots(u, slice(None), slice(None), self.cols(u))
        pc.go(remote(ref, ref, self.cs.at[u, 0], self.cr.at[u, 0], pc.dev(c=1 - pc.c)))

    def plane(self, u):
        pc = self.pc
        unit = GATHER_UNITS[u]
        if not unit[3]:
            return
        take = pc.take(unit)
        for h in range(1, pc.Z):
            for z, here, onward, to, k in self.hops(h):
                ref = self.slots(u, z, pc.y, take)
                pl.when(here)(remote(ref, ref, self.xs.at[u, k], self.xr.at[u, k], pc.dev(x=1 - pc.x)).wait_recv)
        k = 2 * pc.Z - 2
        ref = self.slots(u, slice(None), 1 - pc.y, take)
        remote(ref, ref, self.xs.at[u, k], self.xr.at[u, k], pc.dev(x=1 - pc.x)).wait_recv()
        ref = self.slots(u, slice(None), slice(None), take)
        pc.go(remote(ref, ref, self.cs.at[u, 1], self.cr.at[u, 1], pc.dev(c=1 - pc.c)))

    def core(self, u):
        pc = self.pc
        parts = [pc.cols(GATHER_UNITS[u])] + ([pc.take(GATHER_UNITS[u])] if GATHER_UNITS[u][3] else [])
        for k, cols in enumerate(parts):
            ref = self.place(GATHER_UNITS[u][0], slice(None), slice(None), 1 - pc.c, cols)
            remote(ref, ref, self.cs.at[u, k], self.cr.at[u, k], pc.dev(c=1 - pc.c)).wait_recv()


class Scatter:
    def __init__(self, pc, terms, get, put, from_c, from_x, from_y, from_z, from_f, sems):
        self.pc, self.terms, self.get, self.put = pc, terms, get, put
        self.from_c, self.from_x, self.from_y, self.from_z, self.from_f = from_c, from_x, from_y, from_z, from_f
        self.cs, self.cr, self.xs, self.xr, self.ys, self.yr, self.zs, self.zr, self.fs, self.fr, self.free = sems
        z = pc.z
        self.inner = jnp.logical_or(z == 1, z == 2)
        self.outer = jnp.logical_not(self.inner)
        self.mate = z + 1 - 2 * lax.rem(z, 2)
        self.far_in = jnp.where(z < 2, 2, 1)
        self.far_out = jnp.where(z < 2, 3, 0)
        self.x_lo, self.y_lo = [], []
        used = {}
        for p, lo, n, w in SCATTER_UNITS:
            a, b = used.get(p, (0, 0))
            self.x_lo.append(a)
            self.y_lo.append(b)
            used[p] = (a + w, b + n - w)

    @staticmethod
    def sems():
        T = pltpu.SemaphoreType.DMA
        n = len(SCATTER_UNITS)
        return [
            T((n,)), T((n,)), T((n,)), T((n,)), T((n,)), T((n,)), T((n, 5)), T((n, 4)), T((n,)), T((n,)),
            pltpu.SemaphoreType.REGULAR((n,)),
        ]

    @staticmethod
    def buffers(Z, rows):
        n = PIECES
        give, win = [0] * n, [0] * n
        for p, lo, k, w in SCATTER_UNITS:
            give[p] += w
            win[p] += k - w
        give, win = max(give), max(win)
        return [
            pltpu.VMEM((RING, Z, 2, rows, D), BF),
            pltpu.VMEM((n, Z, 2, rows, give), BF),
            pltpu.VMEM((n, Z, rows, win), BF),
            pltpu.VMEM((n, 4, rows, win), BF),
            pltpu.VMEM((n, rows, win), BF),
        ]

    def x_at(self, u):
        return pl.ds(self.x_lo[u], SCATTER_UNITS[u][3])

    def y_at(self, u):
        p, lo, n, w = SCATTER_UNITS[u]
        return pl.ds(self.y_lo[u], n - w)

    def add(self, u, z, y, cols, value):
        p = SCATTER_UNITS[u][0]
        c = self.pc.c
        self.put(p, z, y, c, cols, self.get(p, z, y, c, cols) + value)

    def part(self, u, z, y, cols):
        return self.terms(SCATTER_UNITS[u][0], z, y, self.pc.c, cols)

    def start(self, u):
        pc = self.pc
        p, lo, n, w = SCATTER_UNITS[u]
        if u >= RING:
            pl.semaphore_wait(self.free.at[u], 1)
        src = self.terms(p, slice(None), slice(None), 1 - pc.c, pl.ds(lo, n))
        dst = self.from_c.at[u % RING, :, :, :, pl.ds(0, n)]
        pc.go(remote(src, dst, self.cs.at[u], self.cr.at[u], pc.dev(c=1 - pc.c)))

    def core(self, u):
        pc = self.pc
        p, lo, n, w = SCATTER_UNITS[u]
        ref = self.from_c.at[u % RING, :, :, :, pl.ds(0, n)]
        remote(ref, ref, self.cs.at[u], self.cr.at[u], pc.dev(c=1 - pc.c)).wait_recv()
        for z in range(pc.Z):
            for y in range(2):
                self.add(u, z, y, pl.ds(lo, n), self.from_c[u % RING, z, y, :, pl.ds(0, n)])
        if u + RING < len(SCATTER_UNITS):
            pl.semaphore_signal(self.free.at[u + RING], inc=1, device_id=pc.dev(c=1 - pc.c), device_id_type=MESH)
        if w:
            src = self.part(u, slice(None), slice(None), pc.take(SCATTER_UNITS[u]))
            dst = self.from_x.at[p, :, :, :, self.x_at(u)]
            pc.go(remote(src, dst, self.xs.at[u], self.xr.at[u], pc.dev(x=1 - pc.x)))
        else:
            self.across(u)

    def plane(self, u):
        pc = self.pc
        p, lo, n, w = SCATTER_UNITS[u]
        if w:
            ref = self.from_x.at[p, :, :, :, self.x_at(u)]
            remote(ref, ref, self.xs.at[u], self.xr.at[u], pc.dev(x=1 - pc.x)).wait_recv()
            for z in range(pc.Z):
                for y in range(2):
                    self.add(u, z, y, pc.give(SCATTER_UNITS[u]), self.from_x[p, z, y, :, self.x_at(u)])
            self.across(u)

    def across(self, u):
        pc = self.pc
        src = self.part(u, slice(None), 1 - pc.y, pc.cols(SCATTER_UNITS[u]))
        dst = self.from_y.at[SCATTER_UNITS[u][0], :, :, self.y_at(u)]
        pc.go(remote(src, dst, self.ys.at[u], self.yr.at[u], pc.dev(y=1 - pc.y)))

    def z_ref(self, u, k):
        return self.from_z.at[SCATTER_UNITS[u][0], k, :, self.y_at(u)]

    def z_add(self, u, k, z):
        ref = self.z_ref(u, k)
        remote(ref, ref, self.zs.at[u, k], self.zr.at[u, k], self.pc.dev(z=self.mate)).wait_recv()
        value = self.from_z[SCATTER_UNITS[u][0], k, :, self.y_at(u)]
        self.add(u, z, self.pc.y, self.pc.cols(SCATTER_UNITS[u]), value)

    def row(self, u):
        pc = self.pc
        p = SCATTER_UNITS[u][0]
        cols = pc.cols(SCATTER_UNITS[u])
        ref = self.from_y.at[p, :, :, self.y_at(u)]
        remote(ref, ref, self.ys.at[u], self.yr.at[u], pc.dev(y=1 - pc.y)).wait_recv()
        for z in range(pc.Z):
            self.add(u, z, pc.y, cols, self.from_y[p, z, :, self.y_at(u)])
        for k, z in enumerate((self.mate, self.far_in, self.far_out)):
            copy = remote(
                self.part(u, z, pc.y, cols), self.z_ref(u, k), self.zs.at[u, k], self.zr.at[u, k], pc.dev(z=self.mate)
            )
            pc.go(copy, self.outer if k else None)

    def middle(self, u):
        pc = self.pc
        cols = pc.cols(SCATTER_UNITS[u])
        far = ((1, self.far_in), (2, self.far_out))

        @pl.when(self.inner)
        def _():
            for k, z in far:
                self.z_add(u, k, z)

        for k, z in far:
            src = self.part(u, z, pc.y, cols)
            pc.go(remote(src, self.z_ref(u, 3), self.zs.at[u, 2 + k], self.zr.at[u, 3], pc.dev(z=z)), self.inner)

    def f_ref(self, u):
        return self.from_f.at[SCATTER_UNITS[u][0], :, self.y_at(u)]

    def line(self, u):
        pc = self.pc
        for k in (0, 3):
            self.z_add(u, k, pc.z)
        src = self.part(u, pc.z, pc.y, pc.cols(SCATTER_UNITS[u]))
        pc.go(remote(src, self.f_ref(u), self.fs.at[u], self.fr.at[u], pc.dev(x=1 - pc.x)))

    def last(self, u, out):
        pc = self.pc
        unit = p, lo, n, w = SCATTER_UNITS[u]
        ref = self.f_ref(u)
        remote(ref, ref, self.fs.at[u], self.fr.at[u], pc.dev(x=1 - pc.x)).wait_recv()
        at = self.y_lo[u]

        def own(cols):
            return self.get(p, pc.z, pc.y, pc.c, cols).astype(F32)

        if w:
            out[:, pc.give(unit)] = own(pc.give(unit))
            theirs = pl.ds(pl.multiple_of(at + (1 - pc.x) * (n - 2 * w), 128), w)
            out[:, pc.take(unit)] = self.from_f[p, :, theirs].astype(F32)
        if n > 2 * w:
            both = pl.ds(pl.multiple_of(at + pc.x * w, 128), n - 2 * w)
            shared = pl.ds(lo + w, n - 2 * w)
            out[:, shared] = own(shared) + self.from_f[p, :, both].astype(F32)


def row_mean(v):
    return jnp.sum(v, axis=-1, keepdims=True) * (1.0 / D)


BQ, BV, BO, G1, B1, BD, G2, B2 = range(8)


def layer_kernel(
    fsdp, rows,
    order, lengths, slopes, tokens_in, grads_in, *refs,
):
    small_in, (wq_in, wo_in, wg_in, wd_in) = refs[:8], refs[8:12]
    OUT, DX, GQ, GW, GG, GD, SMALLG, *refs = refs[12:]
    (
    wa, wd, raw, outv, xs, gs, small, small_own, smallf, qkv, dist, lse, ctxt, y1, y1b, xhat, rstd, act, slope_up, zed, acc, dfb, tr,
    dxr, sgrad, sparts, gsum, from_c, from_x, from_y, from_z, from_f, *sems,
    ) = refs
    pc = Place(fsdp)
    Z = pc.Z
    L = pc.total * raw.shape[1]
    gsems, ssems, esems, rsem = sems[:9], sems[9:20], sems[20:23], sems[23]
    w_pc = wa.shape[1:]

    def own(p, cols):
        if p < 3:
            return wq_in.at[:, pl.ds(pl.multiple_of(D * p + cols.start, 128), cols.size)]
        if p == 3:
            return wo_in.at[:, cols]
        if p < 12:
            i, j = (p - 4) // 2, (p - 4) % 2
            return wg_in.at[:, pl.ds(pl.multiple_of(FF * j + D * i + cols.start, 128), cols.size)]
        return wd_in.at[pl.ds(rows * (p - 12), rows), cols]

    def slots(p, z, y, c, cols):
        if p < 12:
            return wa.at[p, z, y, c, :, cols]
        return wd.at[z, y, c, p - 12, :, cols]

    def get(p, z, y, c, cols):
        if p < 12:
            return wa[p, z, y, c, :, cols]
        return wd[z, y, c, p - 12, :, cols]

    def put(p, z, y, c, cols, value):
        if p < 12:
            wa[p, z, y, c, :, cols] = value
        else:
            wd[z, y, c, p - 12, :, cols] = value

    def out_of(p):
        if p >= 12:
            return GD.at[pl.ds(rows * (p - 12), rows)]
        if p == 3:
            return GW
        if p < 3:
            return GQ.at[:, pl.ds(D * p, D)]
        i, j = (p - 4) // 2, (p - 4) % 2
        return GG.at[:, pl.ds(FF * j + D * i, D)]

    def w_cols(p, cols):
        return wa[p, :, :, :, :, cols].reshape(D, cols.size)

    def w_all(p):
        return wa[p].reshape(D, D)

    g = Gather(pc, own, slots, gsems)
    sc = Scatter(pc, slots, get, put, from_c, from_x, from_y, from_z, from_f, ssems)
    ex_x = Exchange(pc, outv, xs, esems, 0)
    ex_g = Exchange(pc, grads_in, gs, esems, 1)
    ex_o = Exchange(pc, outv, OUT, esems, 3)
    ex_d = Exchange(pc, raw, dxr, esems, 4)
    ex_s = Exchange(pc, sparts, gsum, esems, 5)
    len_s = lengths[pc.x, order[pc.x, pc.f]]

    def tokens(r):
        n = r.size // 16
        return xs[pl.ds(r.start // 16, n)].reshape(r.size, D)

    def deal():
        @pl.loop(0, pc.total)
        def _(d):
            m = d // fsdp
            outv[d] = raw[m * fsdp + order[m, lax.rem(d, fsdp)]]

    def prepare():
        k = lax.broadcasted_iota(jnp.int32, (L, L), 0)
        q = lax.broadcasted_iota(jnp.int32, (L, L), 1)
        dist[...] = jnp.where(k < len_s, jnp.abs(k - q).astype(F32), -NEGATIVE)

    def place_small():
        for f in range(fsdp):
            smallf[:, pl.ds(f * rows, rows)] = small[f, :, pl.ds(0, rows)]

    def project(p):
        @pl.loop(0, D // 256)
        def _(t):
            cols = block(t, 256)
            r = mm(xs[...].reshape(L, D), w_cols(p, cols))
            if p != 1:
                r = r + smallf[pl.ds(BQ if p == 0 else BV, 1), cols]
            qkv[p, :, cols] = r.astype(BF)

    def attend(j):
        cols = block(j, 128)
        lane = lax.broadcasted_iota(jnp.int32, (L, 128), 1)
        q2, k2 = qkv[0, :, cols], qkv[1, :, cols]
        vt = qkv[2, :, cols].T
        for q in range(L // 256):
            qr = pl.ds(256 * q, 256)
            parts = []
            for s in range(2):
                qm = jnp.where((lane < 64) if s == 0 else (lane >= 64), q2, jnp.zeros_like(q2))
                st = mm_nt(k2, qm[256 * q : 256 * q + 256])
                st = st * (0.125 * LOG2E) - dist[:, qr] * slopes[2 * j + s]
                top = jnp.max(st, axis=0, keepdims=True)
                e = jnp.exp2(st - top)
                total = jnp.sum(e, axis=0, keepdims=True)
                lse[2 * j + s, :, qr] = top + jnp.log2(total)
                pr = (e * (1.0 / total)).astype(BF)
                parts.append(mm(vt[64 * s : 64 * s + 64], pr))
            ctxt[qr, cols] = jnp.concatenate(parts, axis=0).T.astype(BF)

    def first_sum():
        @pl.loop(0, D // 256)
        def _(t):
            cols = block(t, 256)
            acc[:, cols] = mm(ctxt[...], w_cols(3, cols)) + smallf[pl.ds(BO, 1), cols]

    def first_norm():
        @pl.loop(0, L // 64)
        def _(i):
            r = block(i, 64)
            h = acc[r, :] + tokens(r).astype(F32)
            centre = h - row_mean(h)
            rs = lax.rsqrt(row_mean(centre * centre) + EPSILON)
            xh = centre * rs
            xhat[r, :] = xh
            rstd[r, :] = jnp.broadcast_to(rs, (64, 128))
            yy = xh * smallf[pl.ds(G1, 1), :] + smallf[pl.ds(B1, 1), :]
            y1[r, :] = yy
            y1b[r, :] = yy.astype(BF)

        tr[...] = y1b[...].T

    def gated(i):
        for s in range(D // 256):
            gated_part(i, s)

    def gated_part(i, s):
        wc = block(s, 256)
        cols = block(i * 3 + s, 256)
        a = mm(y1b[...], w_cols(4 + 2 * i, wc))
        u = mm(y1b[...], w_cols(5 + 2 * i, wc))
        cdf = 0.5 + 0.5 * lax.erf(a * math.sqrt(0.5))
        pdf = jnp.exp2(a * a * (-0.5 * LOG2E)) * (1.0 / math.sqrt(2.0 * math.pi))
        gelu = a * cdf
        zed[:, cols] = (gelu * u).astype(BF)
        act[:, cols] = gelu.astype(BF)
        slope_up[:, cols] = (u * (cdf + a * pdf)).astype(BF)

    def second_norm():
        @pl.loop(0, D // 256)
        def _(t):
            cols = block(t, 256)
            w = wd[:, :, :, :, :, cols].reshape(FF, 256)
            acc[:, cols] = mm(zed[...], w) + smallf[pl.ds(BD, 1), cols]

        def step(i, sums):
            r = block(i, 64)
            h = acc[r, :] + y1[r, :]
            centre = h - row_mean(h)
            rs = lax.rsqrt(row_mean(centre * centre) + EPSILON)
            xh = centre * rs
            gain = smallf[pl.ds(G2, 1), :]
            valid = (lax.broadcasted_iota(jnp.int32, (64, D), 0) + i * 64) < len_s
            res = jnp.where(valid, xh * gain + smallf[pl.ds(B2, 1), :], 0.0).astype(BF)
            outv[pl.ds(i * 4, 4)] = res.reshape(4, 16, D)
            up = jnp.where(valid, gs[pl.ds(i * 4, 4)].reshape(64, D).astype(F32), 0.0)
            dx = up * gain
            dh = rs * (dx - row_mean(dx) - xh * row_mean(dx * xh))
            low = dh.astype(BF)
            acc[r, :] = dh
            dfb[r, :] = low
            sg, sb, sd = sums
            return (
                sg + jnp.sum(up * xh, axis=0, keepdims=True),
                sb + jnp.sum(up, axis=0, keepdims=True),
                sd + jnp.sum(low.astype(F32), axis=0, keepdims=True),
            )

        zero = jnp.zeros((1, D), F32)
        sg, sb, sd = lax.fori_loop(0, L // 64, step, (zero, zero, zero))
        sgrad[pl.ds(G2, 1), :] = sg
        sgrad[pl.ds(B2, 1), :] = sb
        sgrad[pl.ds(BD, 1), :] = sd

    def ff_back(i):
        cols = block(i, D)
        dz = mm_nt(dfb[...], wd[pl.ds(i * Z // 4, Z // 4)].reshape(D, D))
        dgate = (dz * slope_up[:, cols].astype(F32)).astype(BF)
        dup = (dz * act[:, cols].astype(F32)).astype(BF)
        act[:, cols] = dup
        acc[...] += mm_nt(dgate, w_all(4 + 2 * i))
        wa[4 + 2 * i] = mm(tr[...], dgate).astype(BF).reshape(w_pc)

    def ff_back_rest(i):
        cols = block(i, D)
        acc[...] += mm_nt(act[:, cols], w_all(5 + 2 * i))
        wa[5 + 2 * i] = mm(tr[...], act[:, cols]).astype(BF).reshape(w_pc)
        wd[pl.ds(i * Z // 4, Z // 4)] = mm_tn(zed[:, cols], dfb[...]).astype(BF).reshape((Z // 4,) + wd.shape[1:])

    def first_norm_back():
        def step(i, sums):
            r = block(i, 64)
            up = acc[r, :]
            xh = xhat[r, :]
            dx = up * smallf[pl.ds(G1, 1), :]
            dh = rstd[r, :][:, :1] * (dx - row_mean(dx) - xh * row_mean(dx * xh))
            low = dh.astype(BF)
            xhat[r, :] = dh
            dfb[r, :] = low
            sg, sb, sd = sums
            return (
                sg + jnp.sum(up * xh, axis=0, keepdims=True),
                sb + jnp.sum(up, axis=0, keepdims=True),
                sd + jnp.sum(low.astype(F32), axis=0, keepdims=True),
            )

        zero = jnp.zeros((1, D), F32)
        sg, sb, sd = lax.fori_loop(0, L // 64, step, (zero, zero, zero))
        sgrad[pl.ds(G1, 1), :] = sg
        sgrad[pl.ds(B1, 1), :] = sb
        sgrad[pl.ds(BO, 1), :] = sd

    def out_back():
        y1b[...] = mm_nt(dfb[...], w_all(3)).astype(BF)
        wa[3] = mm_tn(ctxt[...], dfb[...]).astype(BF).reshape(w_pc)

    def dqkv(p):
        return act.at[:, pl.ds(D * p, D)]

    def attend_back(j):
        cols = block(j, 128)
        lane = lax.broadcasted_iota(jnp.int32, (L, 128), 1)
        q2, k2, v2 = (qkv[i, :, cols] for i in range(3))
        do2 = y1b[:, cols]
        kt = k2.T
        dv = dk = None
        for q in range(L // 256):
            qr = pl.ds(256 * q, 256)
            qs = slice(256 * q, 256 * q + 256)
            parts = []
            for s in range(2):
                half = (lane < 64) if s == 0 else (lane >= 64)
                qm = jnp.where(half, q2, jnp.zeros_like(q2))[qs]
                dm = jnp.where(half, do2, jnp.zeros_like(do2))[qs]
                st = mm_nt(k2, qm) * (0.125 * LOG2E) - dist[:, qr] * slopes[2 * j + s]
                pr = jnp.exp2(st - lse[2 * j + s, :, qr])
                dp = mm_nt(v2, dm)
                ds = (pr * (dp - jnp.sum(pr * dp, axis=0, keepdims=True))).astype(BF)
                a, b = mm(pr.astype(BF), dm), mm(ds, qm)
                dv = a if dv is None else dv + a
                dk = b if dk is None else dk + b
                parts.append(mm(kt[64 * s : 64 * s + 64], ds))
            dqkv(0)[qr, cols] = (jnp.concatenate(parts, axis=0).T * 0.125).astype(BF)
        dqkv(1)[:, cols] = (dk * 0.125).astype(BF)
        dqkv(2)[:, cols] = dv.astype(BF)

    def weights_back(p):
        x = xs[...].reshape(L, D)
        d = dqkv(p)
        wa[p] = mm_tn(x, d[...]).astype(BF).reshape(w_pc)
        if p != 1:
            r = BQ if p == 0 else BV
            sgrad[pl.ds(r, 1), :] = jnp.sum(d[...].astype(F32), axis=0, keepdims=True)

    def tokens_back():
        @pl.loop(0, L // 128)
        def _(i):
            r = block(i, 128)
            v = xhat[r, :]
            for p in range(3):
                v = v + mm_nt(dqkv(p)[r, :], w_all(p))
            raw[pl.ds(i * 8, 8)] = v.astype(BF).reshape(8, 16, D)

    def split_small():
        sparts[...] = jnp.zeros_like(sparts)
        for d in range(pc.total):
            at = d % fsdp * rows
            sparts[d, :, pl.ds(0, rows)] = sgrad[:, pl.ds(at, rows)]

    def undeal():
        @pl.loop(0, pc.total)
        def _(k):
            m, n = k // fsdp, lax.rem(k, fsdp)

            def find(f, at):
                return jnp.where(order[m, f] == n, f, at)

            DX[k] = dxr[m * fsdp + lax.fori_loop(0, fsdp, find, 0)]

    def spread(ex, t, at):
        first, count = at
        if first <= t < first + count:
            ex.start(t - first, count)

    take_raw = pltpu.make_async_copy(tokens_in, raw, rsem)
    take_raw.start()
    pc.signal()
    small_own[...] = jnp.zeros_like(small_own)
    for i, ref in enumerate(small_in):
        small_own[pl.ds(i, 1), pl.ds(0, rows)] = ref[...].astype(F32)
    prepare()
    take_raw.wait()
    deal()
    pc.wait()

    me_small = small.at[pc.f]
    keep_small = pltpu.make_async_copy(small_own, me_small, esems[2].at[2])
    keep_small.start()

    @pl.loop(1, fsdp)
    def _(k):
        f = lax.rem(pc.f + k, fsdp)
        remote(small_own, me_small, esems[0].at[2], esems[1].at[2], (pc.x, f)).start()

    small_all = remote(
        small.at[pl.ds(0, fsdp - 1)], small.at[pl.ds(0, fsdp - 1)], esems[0].at[2], esems[1].at[2],
        pc.dev(c=1 - pc.c),
    )

    def begin():
        ex_x.wait()
        small_all.wait_recv()
        keep_small.wait()
        place_small()
        for p in range(3):
            project(p)

    tasks = [(2, begin)]
    tasks += [(2, functools.partial(attend, j)) for j in range(HEADS // 2)]
    tasks += [(3, first_sum), (3, first_norm)]
    tasks += [(5 + 2 * i, functools.partial(gated, i)) for i in range(FF // D)]
    there = -1

    units = len(GATHER_UNITS)
    finished = [max(u for u in range(units) if GATHER_UNITS[u][0] == p) for p in range(PIECES)]
    for t in range(units + CORE_AT):
        pc.turn = t
        pc.finish(t - SETTLE)
        spread(ex_x, t, X_AT)
        spread(ex_g, t, G_AT)
        for u in range(units):
            if t == max(0, u - AHEAD):
                g.start(u)
        for h in range(1, Z):
            for u in range(units):
                if t == max(0, u - AHEAD) + h:
                    g.hop(u, h)
        if 0 <= t - ROW_AT < units:
            g.row(t - ROW_AT)
        if 0 <= t - PLANE_AT < units:
            g.plane(t - PLANE_AT)
        if 0 <= t - CORE_AT < units:
            u = t - CORE_AT
            g.core(u)
            there = max([p for p in range(PIECES) if finished[p] <= u], default=-1)
            left = units + CORE_AT - 1 - t
            if tasks and tasks[0][0] <= there:
                tasks.pop(0)[1]()
            while len(tasks) > left and tasks[0][0] <= there:
                tasks.pop(0)[1]()
    ex_g.wait()
    ex_x.done()
    second_norm()
    if O_FIRST:
        ex_o.start()
    pc.finish()

    units = len(SCATTER_UNITS)
    stages = STAGES if STAGES else (("core", 1), ("plane", 3), ("row", 5), ("middle", 6), ("line", 8), ("last", 10))
    for t in range(units + stages[-1][1]):
        pc.turn = t
        pc.finish(t - SETTLE)
        if t < 8:
            (ff_back_rest if t % 2 else ff_back)(t // 2)
        if t == 8:
            first_norm_back()
            out_back()
        if 9 <= t < 12:
            pl.loop(2 * (t - 9), 2 * (t - 9) + 2)(attend_back)
        if t == 12:
            tokens_back()
            for p in range(3):
                weights_back(p)
            split_small()
            ex_s.start()
        if not O_FIRST:
            spread(ex_o, t, O_AT)
        spread(ex_d, t, D_AT)
        if t < units:
            sc.start(t)
        for name, off in stages:
            if 0 <= t - off < units:
                u = t - off
                if name == "last":
                    sc.last(u, out_of(SCATTER_UNITS[u][0]))
                else:
                    getattr(sc, name)(u)
    ex_s.wait()

    def add(i, v):
        return v + gsum[i]

    total = lax.fori_loop(1, pc.total, add, gsum[0])
    SMALLG[...] = total[:, :rows]
    ex_d.wait()
    undeal()
    ex_o.wait()
    for e in (ex_g, ex_o, ex_d, ex_s):
        e.done()
    small_all.wait_send()
    pc.finish()


def hand_over(*refs):
    src, small, dst, parts, through, sem = refs[:6], refs[6], refs[7:13], refs[13:21], refs[21:27], refs[27]
    take = [pltpu.make_async_copy(a, b, sem.at[0, k]) for k, (a, b) in enumerate(zip(src, through))]
    give = [pltpu.make_async_copy(a, b, sem.at[1, k]) for k, (a, b) in enumerate(zip(through, dst))]
    for c in take:
        c.start()
    for k, ref in enumerate(parts):
        ref[...] = small[pl.ds(k, 1), :]
    for a, b in zip(take, give):
        a.wait()
        b.start()
    for c in give:
        c.wait()


def per_device(
    tokens_in, out_grad, seq_lengths, order, w_qkv, bias_q, bias_v, w_out, bias_out, ln1_gain, ln1_bias, w_gate_up,
    w_down, bias_down, ln2_gain, ln2_bias,
):
    fsdp = lax.axis_size("fsdp")
    total = 2 * fsdp
    rows = w_out.shape[0]
    here = tokens_in.shape[2]
    L = here * total
    Z = fsdp // 4
    small = [v.reshape(1, rows) for v in (bias_q, bias_v, bias_out, ln1_gain, ln1_bias, bias_down, ln2_gain, ln2_bias)]
    slopes = jnp.array(slope_list(HEADS), F32) * LOG2E
    hbm = pl.BlockSpec(memory_space=pl.ANY)
    smem = pl.BlockSpec(memory_space=pltpu.SMEM)
    vmem = pl.BlockSpec(memory_space=pltpu.VMEM)
    S = jax.ShapeDtypeStruct
    T = pltpu.SemaphoreType.DMA
    V = pltpu.VMEM
    rows_of = (total, here, D)
    results = pl.pallas_call(
        functools.partial(layer_kernel, fsdp, rows),
        out_shape=[
            S(rows_of, BF), S(rows_of, BF), S((rows, 3 * D), F32), S((rows, D), F32), S((rows, 2 * FF), F32),
            S((4 * rows, D), F32), S((8, rows), F32),
        ],
        in_specs=[smem] * 3 + [hbm] * 2 + [vmem] * 8 + [hbm] * 4,
        out_specs=[hbm] + [vmem] * 6,
        scratch_shapes=[
            V((12, Z, 2, 2, rows, D), BF), V((Z, 2, 2, 4, rows, D), BF), V(rows_of, BF), V(rows_of, BF),
            V(rows_of, BF), V(rows_of, BF), V((fsdp, 8, 128), F32), V((8, 128), F32), V((8, D), F32), V((3, L, D), BF), V((L, L), F32),
            V((HEADS, 1, L), F32), V((L, D), BF), V((L, D), F32), V((L, D), BF), V((L, D), F32), V((L, 128), F32),
            V((L, FF), BF), V((L, FF), BF), V((L, FF), BF), V((L, D), F32), V((L, D), BF), V((D, L), BF),
            V(rows_of, BF), V((8, D), F32), V((total, 8, 128), F32), V((total, 8, 128), F32),
            *Scatter.buffers(Z, rows), *Gather.sems(Z), *Scatter.sems(), T((6,)), T((6,)), T((6,)), T,
        ],
        compiler_params=pltpu.CompilerParams(collective_id=0, has_side_effects=True, vmem_limit_bytes=VMEM_LIMIT),
        name="layer",
    )(order, seq_lengths, slopes, tokens_in.reshape(rows_of), out_grad.reshape(rows_of), *small, w_qkv, w_out, w_gate_up, w_down)
    output, input_grad, gq, gw, gg, gd, *mine = pl.pallas_call(
        hand_over,
        out_shape=[S(r.shape, r.dtype) for r in results[:6]] + [S((1, rows), F32)] * 8,
        in_specs=[hbm] * 6 + [vmem],
        out_specs=[hbm] * 6 + [vmem] * 8,
        scratch_shapes=[V(r.shape, r.dtype) for r in results[:6]] + [T((2, 6))],
        name="hand_over",
    )(*results)
    mine = [v.reshape(rows) for v in mine]
    return (
        output.reshape(tokens_in.shape), input_grad.reshape(tokens_in.shape), gq, mine[BQ], mine[BV], gw, mine[BO],
        mine[G1], mine[B1], gg, gd, mine[BD], mine[G2], mine[B2],
    )


def solution(mesh):
    fsdp = mesh.shape["fsdp"]
    rows = D // fsdp
    kernels = mesh.shape["ctx"] == M and fsdp == 16 and rows % 16 == 0
    return jax.shard_map(
        per_device if kernels else per_device_plain,
        mesh=mesh,
        in_specs=(
            P(None, None, ("ctx", "fsdp"), None),
            P(None, None, ("ctx", "fsdp"), None),
            P(),
            P(),
            P("fsdp", None),
            P("fsdp"),
            P("fsdp"),
            P("fsdp", None),
            P("fsdp"),
            P("fsdp"),
            P("fsdp"),
            P("fsdp", None),
            P("fsdp", None),
            P("fsdp"),
            P("fsdp"),
            P("fsdp"),
        ),
        out_specs=(
            P(None, None, ("ctx", "fsdp"), None),
            P(None, None, ("ctx", "fsdp"), None),
            P("fsdp", None),
            P("fsdp"),
            P("fsdp"),
            P("fsdp", None),
            P("fsdp"),
            P("fsdp"),
            P("fsdp"),
            P("fsdp", None),
            P("fsdp", None),
            P("fsdp"),
            P("fsdp"),
            P("fsdp"),
        ),
        check_vma=False,
    )
```

```python
import functools
import math

import jax
import jax.numpy as jnp
from jax import lax
from jax.experimental import pallas as pl
from jax.experimental.pallas import tpu as pltpu
from jax.sharding import PartitionSpec as P

D = 768
HEADS = 12
HEAD_DIM = 64
FF = 3072
M = 2
EPSILON = 1e-12
NEGATIVE = -1e30
MESH = pl.DeviceIdType.MESH
BF = jnp.bfloat16
F32 = jnp.float32
LOG2E = math.log2(math.e)
VMEM_LIMIT = 62 << 20


def slope_list(head_count):

    def powers(number):
        anchor = 2.0 ** (-(2.0 ** (-(math.log2(number) - 3))))
        return [anchor ** (power_index + 1) for power_index in range(number)]

    closest = 2 ** int(math.floor(math.log2(head_count)))
    return powers(closest) + powers(2 * closest)[0::2][: head_count - closest]


def layer_norm(inputs, gain_row, offset_row):
    centre = inputs - jnp.mean(inputs, axis=-1, keepdims=True)
    spread = jnp.mean(centre * centre, axis=-1, keepdims=True)
    return centre * lax.rsqrt(spread + EPSILON) * gain_row + offset_row


def gated_unit(gate_up):
    return jax.nn.gelu(gate_up[:, :FF], approximate=False) * gate_up[:, FF:]


def rows_product(former, latter):
    return lax.dot_general(
        former, latter, (((0,), (0,)), ((), ())), preferred_element_type=jnp.float32
    )


def by_transpose(former, latter):
    return lax.dot_general(
        former, latter, (((1,), (1,)), ((), ())), preferred_element_type=jnp.float32
    )


def plain_product(former, latter):
    return jnp.dot(former, latter, preferred_element_type=jnp.float32)


def masked_scores(heads_q, heads_k, position, key_place, length, slopes):
    raw_scores = (
        jnp.einsum("qhd,khd->hqk", heads_q, heads_k, preferred_element_type=jnp.float32) * 0.125
    )
    distance = jnp.abs(position[:, None] - key_place[None, :]).astype(jnp.float32)
    raw_scores = raw_scores - slopes[:, None, None] * distance[None]
    return jnp.where((key_place < length)[None, None, :], raw_scores, NEGATIVE)


def fetch_weights(shards):
    return (
        lax.all_gather(shards[0], "fsdp", axis=0, tiled=True),
        lax.all_gather(shards[1], "fsdp", axis=0, tiled=True),
        lax.all_gather(shards[2], "fsdp", axis=0, tiled=True),
        lax.all_gather(shards[3], "fsdp", axis=0, tiled=True),
        lax.all_gather(shards[4], "fsdp", axis=0, tiled=True),
        lax.all_gather(shards[5], "fsdp", axis=0, tiled=True),
        lax.all_gather(shards[6], "fsdp", axis=0, tiled=True),
        lax.all_gather(shards[7], "fsdp", axis=0, tiled=True),
        lax.all_gather(shards[8], "fsdp", axis=0, tiled=True),
        lax.all_gather(shards[9], "fsdp", axis=0, tiled=True),
        lax.all_gather(shards[10], "fsdp", axis=0, tiled=True),
        lax.all_gather(shards[11], "fsdp", axis=0, tiled=True),
    )


def reduce_grads(grad_terms):
    shard_sums = (
        lax.psum_scatter(grad_terms[0], "fsdp", scatter_dimension=0, tiled=True),
        lax.psum_scatter(grad_terms[1], "fsdp", scatter_dimension=0, tiled=True),
        lax.psum_scatter(grad_terms[2], "fsdp", scatter_dimension=0, tiled=True),
        lax.psum_scatter(grad_terms[3], "fsdp", scatter_dimension=0, tiled=True),
        lax.psum_scatter(grad_terms[4], "fsdp", scatter_dimension=0, tiled=True),
        lax.psum_scatter(grad_terms[5], "fsdp", scatter_dimension=0, tiled=True),
        lax.psum_scatter(grad_terms[6], "fsdp", scatter_dimension=0, tiled=True),
        lax.psum_scatter(grad_terms[7], "fsdp", scatter_dimension=0, tiled=True),
        lax.psum_scatter(grad_terms[8], "fsdp", scatter_dimension=0, tiled=True),
        lax.psum_scatter(grad_terms[9], "fsdp", scatter_dimension=0, tiled=True),
        lax.psum_scatter(grad_terms[10], "fsdp", scatter_dimension=0, tiled=True),
        lax.psum_scatter(grad_terms[11], "fsdp", scatter_dimension=0, tiled=True),
    )
    return (
        lax.psum(shard_sums[0].astype(jnp.bfloat16), "ctx").astype(jnp.float32),
        lax.psum(shard_sums[1].astype(jnp.bfloat16), "ctx").astype(jnp.float32),
        lax.psum(shard_sums[2].astype(jnp.bfloat16), "ctx").astype(jnp.float32),
        lax.psum(shard_sums[3].astype(jnp.bfloat16), "ctx").astype(jnp.float32),
        lax.psum(shard_sums[4].astype(jnp.bfloat16), "ctx").astype(jnp.float32),
        lax.psum(shard_sums[5].astype(jnp.bfloat16), "ctx").astype(jnp.float32),
        lax.psum(shard_sums[6].astype(jnp.bfloat16), "ctx").astype(jnp.float32),
        lax.psum(shard_sums[7].astype(jnp.bfloat16), "ctx").astype(jnp.float32),
        lax.psum(shard_sums[8].astype(jnp.bfloat16), "ctx").astype(jnp.float32),
        lax.psum(shard_sums[9].astype(jnp.bfloat16), "ctx").astype(jnp.float32),
        lax.psum(shard_sums[10].astype(jnp.bfloat16), "ctx").astype(jnp.float32),
        lax.psum(shard_sums[11].astype(jnp.bfloat16), "ctx").astype(jnp.float32),
    )


def per_device_plain(
    tokens_in,
    out_grad,
    seq_lengths,
    order,
    w_qkv,
    bias_q,
    bias_v,
    w_out,
    bias_out,
    ln1_gain,
    ln1_bias,
    w_gate_up,
    w_down,
    bias_down,
    ln2_gain,
    ln2_bias,
):
    shards = (
        w_qkv,
        bias_q,
        bias_v,
        w_out,
        bias_out,
        ln1_gain,
        ln1_bias,
        w_gate_up,
        w_down,
        bias_down,
        ln2_gain,
        ln2_bias,
    )
    group_index = lax.axis_index("fsdp")
    ctx_index = lax.axis_index("ctx")
    dealt_tokens = jnp.take_along_axis(tokens_in, order[:, :, None, None], axis=1)
    tokens_grp, grads_grp = (
        lax.all_to_all(dealt_tokens, "fsdp", split_axis=1, concat_axis=2, tiled=True),
        lax.all_to_all(out_grad, "fsdp", split_axis=1, concat_axis=2, tiled=True),
    )
    dealt_lengths = jnp.take_along_axis(seq_lengths, order, axis=1)
    local_rows = tokens_grp.shape[2]
    key_place = jnp.arange(local_rows * lax.axis_size("ctx"))
    position = ctx_index * local_rows + jnp.arange(local_rows)
    slopes = jnp.array(slope_list(HEADS), jnp.float32)
    output_list = []
    input_list = []
    running = None
    for micro_batch in range(M):
        weights = fetch_weights(shards)
        (
            full_qkv,
            full_bias_q,
            full_bias_v,
            full_out,
            full_bias_out,
            full_ln1_gain,
            full_ln1_bias,
            full_gate_up,
            full_down,
            full_bias_down,
            full_ln2_gain,
            full_ln2_bias,
        ) = weights
        tokens = tokens_grp[micro_batch, 0]
        cotangent = grads_grp[micro_batch, 0]
        length = lax.dynamic_index_in_dim(
            dealt_lengths[micro_batch], group_index, 0, keepdims=False
        )
        valid_rows = position < length
        projected = plain_product(tokens, full_qkv)
        queries = (projected[:, :D] + full_bias_q.astype(jnp.float32)).astype(jnp.bfloat16)
        key_rows = projected[:, D : 2 * D].astype(jnp.bfloat16)
        values = (projected[:, 2 * D :] + full_bias_v.astype(jnp.float32)).astype(jnp.bfloat16)
        keys_all, values_all = (
            lax.all_gather(key_rows, "ctx", axis=0, tiled=True),
            lax.all_gather(values, "ctx", axis=0, tiled=True),
        )
        heads_q = queries.reshape(local_rows, HEADS, HEAD_DIM)
        heads_k = keys_all.reshape(-1, HEADS, HEAD_DIM)
        heads_v = values_all.reshape(-1, HEADS, HEAD_DIM)
        scores = masked_scores(heads_q, heads_k, position, key_place, length, slopes)
        row_max = jnp.max(scores, axis=-1, keepdims=True)
        exp_terms = jnp.exp(scores - row_max)
        row_total = jnp.sum(exp_terms, axis=-1, keepdims=True)
        log_total = row_max + jnp.log(row_total)
        attn_probs = (exp_terms / row_total).astype(jnp.bfloat16)
        context = (
            jnp.einsum("hqk,khd->qhd", attn_probs, heads_v, preferred_element_type=jnp.float32)
            .reshape(local_rows, D)
            .astype(jnp.bfloat16)
        )
        attn_out = plain_product(context, full_out) + full_bias_out.astype(jnp.float32)
        first_sum = tokens.astype(jnp.float32) + attn_out
        normed_one, norm_one_pull = jax.vjp(
            layer_norm,
            first_sum,
            full_ln1_gain.astype(jnp.float32),
            full_ln1_bias.astype(jnp.float32),
        )
        normed_low = normed_one.astype(jnp.bfloat16)
        gate_up = plain_product(normed_low, full_gate_up)
        hidden, gated_pull = jax.vjp(gated_unit, gate_up)
        hidden_low = hidden.astype(jnp.bfloat16)
        branch = plain_product(hidden_low, full_down) + full_bias_down.astype(jnp.float32)
        result, norm_two_pull = jax.vjp(
            layer_norm,
            normed_one + branch,
            full_ln2_gain.astype(jnp.float32),
            full_ln2_bias.astype(jnp.float32),
        )
        output_list.append(jnp.where(valid_rows[:, None], result, 0.0).astype(jnp.bfloat16))
        grad_result = jnp.where(valid_rows[:, None], cotangent.astype(jnp.float32), 0.0)
        grad_second, grad_ln2_gain, grad_ln2_bias = norm_two_pull(grad_result)
        grad_branch = grad_second.astype(jnp.bfloat16)
        grad_bias_down = jnp.sum(grad_branch.astype(jnp.float32), axis=0)
        grad_w_down = rows_product(hidden_low, grad_branch)
        grad_hidden = by_transpose(grad_branch, full_down)
        (grad_gate_up,) = gated_pull(grad_hidden)
        grad_gate_low = grad_gate_up.astype(jnp.bfloat16)
        grad_w_gate_up = rows_product(normed_low, grad_gate_low)
        grad_normed = grad_second + by_transpose(grad_gate_low, full_gate_up)
        grad_first, grad_ln1_gain, grad_ln1_bias = norm_one_pull(grad_normed)
        grad_attn = grad_first.astype(jnp.bfloat16)
        grad_bias_out = jnp.sum(grad_attn.astype(jnp.float32), axis=0)
        grad_w_out = rows_product(context, grad_attn)
        grad_context = (
            by_transpose(grad_attn, full_out)
            .astype(jnp.bfloat16)
            .reshape(local_rows, HEADS, HEAD_DIM)
        )
        scores = masked_scores(heads_q, heads_k, position, key_place, length, slopes)
        attn_exact = jnp.exp(scores - log_total)
        grad_values_term = jnp.einsum(
            "hqk,qhd->khd",
            attn_exact.astype(jnp.bfloat16),
            grad_context,
            preferred_element_type=jnp.float32,
        )
        grad_probs = jnp.einsum(
            "qhd,khd->hqk", grad_context, heads_v, preferred_element_type=jnp.float32
        )
        grad_scores = (
            attn_exact * (grad_probs - jnp.sum(attn_exact * grad_probs, axis=-1, keepdims=True))
        ).astype(jnp.bfloat16)
        grad_queries = (
            jnp.einsum("hqk,khd->qhd", grad_scores, heads_k, preferred_element_type=jnp.float32)
            * 0.125
        ).reshape(local_rows, D)
        grad_keys_term = (
            jnp.einsum("hqk,qhd->khd", grad_scores, heads_q, preferred_element_type=jnp.float32)
            * 0.125
        )
        grad_keys, grad_values = (
            lax.psum_scatter(
                grad_keys_term.reshape(-1, D).astype(jnp.bfloat16),
                "ctx",
                scatter_dimension=0,
                tiled=True,
            ).astype(jnp.float32),
            lax.psum_scatter(
                grad_values_term.reshape(-1, D).astype(jnp.bfloat16),
                "ctx",
                scatter_dimension=0,
                tiled=True,
            ).astype(jnp.float32),
        )
        grad_qkv = jnp.concatenate(
            [
                grad_queries.astype(jnp.bfloat16),
                grad_keys.astype(jnp.bfloat16),
                grad_values.astype(jnp.bfloat16),
            ],
            axis=1,
        )
        grad_w_qkv = rows_product(tokens, grad_qkv)
        grad_bias_q = jnp.sum(grad_qkv[:, :D].astype(jnp.float32), axis=0)
        grad_bias_v = jnp.sum(grad_qkv[:, 2 * D :].astype(jnp.float32), axis=0)
        grad_tokens = grad_first + by_transpose(grad_qkv, full_qkv)
        input_list.append(grad_tokens.astype(jnp.bfloat16))
        grad_terms = (
            grad_w_qkv,
            grad_bias_q,
            grad_bias_v,
            grad_w_out,
            grad_bias_out,
            grad_ln1_gain,
            grad_ln1_bias,
            grad_w_gate_up,
            grad_w_down,
            grad_bias_down,
            grad_ln2_gain,
            grad_ln2_bias,
        )
        reduced = reduce_grads(grad_terms)
        if micro_batch == 0:
            running = reduced
        else:
            running = tuple((left_sum + right_sum for left_sum, right_sum in zip(running, reduced)))
    output_stack = jnp.stack(output_list, axis=0)[:, None]
    input_stack = jnp.stack(input_list, axis=0)[:, None]
    output, dealt_grads = (
        lax.all_to_all(output_stack, "fsdp", split_axis=2, concat_axis=1, tiled=True),
        lax.all_to_all(input_stack, "fsdp", split_axis=2, concat_axis=1, tiled=True),
    )
    inverse = jnp.argsort(order, axis=1)
    input_grad = jnp.take_along_axis(dealt_grads, inverse[:, :, None, None], axis=1)
    return (
        output,
        input_grad,
        running[0],
        running[1],
        running[2],
        running[3],
        running[4],
        running[5],
        running[6],
        running[7],
        running[8],
        running[9],
        running[10],
        running[11],
    )


PIECES = 16
RING = 4


def whole(p, w=256):
    return [(p, 0, D, w)]


GATHER_UNITS = sum([whole(p, 0 if p == 15 else 384 if p in (6, 10) else 256) for p in range(PIECES)], [])
SCATTER_UNITS = sum([whole(p, 256 if i % 4 else 128) for i, p in enumerate([*range(4, 16), 3, 0, 1, 2])], [])
STAGES = ()
SETTLE = 4
AHEAD = 1
ROW_AT = 4
PLANE_AT = 6
CORE_AT = 7
X_AT = (0, 7)
G_AT = (7, 9)
O_AT = (0, 8)
O_FIRST = True
D_AT = (13, 7)


def mm(a, b):
    return jnp.dot(a, b, preferred_element_type=F32)


def mm_nt(a, b):
    return lax.dot_general(a, b, (((1,), (1,)), ((), ())), preferred_element_type=F32)


def mm_tn(a, b):
    return lax.dot_general(a, b, (((0,), (0,)), ((), ())), preferred_element_type=F32)


def block(i, size):
    if isinstance(i, int):
        return pl.ds(i * size, size)
    return pl.ds(pl.multiple_of(i * size, size), size)


class Place:
    def __init__(self, fsdp):
        self.fsdp = fsdp
        self.total = 2 * fsdp
        self.Z = fsdp // 4
        self.x = lax.axis_index("ctx")
        self.f = lax.axis_index("fsdp")
        self.z = self.f // 4
        self.y = lax.rem(self.f // 2, 2)
        self.c = lax.rem(self.f, 2)
        self.me = self.x * fsdp + self.f
        self.pending = []
        self.turn = 0

    def dev(self, x=None, z=None, y=None, c=None):
        x = self.x if x is None else x
        z = self.z if z is None else z
        y = self.y if y is None else y
        c = self.c if c is None else c
        return (x, z * 4 + y * 2 + c)

    def cols(self, unit):
        p, lo, n, w = unit
        return pl.ds(pl.multiple_of(lo + self.x * w, 128), n - w)

    def give(self, unit):
        p, lo, n, w = unit
        return pl.ds(pl.multiple_of(lo + self.x * (n - w), 128), w)

    def take(self, unit):
        p, lo, n, w = unit
        return pl.ds(pl.multiple_of(lo + (1 - self.x) * (n - w), 128), w)

    def at(self, d):
        return (d // self.fsdp, lax.rem(d, self.fsdp))

    def signal(self):
        sem = pltpu.get_barrier_semaphore()

        @pl.loop(1, self.total)
        def _(k):
            d = lax.rem(self.me + k, self.total)
            pl.semaphore_signal(sem, inc=1, device_id=self.at(d), device_id_type=MESH)

    def wait(self):
        pl.semaphore_wait(pltpu.get_barrier_semaphore(), self.total - 1)

    def go(self, copy, cond=None):
        if cond is None:
            copy.start()
        else:
            pl.when(cond)(copy.start)
        self.pending.append((self.turn, cond, copy))

    def finish(self, before=None):
        left = []
        for turn, cond, copy in self.pending:
            if before is not None and turn >= before:
                left.append((turn, cond, copy))
            elif cond is None:
                copy.wait_send()
            else:
                pl.when(cond)(copy.wait_send)
        self.pending = left


def remote(src, dst, send, recv, device):
    return pltpu.make_async_remote_copy(
        src_ref=src, dst_ref=dst, send_sem=send, recv_sem=recv, device_id=device, device_id_type=MESH
    )


class Exchange:
    def __init__(self, pc, src, dst, sems, k):
        self.pc, self.src, self.dst = pc, src, dst
        self.send, self.recv, self.local = sems[0].at[k], sems[1].at[k], sems[2].at[k]

    def own(self):
        return pltpu.make_async_copy(self.src.at[self.pc.me], self.dst.at[self.pc.me], self.local)

    def start(self, turn=0, turns=1):
        pc = self.pc
        if turn == 0:
            self.own().start()
        near = [(x, 0, y, c) for x in range(2) for y in range(2) for c in range(2) if x + y + c]
        far = [(x, z, y, c) for x in range(2) for y in range(2) for c in range(2) for z in (2, 3, 1)]
        if turns > 1:
            per = -(-len(far) // (turns - 1))
            picked = far[(turn - 1) * per : turn * per] if turn else near
        else:
            picked = near + far
        for x, z, y, c in picked:
            to = pc.dev(
                x=(1 - pc.x) if x else None,
                y=(1 - pc.y) if y else None,
                c=(1 - pc.c) if c else None,
                z=(None, pc.z + 1 - 2 * lax.rem(pc.z, 2), lax.rem(pc.z + 2, 4), 3 - pc.z)[z],
            )
            d = to[0] * pc.fsdp + to[1]
            remote(self.src.at[d], self.dst.at[pc.me], self.send, self.recv, to).start()

    def whole(self):
        blocks = pl.ds(0, self.pc.total - 1)
        return remote(self.src.at[blocks], self.dst.at[blocks], self.send, self.recv, self.pc.dev(c=1 - self.pc.c))

    def wait(self):
        self.own().wait()
        self.whole().wait_recv()

    def done(self):
        self.whole().wait_send()


class Gather:
    def __init__(self, pc, own, slots, sems):
        self.pc, self.own = pc, own
        self.place = slots
        self.zs, self.zr, self.ys, self.yr, self.xs, self.xr, self.cs, self.cr, self.ls = sems

    @staticmethod
    def sems(Z):
        T = pltpu.SemaphoreType.DMA
        n = len(GATHER_UNITS)
        return [
            T((n, 2 * Z - 2)), T((n, 2 * Z - 2)), T((n, 2 * Z - 1)), T((n,)),
            T((n, 2 * Z - 1)), T((n, 2 * Z - 1)), T((n, 2)), T((n, 2)), T((n,)),
        ]

    def up(self):
        return jnp.minimum(self.pc.z + 1, self.pc.Z - 1)

    def down(self):
        return jnp.maximum(self.pc.z - 1, 0)

    def slots(self, u, z, y, cols):
        return self.place(GATHER_UNITS[u][0], z, y, self.pc.c, cols)

    def cols(self, u):
        return self.pc.cols(GATHER_UNITS[u])

    def mine(self, u):
        pc = self.pc
        p, lo, n, w = GATHER_UNITS[u]
        return pltpu.make_async_copy(self.own(p, pl.ds(lo, n)), self.slots(u, pc.z, pc.y, pl.ds(lo, n)), self.ls.at[u])

    def start(self, u):
        pc = self.pc
        Z = pc.Z
        src = self.own(GATHER_UNITS[u][0], self.cols(u))
        dst = self.slots(u, pc.z, pc.y, self.cols(u))
        self.mine(u).start()
        pc.go(remote(src, dst, self.zs.at[u, 0], self.zr.at[u, 0], pc.dev(z=self.up())), pc.z < Z - 1)
        k = Z - 1
        pc.go(remote(src, dst, self.zs.at[u, k], self.zr.at[u, k], pc.dev(z=self.down())), pc.z > 0)
        pc.go(remote(src, dst, self.ys.at[u, 0], self.yr.at[u], pc.dev(y=1 - pc.y)))

    def hops(self, h):
        pc = self.pc
        Z = pc.Z
        return (
            (jnp.maximum(pc.z - h, 0), pc.z >= h, pc.z < Z - 1, self.up(), h - 1),
            (jnp.minimum(pc.z + h, Z - 1), pc.z + h < Z, pc.z > 0, self.down(), Z + h - 2),
        )

    def hop(self, u, h):
        pc = self.pc
        for z, here, onward, to, k in self.hops(h):
            ref = self.slots(u, z, pc.y, self.cols(u))
            pl.when(here)(remote(ref, ref, self.zs.at[u, k], self.zr.at[u, k], pc.dev(z=to)).wait_recv)
            if h < pc.Z - 1:
                pc.go(
                    remote(ref, ref, self.zs.at[u, k + 1], self.zr.at[u, k + 1], pc.dev(z=to)),
                    jnp.logical_and(here, onward),
                )
            pc.go(remote(ref, ref, self.ys.at[u, 1 + k], self.yr.at[u], pc.dev(y=1 - pc.y)), here)
            if GATHER_UNITS[u][3]:
                ref = self.slots(u, z, pc.y, pc.give(GATHER_UNITS[u]))
                pc.go(remote(ref, ref, self.xs.at[u, k], self.xr.at[u, k], pc.dev(x=1 - pc.x)), here)

    def row(self, u):
        pc = self.pc
        unit = GATHER_UNITS[u]
        ref = self.slots(u, slice(None), 1 - pc.y, self.cols(u))
        remote(ref, ref, self.ys.at[u, 0], self.yr.at[u], pc.dev(y=1 - pc.y)).wait_recv()
        if unit[3]:
            k = 2 * pc.Z - 2
            ref = self.slots(u, slice(None), 1 - pc.y, pc.give(unit))
            pc.go(remote(ref, ref, self.xs.at[u, k], self.xr.at[u, k], pc.dev(x=1 - pc.x)))
        self.mine(u).wait()
        ref = self.slots(u, slice(None), slice(None), self.cols(u))
        pc.go(remote(ref, ref, self.cs.at[u, 0], self.cr.at[u, 0], pc.dev(c=1 - pc.c)))

    def plane(self, u):
        pc = self.pc
        unit = GATHER_UNITS[u]
        if not unit[3]:
            return
        take = pc.take(unit)
        for h in range(1, pc.Z):
            for z, here, onward, to, k in self.hops(h):
                ref = self.slots(u, z, pc.y, take)
                pl.when(here)(remote(ref, ref, self.xs.at[u, k], self.xr.at[u, k], pc.dev(x=1 - pc.x)).wait_recv)
        k = 2 * pc.Z - 2
        ref = self.slots(u, slice(None), 1 - pc.y, take)
        remote(ref, ref, self.xs.at[u, k], self.xr.at[u, k], pc.dev(x=1 - pc.x)).wait_recv()
        ref = self.slots(u, slice(None), slice(None), take)
        pc.go(remote(ref, ref, self.cs.at[u, 1], self.cr.at[u, 1], pc.dev(c=1 - pc.c)))

    def core(self, u):
        pc = self.pc
        parts = [pc.cols(GATHER_UNITS[u])] + ([pc.take(GATHER_UNITS[u])] if GATHER_UNITS[u][3] else [])
        for k, cols in enumerate(parts):
            ref = self.place(GATHER_UNITS[u][0], slice(None), slice(None), 1 - pc.c, cols)
            remote(ref, ref, self.cs.at[u, k], self.cr.at[u, k], pc.dev(c=1 - pc.c)).wait_recv()


class Scatter:
    def __init__(self, pc, terms, get, put, from_c, from_x, from_y, from_z, from_f, sems):
        self.pc, self.terms, self.get, self.put = pc, terms, get, put
        self.from_c, self.from_x, self.from_y, self.from_z, self.from_f = from_c, from_x, from_y, from_z, from_f
        self.cs, self.cr, self.xs, self.xr, self.ys, self.yr, self.zs, self.zr, self.fs, self.fr, self.free = sems
        z = pc.z
        self.inner = jnp.logical_or(z == 1, z == 2)
        self.outer = jnp.logical_not(self.inner)
        self.mate = z + 1 - 2 * lax.rem(z, 2)
        self.far_in = jnp.where(z < 2, 2, 1)
        self.far_out = jnp.where(z < 2, 3, 0)
        self.x_lo, self.y_lo = [], []
        used = {}
        for p, lo, n, w in SCATTER_UNITS:
            a, b = used.get(p, (0, 0))
            self.x_lo.append(a)
            self.y_lo.append(b)
            used[p] = (a + w, b + n - w)

    @staticmethod
    def sems():
        T = pltpu.SemaphoreType.DMA
        n = len(SCATTER_UNITS)
        return [
            T((n,)), T((n,)), T((n,)), T((n,)), T((n,)), T((n,)), T((n, 5)), T((n, 4)), T((n,)), T((n,)),
            pltpu.SemaphoreType.REGULAR((n,)),
        ]

    @staticmethod
    def buffers(Z, rows):
        n = PIECES
        give, win = [0] * n, [0] * n
        for p, lo, k, w in SCATTER_UNITS:
            give[p] += w
            win[p] += k - w
        give, win = max(give), max(win)
        return [
            pltpu.VMEM((RING, Z, 2, rows, D), BF),
            pltpu.VMEM((n, Z, 2, rows, give), BF),
            pltpu.VMEM((n, Z, rows, win), BF),
            pltpu.VMEM((n, 4, rows, win), BF),
            pltpu.VMEM((n, rows, win), BF),
        ]

    def x_at(self, u):
        return pl.ds(self.x_lo[u], SCATTER_UNITS[u][3])

    def y_at(self, u):
        p, lo, n, w = SCATTER_UNITS[u]
        return pl.ds(self.y_lo[u], n - w)

    def add(self, u, z, y, cols, value):
        p = SCATTER_UNITS[u][0]
        c = self.pc.c
        self.put(p, z, y, c, cols, self.get(p, z, y, c, cols) + value)

    def part(self, u, z, y, cols):
        return self.terms(SCATTER_UNITS[u][0], z, y, self.pc.c, cols)

    def start(self, u):
        pc = self.pc
        p, lo, n, w = SCATTER_UNITS[u]
        if u >= RING:
            pl.semaphore_wait(self.free.at[u], 1)
        src = self.terms(p, slice(None), slice(None), 1 - pc.c, pl.ds(lo, n))
        dst = self.from_c.at[u % RING, :, :, :, pl.ds(0, n)]
        pc.go(remote(src, dst, self.cs.at[u], self.cr.at[u], pc.dev(c=1 - pc.c)))

    def core(self, u):
        pc = self.pc
        p, lo, n, w = SCATTER_UNITS[u]
        ref = self.from_c.at[u % RING, :, :, :, pl.ds(0, n)]
        remote(ref, ref, self.cs.at[u], self.cr.at[u], pc.dev(c=1 - pc.c)).wait_recv()
        for z in range(pc.Z):
            for y in range(2):
                self.add(u, z, y, pl.ds(lo, n), self.from_c[u % RING, z, y, :, pl.ds(0, n)])
        if u + RING < len(SCATTER_UNITS):
            pl.semaphore_signal(self.free.at[u + RING], inc=1, device_id=pc.dev(c=1 - pc.c), device_id_type=MESH)
        if w:
            src = self.part(u, slice(None), slice(None), pc.take(SCATTER_UNITS[u]))
            dst = self.from_x.at[p, :, :, :, self.x_at(u)]
            pc.go(remote(src, dst, self.xs.at[u], self.xr.at[u], pc.dev(x=1 - pc.x)))
        else:
            self.across(u)

    def plane(self, u):
        pc = self.pc
        p, lo, n, w = SCATTER_UNITS[u]
        if w:
            ref = self.from_x.at[p, :, :, :, self.x_at(u)]
            remote(ref, ref, self.xs.at[u], self.xr.at[u], pc.dev(x=1 - pc.x)).wait_recv()
            for z in range(pc.Z):
                for y in range(2):
                    self.add(u, z, y, pc.give(SCATTER_UNITS[u]), self.from_x[p, z, y, :, self.x_at(u)])
            self.across(u)

    def across(self, u):
        pc = self.pc
        src = self.part(u, slice(None), 1 - pc.y, pc.cols(SCATTER_UNITS[u]))
        dst = self.from_y.at[SCATTER_UNITS[u][0], :, :, self.y_at(u)]
        pc.go(remote(src, dst, self.ys.at[u], self.yr.at[u], pc.dev(y=1 - pc.y)))

    def z_ref(self, u, k):
        return self.from_z.at[SCATTER_UNITS[u][0], k, :, self.y_at(u)]

    def z_add(self, u, k, z):
        ref = self.z_ref(u, k)
        remote(ref, ref, self.zs.at[u, k], self.zr.at[u, k], self.pc.dev(z=self.mate)).wait_recv()
        value = self.from_z[SCATTER_UNITS[u][0], k, :, self.y_at(u)]
        self.add(u, z, self.pc.y, self.pc.cols(SCATTER_UNITS[u]), value)

    def row(self, u):
        pc = self.pc
        p = SCATTER_UNITS[u][0]
        cols = pc.cols(SCATTER_UNITS[u])
        ref = self.from_y.at[p, :, :, self.y_at(u)]
        remote(ref, ref, self.ys.at[u], self.yr.at[u], pc.dev(y=1 - pc.y)).wait_recv()
        for z in range(pc.Z):
            self.add(u, z, pc.y, cols, self.from_y[p, z, :, self.y_at(u)])
        for k, z in enumerate((self.mate, self.far_in, self.far_out)):
            copy = remote(
                self.part(u, z, pc.y, cols), self.z_ref(u, k), self.zs.at[u, k], self.zr.at[u, k], pc.dev(z=self.mate)
            )
            pc.go(copy, self.outer if k else None)

    def middle(self, u):
        pc = self.pc
        cols = pc.cols(SCATTER_UNITS[u])
        far = ((1, self.far_in), (2, self.far_out))

        @pl.when(self.inner)
        def _():
            for k, z in far:
                self.z_add(u, k, z)

        for k, z in far:
            src = self.part(u, z, pc.y, cols)
            pc.go(remote(src, self.z_ref(u, 3), self.zs.at[u, 2 + k], self.zr.at[u, 3], pc.dev(z=z)), self.inner)

    def f_ref(self, u):
        return self.from_f.at[SCATTER_UNITS[u][0], :, self.y_at(u)]

    def line(self, u):
        pc = self.pc
        for k in (0, 3):
            self.z_add(u, k, pc.z)
        src = self.part(u, pc.z, pc.y, pc.cols(SCATTER_UNITS[u]))
        pc.go(remote(src, self.f_ref(u), self.fs.at[u], self.fr.at[u], pc.dev(x=1 - pc.x)))

    def last(self, u, out):
        pc = self.pc
        unit = p, lo, n, w = SCATTER_UNITS[u]
        ref = self.f_ref(u)
        remote(ref, ref, self.fs.at[u], self.fr.at[u], pc.dev(x=1 - pc.x)).wait_recv()
        at = self.y_lo[u]

        def own(cols):
            return self.get(p, pc.z, pc.y, pc.c, cols).astype(F32)

        if w:
            out[:, pc.give(unit)] = own(pc.give(unit))
            theirs = pl.ds(pl.multiple_of(at + (1 - pc.x) * (n - 2 * w), 128), w)
            out[:, pc.take(unit)] = self.from_f[p, :, theirs].astype(F32)
        if n > 2 * w:
            both = pl.ds(pl.multiple_of(at + pc.x * w, 128), n - 2 * w)
            shared = pl.ds(lo + w, n - 2 * w)
            out[:, shared] = own(shared) + self.from_f[p, :, both].astype(F32)


def row_mean(v):
    return jnp.sum(v, axis=-1, keepdims=True) * (1.0 / D)


BQ, BV, BO, G1, B1, BD, G2, B2 = range(8)


def layer_kernel(
    fsdp, rows,
    order, lengths, slopes, tokens_in, grads_in, *refs,
):
    small_in, (wq_in, wo_in, wg_in, wd_in) = refs[:8], refs[8:12]
    OUT, DX, GQ, GW, GG, GD, SMALLG, *refs = refs[12:]
    (
    wa, wd, raw, outv, xs, gs, small, small_own, smallf, qkv, dist, lse, ctxt, y1, y1b, xhat, rstd, act, slope_up, zed, acc, dfb, tr,
    dxr, sgrad, sparts, gsum, from_c, from_x, from_y, from_z, from_f, *sems,
    ) = refs
    pc = Place(fsdp)
    Z = pc.Z
    L = pc.total * raw.shape[1]
    gsems, ssems, esems, rsem = sems[:9], sems[9:20], sems[20:23], sems[23]
    w_pc = wa.shape[1:]

    def own(p, cols):
        if p < 3:
            return wq_in.at[:, pl.ds(pl.multiple_of(D * p + cols.start, 128), cols.size)]
        if p == 3:
            return wo_in.at[:, cols]
        if p < 12:
            i, j = (p - 4) // 2, (p - 4) % 2
            return wg_in.at[:, pl.ds(pl.multiple_of(FF * j + D * i + cols.start, 128), cols.size)]
        return wd_in.at[pl.ds(rows * (p - 12), rows), cols]

    def slots(p, z, y, c, cols):
        if p < 12:
            return wa.at[p, z, y, c, :, cols]
        return wd.at[z, y, c, p - 12, :, cols]

    def get(p, z, y, c, cols):
        if p < 12:
            return wa[p, z, y, c, :, cols]
        return wd[z, y, c, p - 12, :, cols]

    def put(p, z, y, c, cols, value):
        if p < 12:
            wa[p, z, y, c, :, cols] = value
        else:
            wd[z, y, c, p - 12, :, cols] = value

    def out_of(p):
        if p >= 12:
            return GD.at[pl.ds(rows * (p - 12), rows)]
        if p == 3:
            return GW
        if p < 3:
            return GQ.at[:, pl.ds(D * p, D)]
        i, j = (p - 4) // 2, (p - 4) % 2
        return GG.at[:, pl.ds(FF * j + D * i, D)]

    def w_cols(p, cols):
        return wa[p, :, :, :, :, cols].reshape(D, cols.size)

    def w_all(p):
        return wa[p].reshape(D, D)

    g = Gather(pc, own, slots, gsems)
    sc = Scatter(pc, slots, get, put, from_c, from_x, from_y, from_z, from_f, ssems)
    ex_x = Exchange(pc, outv, xs, esems, 0)
    ex_g = Exchange(pc, grads_in, gs, esems, 1)
    ex_o = Exchange(pc, outv, OUT, esems, 3)
    ex_d = Exchange(pc, raw, dxr, esems, 4)
    ex_s = Exchange(pc, sparts, gsum, esems, 5)
    len_s = lengths[pc.x, order[pc.x, pc.f]]

    def tokens(r):
        n = r.size // 16
        return xs[pl.ds(r.start // 16, n)].reshape(r.size, D)

    def deal():
        @pl.loop(0, pc.total)
        def _(d):
            m = d // fsdp
            outv[d] = raw[m * fsdp + order[m, lax.rem(d, fsdp)]]

    def prepare():
        k = lax.broadcasted_iota(jnp.int32, (L, L), 0)
        q = lax.broadcasted_iota(jnp.int32, (L, L), 1)
        dist[...] = jnp.where(k < len_s, jnp.abs(k - q).astype(F32), -NEGATIVE)

    def place_small():
        for f in range(fsdp):
            smallf[:, pl.ds(f * rows, rows)] = small[f, :, pl.ds(0, rows)]

    def project(p):
        @pl.loop(0, D // 256)
        def _(t):
            cols = block(t, 256)
            r = mm(xs[...].reshape(L, D), w_cols(p, cols))
            if p != 1:
                r = r + smallf[pl.ds(BQ if p == 0 else BV, 1), cols]
            qkv[p, :, cols] = r.astype(BF)

    def attend(j):
        cols = block(j, 128)
        lane = lax.broadcasted_iota(jnp.int32, (L, 128), 1)
        q2, k2 = qkv[0, :, cols], qkv[1, :, cols]
        vt = qkv[2, :, cols].T
        for q in range(L // 256):
            qr = pl.ds(256 * q, 256)
            parts = []
            for s in range(2):
                qm = jnp.where((lane < 64) if s == 0 else (lane >= 64), q2, jnp.zeros_like(q2))
                st = mm_nt(k2, qm[256 * q : 256 * q + 256])
                st = st * (0.125 * LOG2E) - dist[:, qr] * slopes[2 * j + s]
                top = jnp.max(st, axis=0, keepdims=True)
                e = jnp.exp2(st - top)
                total = jnp.sum(e, axis=0, keepdims=True)
                lse[2 * j + s, :, qr] = top + jnp.log2(total)
                pr = (e * (1.0 / total)).astype(BF)
                parts.append(mm(vt[64 * s : 64 * s + 64], pr))
            ctxt[qr, cols] = jnp.concatenate(parts, axis=0).T.astype(BF)

    def first_sum():
        @pl.loop(0, D // 256)
        def _(t):
            cols = block(t, 256)
            acc[:, cols] = mm(ctxt[...], w_cols(3, cols)) + smallf[pl.ds(BO, 1), cols]

    def first_norm():
        @pl.loop(0, L // 64)
        def _(i):
            r = block(i, 64)
            h = acc[r, :] + tokens(r).astype(F32)
            centre = h - row_mean(h)
            rs = lax.rsqrt(row_mean(centre * centre) + EPSILON)
            xh = centre * rs
            xhat[r, :] = xh
            rstd[r, :] = jnp.broadcast_to(rs, (64, 128))
            yy = xh * smallf[pl.ds(G1, 1), :] + smallf[pl.ds(B1, 1), :]
            y1[r, :] = yy
            y1b[r, :] = yy.astype(BF)

        tr[...] = y1b[...].T

    def gated(i):
        for s in range(D // 256):
            gated_part(i, s)

    def gated_part(i, s):
        wc = block(s, 256)
        cols = block(i * 3 + s, 256)
        a = mm(y1b[...], w_cols(4 + 2 * i, wc))
        u = mm(y1b[...], w_cols(5 + 2 * i, wc))
        cdf = 0.5 + 0.5 * lax.erf(a * math.sqrt(0.5))
        pdf = jnp.exp2(a * a * (-0.5 * LOG2E)) * (1.0 / math.sqrt(2.0 * math.pi))
        gelu = a * cdf
        zed[:, cols] = (gelu * u).astype(BF)
        act[:, cols] = gelu.astype(BF)
        slope_up[:, cols] = (u * (cdf + a * pdf)).astype(BF)

    def second_norm():
        @pl.loop(0, D // 256)
        def _(t):
            cols = block(t, 256)
            w = wd[:, :, :, :, :, cols].reshape(FF, 256)
            acc[:, cols] = mm(zed[...], w) + smallf[pl.ds(BD, 1), cols]

        def step(i, sums):
            r = block(i, 64)
            h = acc[r, :] + y1[r, :]
            centre = h - row_mean(h)
            rs = lax.rsqrt(row_mean(centre * centre) + EPSILON)
            xh = centre * rs
            gain = smallf[pl.ds(G2, 1), :]
            valid = (lax.broadcasted_iota(jnp.int32, (64, D), 0) + i * 64) < len_s
            res = jnp.where(valid, xh * gain + smallf[pl.ds(B2, 1), :], 0.0).astype(BF)
            outv[pl.ds(i * 4, 4)] = res.reshape(4, 16, D)
            up = jnp.where(valid, gs[pl.ds(i * 4, 4)].reshape(64, D).astype(F32), 0.0)
            dx = up * gain
            dh = rs * (dx - row_mean(dx) - xh * row_mean(dx * xh))
            low = dh.astype(BF)
            acc[r, :] = dh
            dfb[r, :] = low
            sg, sb, sd = sums
            return (
                sg + jnp.sum(up * xh, axis=0, keepdims=True),
                sb + jnp.sum(up, axis=0, keepdims=True),
                sd + jnp.sum(low.astype(F32), axis=0, keepdims=True),
            )

        zero = jnp.zeros((1, D), F32)
        sg, sb, sd = lax.fori_loop(0, L // 64, step, (zero, zero, zero))
        sgrad[pl.ds(G2, 1), :] = sg
        sgrad[pl.ds(B2, 1), :] = sb
        sgrad[pl.ds(BD, 1), :] = sd

    def ff_back(i):
        cols = block(i, D)
        dz = mm_nt(dfb[...], wd[pl.ds(i * Z // 4, Z // 4)].reshape(D, D))
        dgate = (dz * slope_up[:, cols].astype(F32)).astype(BF)
        dup = (dz * act[:, cols].astype(F32)).astype(BF)
        act[:, cols] = dup
        acc[...] += mm_nt(dgate, w_all(4 + 2 * i))
        wa[4 + 2 * i] = mm(tr[...], dgate).astype(BF).reshape(w_pc)

    def ff_back_rest(i):
        cols = block(i, D)
        acc[...] += mm_nt(act[:, cols], w_all(5 + 2 * i))
        wa[5 + 2 * i] = mm(tr[...], act[:, cols]).astype(BF).reshape(w_pc)
        wd[pl.ds(i * Z // 4, Z // 4)] = mm_tn(zed[:, cols], dfb[...]).astype(BF).reshape((Z // 4,) + wd.shape[1:])

    def first_norm_back():
        def step(i, sums):
            r = block(i, 64)
            up = acc[r, :]
            xh = xhat[r, :]
            dx = up * smallf[pl.ds(G1, 1), :]
            dh = rstd[r, :][:, :1] * (dx - row_mean(dx) - xh * row_mean(dx * xh))
            low = dh.astype(BF)
            xhat[r, :] = dh
            dfb[r, :] = low
            sg, sb, sd = sums
            return (
                sg + jnp.sum(up * xh, axis=0, keepdims=True),
                sb + jnp.sum(up, axis=0, keepdims=True),
                sd + jnp.sum(low.astype(F32), axis=0, keepdims=True),
            )

        zero = jnp.zeros((1, D), F32)
        sg, sb, sd = lax.fori_loop(0, L // 64, step, (zero, zero, zero))
        sgrad[pl.ds(G1, 1), :] = sg
        sgrad[pl.ds(B1, 1), :] = sb
        sgrad[pl.ds(BO, 1), :] = sd

    def out_back():
        y1b[...] = mm_nt(dfb[...], w_all(3)).astype(BF)
        wa[3] = mm_tn(ctxt[...], dfb[...]).astype(BF).reshape(w_pc)

    def dqkv(p):
        return act.at[:, pl.ds(D * p, D)]

    def attend_back(j):
        cols = block(j, 128)
        lane = lax.broadcasted_iota(jnp.int32, (L, 128), 1)
        q2, k2, v2 = (qkv[i, :, cols] for i in range(3))
        do2 = y1b[:, cols]
        kt = k2.T
        dv = dk = None
        for q in range(L // 256):
            qr = pl.ds(256 * q, 256)
            qs = slice(256 * q, 256 * q + 256)
            parts = []
            for s in range(2):
                half = (lane < 64) if s == 0 else (lane >= 64)
                qm = jnp.where(half, q2, jnp.zeros_like(q2))[qs]
                dm = jnp.where(half, do2, jnp.zeros_like(do2))[qs]
                st = mm_nt(k2, qm) * (0.125 * LOG2E) - dist[:, qr] * slopes[2 * j + s]
                pr = jnp.exp2(st - lse[2 * j + s, :, qr])
                dp = mm_nt(v2, dm)
                ds = (pr * (dp - jnp.sum(pr * dp, axis=0, keepdims=True))).astype(BF)
                a, b = mm(pr.astype(BF), dm), mm(ds, qm)
                dv = a if dv is None else dv + a
                dk = b if dk is None else dk + b
                parts.append(mm(kt[64 * s : 64 * s + 64], ds))
            dqkv(0)[qr, cols] = (jnp.concatenate(parts, axis=0).T * 0.125).astype(BF)
        dqkv(1)[:, cols] = (dk * 0.125).astype(BF)
        dqkv(2)[:, cols] = dv.astype(BF)

    def weights_back(p):
        x = xs[...].reshape(L, D)
        d = dqkv(p)
        wa[p] = mm_tn(x, d[...]).astype(BF).reshape(w_pc)
        if p != 1:
            r = BQ if p == 0 else BV
            sgrad[pl.ds(r, 1), :] = jnp.sum(d[...].astype(F32), axis=0, keepdims=True)

    def tokens_back():
        @pl.loop(0, L // 128)
        def _(i):
            r = block(i, 128)
            v = xhat[r, :]
            for p in range(3):
                v = v + mm_nt(dqkv(p)[r, :], w_all(p))
            raw[pl.ds(i * 8, 8)] = v.astype(BF).reshape(8, 16, D)

    def split_small():
        sparts[...] = jnp.zeros_like(sparts)
        for d in range(pc.total):
            at = d % fsdp * rows
            sparts[d, :, pl.ds(0, rows)] = sgrad[:, pl.ds(at, rows)]

    def undeal():
        @pl.loop(0, pc.total)
        def _(k):
            m, n = k // fsdp, lax.rem(k, fsdp)

            def find(f, at):
                return jnp.where(order[m, f] == n, f, at)

            DX[k] = dxr[m * fsdp + lax.fori_loop(0, fsdp, find, 0)]

    def spread(ex, t, at):
        first, count = at
        if first <= t < first + count:
            ex.start(t - first, count)

    take_raw = pltpu.make_async_copy(tokens_in, raw, rsem)
    take_raw.start()
    pc.signal()
    small_own[...] = jnp.zeros_like(small_own)
    for i, ref in enumerate(small_in):
        small_own[pl.ds(i, 1), pl.ds(0, rows)] = ref[...].astype(F32)
    prepare()
    take_raw.wait()
    deal()
    pc.wait()

    me_small = small.at[pc.f]
    keep_small = pltpu.make_async_copy(small_own, me_small, esems[2].at[2])
    keep_small.start()

    @pl.loop(1, fsdp)
    def _(k):
        f = lax.rem(pc.f + k, fsdp)
        remote(small_own, me_small, esems[0].at[2], esems[1].at[2], (pc.x, f)).start()

    small_all = remote(
        small.at[pl.ds(0, fsdp - 1)], small.at[pl.ds(0, fsdp - 1)], esems[0].at[2], esems[1].at[2],
        pc.dev(c=1 - pc.c),
    )

    def begin():
        ex_x.wait()
        small_all.wait_recv()
        keep_small.wait()
        place_small()
        for p in range(3):
            project(p)

    tasks = [(2, begin)]
    tasks += [(2, functools.partial(attend, j)) for j in range(HEADS // 2)]
    tasks += [(3, first_sum), (3, first_norm)]
    tasks += [(5 + 2 * i, functools.partial(gated, i)) for i in range(FF // D)]
    there = -1

    units = len(GATHER_UNITS)
    finished = [max(u for u in range(units) if GATHER_UNITS[u][0] == p) for p in range(PIECES)]
    for t in range(units + CORE_AT):
        pc.turn = t
        pc.finish(t - SETTLE)
        spread(ex_x, t, X_AT)
        spread(ex_g, t, G_AT)
        for u in range(units):
            if t == max(0, u - AHEAD):
                g.start(u)
        for h in range(1, Z):
            for u in range(units):
                if t == max(0, u - AHEAD) + h:
                    g.hop(u, h)
        if 0 <= t - ROW_AT < units:
            g.row(t - ROW_AT)
        if 0 <= t - PLANE_AT < units:
            g.plane(t - PLANE_AT)
        if 0 <= t - CORE_AT < units:
            u = t - CORE_AT
            g.core(u)
            there = max([p for p in range(PIECES) if finished[p] <= u], default=-1)
            left = units + CORE_AT - 1 - t
            if tasks and tasks[0][0] <= there:
                tasks.pop(0)[1]()
            while len(tasks) > left and tasks[0][0] <= there:
                tasks.pop(0)[1]()
    ex_g.wait()
    ex_x.done()
    second_norm()
    if O_FIRST:
        ex_o.start()
    pc.finish()

    units = len(SCATTER_UNITS)
    stages = STAGES if STAGES else (("core", 1), ("plane", 3), ("row", 5), ("middle", 6), ("line", 8), ("last", 10))
    for t in range(units + stages[-1][1]):
        pc.turn = t
        pc.finish(t - SETTLE)
        if t < 8:
            (ff_back_rest if t % 2 else ff_back)(t // 2)
        if t == 8:
            first_norm_back()
            out_back()
        if 9 <= t < 12:
            pl.loop(2 * (t - 9), 2 * (t - 9) + 2)(attend_back)
        if t == 12:
            tokens_back()
            for p in range(3):
                weights_back(p)
            split_small()
            ex_s.start()
        if not O_FIRST:
            spread(ex_o, t, O_AT)
        spread(ex_d, t, D_AT)
        if t < units:
            sc.start(t)
        for name, off in stages:
            if 0 <= t - off < units:
                u = t - off
                if name == "last":
                    sc.last(u, out_of(SCATTER_UNITS[u][0]))
                else:
                    getattr(sc, name)(u)
    ex_s.wait()

    def add(i, v):
        return v + gsum[i]

    total = lax.fori_loop(1, pc.total, add, gsum[0])
    SMALLG[...] = total[:, :rows]
    ex_d.wait()
    undeal()
    ex_o.wait()
    for e in (ex_g, ex_o, ex_d, ex_s):
        e.done()
    small_all.wait_send()
    pc.finish()


def hand_over(*refs):
    src, small, dst, parts, through, sem = refs[:6], refs[6], refs[7:13], refs[13:21], refs[21:27], refs[27]
    take = [pltpu.make_async_copy(a, b, sem.at[0, k]) for k, (a, b) in enumerate(zip(src, through))]
    give = [pltpu.make_async_copy(a, b, sem.at[1, k]) for k, (a, b) in enumerate(zip(through, dst))]
    for c in take:
        c.start()
    for k, ref in enumerate(parts):
        ref[...] = small[pl.ds(k, 1), :]
    for a, b in zip(take, give):
        a.wait()
        b.start()
    for c in give:
        c.wait()


def per_device(
    tokens_in, out_grad, seq_lengths, order, w_qkv, bias_q, bias_v, w_out, bias_out, ln1_gain, ln1_bias, w_gate_up,
    w_down, bias_down, ln2_gain, ln2_bias,
):
    fsdp = lax.axis_size("fsdp")
    total = 2 * fsdp
    rows = w_out.shape[0]
    here = tokens_in.shape[2]
    L = here * total
    Z = fsdp // 4
    small = [v.reshape(1, rows) for v in (bias_q, bias_v, bias_out, ln1_gain, ln1_bias, bias_down, ln2_gain, ln2_bias)]
    slopes = jnp.array(slope_list(HEADS), F32) * LOG2E
    hbm = pl.BlockSpec(memory_space=pl.ANY)
    smem = pl.BlockSpec(memory_space=pltpu.SMEM)
    vmem = pl.BlockSpec(memory_space=pltpu.VMEM)
    S = jax.ShapeDtypeStruct
    T = pltpu.SemaphoreType.DMA
    V = pltpu.VMEM
    rows_of = (total, here, D)
    results = pl.pallas_call(
        functools.partial(layer_kernel, fsdp, rows),
        out_shape=[
            S(rows_of, BF), S(rows_of, BF), S((rows, 3 * D), F32), S((rows, D), F32), S((rows, 2 * FF), F32),
            S((4 * rows, D), F32), S((8, rows), F32),
        ],
        in_specs=[smem] * 3 + [hbm] * 2 + [vmem] * 8 + [hbm] * 4,
        out_specs=[hbm] + [vmem] * 6,
        scratch_shapes=[
            V((12, Z, 2, 2, rows, D), BF), V((Z, 2, 2, 4, rows, D), BF), V(rows_of, BF), V(rows_of, BF),
            V(rows_of, BF), V(rows_of, BF), V((fsdp, 8, 128), F32), V((8, 128), F32), V((8, D), F32), V((3, L, D), BF), V((L, L), F32),
            V((HEADS, 1, L), F32), V((L, D), BF), V((L, D), F32), V((L, D), BF), V((L, D), F32), V((L, 128), F32),
            V((L, FF), BF), V((L, FF), BF), V((L, FF), BF), V((L, D), F32), V((L, D), BF), V((D, L), BF),
            V(rows_of, BF), V((8, D), F32), V((total, 8, 128), F32), V((total, 8, 128), F32),
            *Scatter.buffers(Z, rows), *Gather.sems(Z), *Scatter.sems(), T((6,)), T((6,)), T((6,)), T,
        ],
        compiler_params=pltpu.CompilerParams(collective_id=0, has_side_effects=True, vmem_limit_bytes=VMEM_LIMIT),
        name="layer",
    )(order, seq_lengths, slopes, tokens_in.reshape(rows_of), out_grad.reshape(rows_of), *small, w_qkv, w_out, w_gate_up, w_down)
    output, input_grad, gq, gw, gg, gd, *mine = pl.pallas_call(
        hand_over,
        out_shape=[S(r.shape, r.dtype) for r in results[:6]] + [S((1, rows), F32)] * 8,
        in_specs=[hbm] * 6 + [vmem],
        out_specs=[hbm] * 6 + [vmem] * 8,
        scratch_shapes=[V(r.shape, r.dtype) for r in results[:6]] + [T((2, 6))],
        name="hand_over",
    )(*results)
    mine = [v.reshape(rows) for v in mine]
    return (
        output.reshape(tokens_in.shape), input_grad.reshape(tokens_in.shape), gq, mine[BQ], mine[BV], gw, mine[BO],
        mine[G1], mine[B1], gg, gd, mine[BD], mine[G2], mine[B2],
    )


def solution(mesh):
    fsdp = mesh.shape["fsdp"]
    rows = D // fsdp
    kernels = mesh.shape["ctx"] == M and fsdp == 16 and rows % 16 == 0
    return jax.shard_map(
        per_device if kernels else per_device_plain,
        mesh=mesh,
        in_specs=(
            P(None, None, ("ctx", "fsdp"), None),
            P(None, None, ("ctx", "fsdp"), None),
            P(),
            P(),
            P("fsdp", None),
            P("fsdp"),
            P("fsdp"),
            P("fsdp", None),
            P("fsdp"),
            P("fsdp"),
            P("fsdp"),
            P("fsdp", None),
            P("fsdp", None),
            P("fsdp"),
            P("fsdp"),
            P("fsdp"),
        ),
        out_specs=(
            P(None, None, ("ctx", "fsdp"), None),
            P(None, None, ("ctx", "fsdp"), None),
            P("fsdp", None),
            P("fsdp"),
            P("fsdp"),
            P("fsdp", None),
            P("fsdp"),
            P("fsdp"),
            P("fsdp"),
            P("fsdp", None),
            P("fsdp", None),
            P("fsdp"),
            P("fsdp"),
            P("fsdp"),
        ),
        check_vma=False,
    )
```
